128 devices in a mesh: head: 4 (over x), expert: 16 (over y, z_hi, core), dp: 2 (over z_lo).
Axes of the slice: x: 4, y: 4, z: 4 (z_hi: 2, z_lo: 2; z = z_hi * 2 + z_lo), core: 2. Of those that a mesh axis runs over, the one named last changes fastest.
Arguments:
- tokens: bfloat16 [32, 1024, 768], P(('expert', 'dp'), 'head'), may hold values from -6 to 6
- out_grad: bfloat16 [32, 1024, 768], P(('expert', 'dp'), 'head'), may hold values from -6 to 6
- w_query: bfloat16 [768, 768], P(None, 'head'), may hold values from -0.21875 to 0.21875
- w_key: bfloat16 [768, 768], P(None, 'head'), may hold values from -0.21875 to 0.21875
- w_value: bfloat16 [768, 768], P(None, 'head'), may hold values from -0.21875 to 0.21875
- w_output: bfloat16 [768, 768], P('head'), may hold values from -0.875 to 0.875
- gain_one: float32 [768], replicated, may hold values from 0.5 to 1.5
- gain_two: float32 [768], replicated, may hold values from 0.5 to 1.5
- expert_up: bfloat16 [16, 768, 3072], P('expert'), may hold values from -0.21875 to 0.21875
- expert_down: bfloat16 [16, 3072, 768], P('expert'), may hold values from -0.109375 to 0.109375
- hash_table: int32 [32768], replicated, may hold values from 0 to 15, as said below
- token_ids: int32 [32, 1024], P(('expert', 'dp'), 'head'), may hold values from 0 to 32767, as said below
- doc_lengths: int32 [32, 8], P(('expert', 'dp')), may hold values from 1 to 256, 1024 in all within a row
- turn_mask: int32 [32, 1024], P(('expert', 'dp')), may hold values 0 or 1
Outputs:
- final: float32 [32, 1024, 768], P(('expert', 'dp'), 'head')
- tokens_grad: float32 [32, 1024, 768], P(('expert', 'dp'), 'head')
- w_query_grad: float32 [768, 768], P(None, 'head')
- w_key_grad: float32 [768, 768], P(None, 'head')
- w_value_grad: float32 [768, 768], P(None, 'head')
- w_output_grad: float32 [768, 768], P('head')
- gain_one_grad: float32 [768], replicated
- gain_two_grad: float32 [768], replicated
- expert_up_grad: float32 [16, 768, 3072], P('expert')
- expert_down_grad: float32 [16, 3072, 768], P('expert')
- expert_loads: int32 [16], replicated
The draws below stay inside these ranges and needn't reach their ends.
Inputs may be any that keep to these rules, and one draw needn't show every extreme that they name: hash_table[v] is the expert of token id v; every expert has 2048 ids. `token_ids`: cut each packed row into 4 aligned blocks of 256 tokens. Among the tokens of one block at most 32 have the same expert (through hash_table). For each block position b and each c < 2, one expert, drawn from the seed, has exactly 32 tokens in block b of every packed row whose index is c modulo 2. `doc_lengths`: each row sums to 1024 and its largest entry is 256.
All inputs are finite; a program needn't handle non-finite values. No bound on the sum of `turn_mask` on one device may be relied on, other than what follows from the above.
Results may differ from the reference program's by a relative error of at most 0.02.
Values may be sent and summed in bfloat16 or wider, within the bound.
A program may use at most 128 MiB of HBM per device.

```python
import math
import jax
import jax.numpy as jnp
import numpy as np
from jax import lax

D = 768
HEADS = 12
HEAD_DIM = 64
FF = 3072
VOCAB = 32768
TOK_DEV = 256
MAXLEN = 256
EXPERTS = 16
CAP = 32
ROW_PIECES = 4
ROW_BATCH = 2
GROUP_TOK = 1024
GROUPS = 32
NDOC = 8


def shared_order(key):
    return jax.random.permutation(key, VOCAB).astype(jnp.int32)


def draw_hash_table(key, part):
    ordering = shared_order(key)
    labels = jnp.arange(VOCAB, dtype=jnp.int32) % EXPERTS
    return jnp.zeros((VOCAB,), jnp.int32).at[ordering].set(labels)


def block_ranks(block_key):
    choose_key, shuffle_key = jax.random.split(block_key)
    spare_slots = jax.random.permutation(choose_key, (EXPERTS - 1) * CAP)[:TOK_DEV - CAP].astype(jnp.int32)
    rank_rows = jnp.concatenate([jnp.zeros((CAP,), jnp.int32), 1 + spare_slots // CAP])
    return jax.random.permutation(shuffle_key, rank_rows)


def draw_token_ids(key, part):
    ordering = shared_order(key)
    key = jax.random.fold_in(key, 23)
    busiest_key, block_key, pick_key = jax.random.split(key, 3)
    busiest = jax.random.randint(busiest_key, (ROW_PIECES, ROW_BATCH), 0, EXPERTS)
    row_class = jnp.arange(GROUPS, dtype=jnp.int32) % ROW_BATCH
    piece_index = jnp.arange(ROW_PIECES, dtype=jnp.int32)
    leading = busiest[piece_index[None, :], row_class[:, None]]
    rank_rows = jax.vmap(block_ranks)(jax.random.split(block_key, GROUPS * ROW_PIECES))
    rank_rows = rank_rows.reshape(GROUPS, ROW_PIECES, TOK_DEV)
    experts_of = (leading[:, :, None] + rank_rows) % EXPERTS
    pick_rows = jax.random.randint(pick_key, experts_of.shape, 0, VOCAB // EXPERTS)
    return ordering[experts_of + EXPERTS * pick_rows].reshape(GROUPS, GROUP_TOK)


def touch_ends(values, own_key, least, high):
    extent = values.shape
    place = [jax.random.randint(jax.random.fold_in(own_key, axis), (), 0, extent[axis]) for axis in range(len(extent))]
    values = values.at[tuple(place)].set(least)
    longest = extent.index(max(extent))
    place[longest] = (place[longest] + 1) % extent[longest]
    return values.at[tuple(place)].set(high)


def levels(rng, shape, cuts, least, largest):
    level = 1.0
    for axis_at, blocks in cuts:
        draws = jax.random.uniform(jax.random.fold_in(jax.random.fold_in(rng, 6), axis_at), (blocks,), jnp.float32, least / len(cuts), largest / len(cuts))
        level = level * jnp.repeat(jnp.exp(draws), shape[axis_at] // blocks).reshape((-1,) + (1,) * (len(shape) - 1 - axis_at))
    return level


def profile(count, total, limit, lean):
    weights = [(1 << 20) // math.isqrt(rank ** lean) + 1 for rank in range(2, count + 1)]
    surplus, counts = total - limit - (count - 1), [1] * (count - 1)
    while surplus > 0:
        free = [i for i in range(count - 1) if counts[i] < limit]
        mass, remaining = sum([weights[i] for i in free]), surplus
        for i in free:
            more = min(limit - counts[i], max(1, remaining * weights[i] // mass), surplus)
            counts[i] = counts[i] + more
            surplus = surplus - more
    return np.array([limit] + counts)


def ragged(own_key, count, total, bound, lean):
    if count == 2:
        one = jax.random.randint(own_key, (), max(1, total - bound), min(bound, total - 1) + 1)
        return jnp.stack([one, total - one])
    tallies = jnp.asarray(profile(count, total, bound, lean), jnp.int32)
    twos = (count - 1) // 2
    donor, receiver = tallies[1:1 + 2 * twos:2], tallies[2:2 + 2 * twos:2]
    slack = jnp.minimum(donor - 1, bound - receiver)
    moved = jax.random.randint(jax.random.fold_in(own_key, 1), (twos,), 0, 1 << 20) % (slack + 1)
    tallies = tallies.at[1:1 + 2 * twos:2].set(donor - moved).at[2:2 + 2 * twos:2].set(receiver + moved)
    return tallies[jax.random.permutation(jax.random.fold_in(own_key, 2), count)]


def gaussian(rng, extent, deviation, reach, pieces=(), held_as=jnp.bfloat16):
    drawn = jax.random.normal(rng, extent, jnp.float32) * deviation
    if len(pieces) > 0:
        drawn = levels(rng, extent, pieces, -0.22, 0.18) * drawn
    return jnp.clip(drawn, min=-reach, max=reach).astype(held_as)


def setup_inputs(seed: int = 0) -> dict:
    streams_of = jax.random.split(jax.random.key(seed), 15)
    return {
        "tokens": gaussian(streams_of[0], (GROUPS, GROUP_TOK, D), 1.0, 6.0, ((0, 32), (1, 4))),
        "out_grad": gaussian(streams_of[1], (GROUPS, GROUP_TOK, D), 1.0, 6.0, ((0, 32), (1, 4))),
        "w_query": gaussian(streams_of[2], (D, D), D ** -0.5, 0.21875, ((1, 4),)),
        "w_key": gaussian(streams_of[3], (D, D), D ** -0.5, 0.21875, ((1, 4),)),
        "w_value": gaussian(streams_of[4], (D, D), D ** -0.5, 0.21875, ((1, 4),)),
        "w_output": gaussian(streams_of[5], (D, D), (D // 16) ** -0.5, 0.875, ((0, 4),)),
        "gain_one": jnp.clip(1.0 + 0.1 * jax.random.normal(streams_of[6], (D,), jnp.float32), 0.5, 1.5),
        "gain_two": jnp.clip(1.0 + 0.1 * jax.random.normal(streams_of[7], (D,), jnp.float32), 0.5, 1.5),
        "expert_up": gaussian(streams_of[8], (EXPERTS, D, FF), D ** -0.5, 0.21875, ((0, 16),)),
        "expert_down": gaussian(streams_of[9], (EXPERTS, FF, D), FF ** -0.5, 0.109375, ((0, 16),)),
        "hash_table": draw_hash_table(jax.random.fold_in(streams_of[14], 71), 0),
        "token_ids": draw_token_ids(jax.random.fold_in(streams_of[14], 71), 0),
        "doc_lengths": jax.vmap(lambda own: ragged(own, NDOC, GROUP_TOK, MAXLEN, 1))(jax.random.split(streams_of[12], GROUPS)).reshape((GROUPS, NDOC)).astype(jnp.int32),
        "turn_mask": touch_ends((jax.random.randint(streams_of[13], (GROUPS, GROUP_TOK), 0, 2) < 1).astype(jnp.int32), jax.random.fold_in(streams_of[13], 1), 0, 1),
    }


EPSILON = 1e-05
NEGATIVE = -1e+30
HIGHEST = lax.Precision.HIGHEST

@jax.custom_vjp
def low(v):
    return lax.optimization_barrier(v.astype(jnp.bfloat16)).astype(jnp.float32)

@jax.custom_vjp
def low_back(v):
    return v

def low_keep(v):
    return (low(v), None)

def low_pass(kept, grad):
    return (grad,)

def back_keep(v):
    return (v, None)

def back_low(kept, grad):
    return (low(grad),)
low.defvjp(low_keep, low_pass)
low_back.defvjp(back_keep, back_low)

def norm_rows(values, scales):
    average = lax.optimization_barrier(jnp.mean(values, axis=-1, keepdims=True))
    centred = values - average
    variance = lax.optimization_barrier(jnp.mean(centred * centred, axis=-1, keepdims=True))
    return centred * lax.rsqrt(variance + EPSILON) * scales

def doc_ids(doc_lengths, length):
    endings = jnp.cumsum(doc_lengths)
    places = jnp.arange(length, dtype=jnp.int32)
    return lax.optimization_barrier(jnp.sum((endings[None, :] <= places[:, None]).astype(jnp.int32), axis=1))

def forward(tokens, w_query, w_key, w_value, w_output, gain_one, gain_two, expert_up, expert_down, segments, turn_mask, chosen):
    factor = HEAD_DIM ** (-0.5)
    places = jnp.arange(GROUP_TOK, dtype=jnp.int32)
    causal = places[None, :] <= places[:, None]

    def packed_row(inputs):
        row_values, row_segments, row_prompt = inputs
        normed = low(norm_rows(row_values, gain_one))
        queries = low(low_back(jnp.dot(normed, w_query, precision=HIGHEST))).reshape(GROUP_TOK, HEADS, HEAD_DIM)
        keys_all = low(low_back(jnp.dot(normed, w_key, precision=HIGHEST))).reshape(GROUP_TOK, HEADS, HEAD_DIM)
        values_all = low(low_back(jnp.dot(normed, w_value, precision=HIGHEST))).reshape(GROUP_TOK, HEADS, HEAD_DIM)
        scores = low_back(jnp.einsum('qhd,khd->hqk', queries, keys_all, precision=HIGHEST) * factor)
        allowed = (row_segments[:, None] == row_segments[None, :]) & (causal | (row_prompt[None, :] == 1))
        scores = jnp.where(allowed[None], scores, NEGATIVE)
        highest = lax.optimization_barrier(jnp.max(scores, axis=-1, keepdims=True))
        powers = jnp.exp(scores - highest)
        weights = low(powers / lax.optimization_barrier(jnp.sum(powers, axis=-1, keepdims=True)))
        attended = low(low_back(jnp.einsum('hqk,khd->qhd', weights, values_all, precision=HIGHEST))).reshape(GROUP_TOK, D)
        return low_back(jnp.dot(attended, w_output, precision=HIGHEST))
    mixed = lax.map(jax.checkpoint(packed_row), (tokens, segments, turn_mask))
    hidden = tokens + mixed
    expert_rows = low(low_back(norm_rows(hidden, gain_two))).reshape(GROUPS * GROUP_TOK, D)
    flat_choice = chosen.reshape(GROUPS * GROUP_TOK)
    ordering = jnp.argsort(flat_choice, stable=True).astype(jnp.int32)
    sorted_choice = flat_choice[ordering]
    sorted_rows = expert_rows[ordering]
    expert_loads = lax.optimization_barrier(jnp.sum((flat_choice[:, None] == jnp.arange(EXPERTS, dtype=jnp.int32)[None, :]).astype(jnp.int32), axis=0))
    offsets = (jnp.cumsum(expert_loads) - expert_loads).astype(jnp.int32)
    longest = CAP * GROUPS * ROW_PIECES
    padded = jnp.concatenate([sorted_rows, jnp.zeros((longest, D), sorted_rows.dtype)], axis=0)

    def one_expert(inputs):
        expert_index, offset, amount = inputs
        rows_in = lax.dynamic_slice_in_dim(padded, offset.astype(jnp.int32), longest, 0)
        before = low_back(jnp.dot(rows_in, expert_up[expert_index], precision=HIGHEST))
        active = low(jax.nn.gelu(before))
        produced = low(low_back(jnp.dot(active, expert_down[expert_index], precision=HIGHEST)))
        keeping = jnp.arange(longest, dtype=jnp.int32) < amount
        return jnp.where(keeping[:, None], produced, jnp.zeros_like(produced))
    produced_all = lax.map(jax.checkpoint(one_expert), (jnp.arange(EXPERTS, dtype=jnp.int32), offsets, expert_loads))
    within = jnp.arange(GROUPS * GROUP_TOK, dtype=jnp.int32) - offsets[sorted_choice]
    sorted_out = produced_all[sorted_choice, within]
    branch_out = jnp.zeros_like(sorted_out).at[ordering].set(sorted_out)
    return hidden + branch_out.reshape(GROUPS, GROUP_TOK, D)

def reference(tokens, out_grad, w_query, w_key, w_value, w_output, gain_one, gain_two, expert_up, expert_down, hash_table, token_ids, doc_lengths, turn_mask):
    segments = jax.vmap(lambda lengths_row: doc_ids(lengths_row, GROUP_TOK))(doc_lengths)
    chosen = jnp.take(hash_table, token_ids).astype(jnp.int32)
    floats = tuple((item.astype(jnp.float32) for item in (tokens, w_query, w_key, w_value, w_output, gain_one, gain_two, expert_up, expert_down)))

    def run_block(tokens_f, query_f, key_f, value_f, output_f, first_gain, second_gain, up_f, down_f):
        return forward(tokens_f, query_f, key_f, value_f, output_f, first_gain, second_gain, up_f, down_f, segments, turn_mask, chosen)
    final, pull_back = jax.vjp(run_block, *floats)
    grads = pull_back(out_grad.astype(jnp.float32))
    expert_loads = lax.optimization_barrier(jnp.sum((chosen.reshape(-1)[:, None] == jnp.arange(EXPERTS, dtype=jnp.int32)[None, :]).astype(jnp.int32), axis=0))
    return (final, grads[0], grads[1], grads[2], grads[3], grads[4], grads[5], grads[6], grads[7], grads[8], expert_loads)
```

```python
import functools

import jax
import jax.numpy as jnp
from jax import lax
from jax.experimental import pallas as pl
from jax.experimental.pallas import tpu as pltpu
from jax.sharding import PartitionSpec as P

MESH = pl.DeviceIdType.MESH
f32 = jnp.float32
bf16 = jnp.bfloat16
i32 = jnp.int32

HEADS_X = 4
EXPERTS = 16
TOK = 256
ROW = 1024
D = 768
FF = 3072
CAP = 32
SLOTS = EXPERTS * CAP
WIN = 768
HEAD_COLS = 192
PAD_COLS = 256
FF_CHUNK = 512
EPSILON = 1e-05
NEGATIVE = -1e30
GELU_A = 0.7978845608028654
GELU_B = 0.044715

NN = (((1,), (0,)), ((), ()))
NT = (((1,), (1,)), ((), ()))
TN = (((0,), (0,)), ((), ()))


def dot(a, b, dims=NN):
    return lax.dot_general(a, b, dims, preferred_element_type=f32)


def iota(shape, dim):
    return lax.broadcasted_iota(i32, shape, dim)


def norm_parts(x):
    average = jnp.mean(x, axis=-1, keepdims=True)
    centred = x - average
    variance = jnp.mean(centred * centred, axis=-1, keepdims=True)
    scale = lax.rsqrt(variance + EPSILON)
    return centred * scale, scale


def norm_pull(upstream, normed, scale, gain):
    m = upstream * gain
    first = jnp.mean(m, axis=-1, keepdims=True)
    second = jnp.mean(m * normed, axis=-1, keepdims=True)
    return scale * (m - first - normed * second)


def gelu_pair(u):
    u2 = u * u
    half = 0.5 + 0.5 * jnp.tanh(u * (GELU_A + (GELU_A * GELU_B) * u2))
    slope = half + (u + u) * (half * (1.0 - half)) * (GELU_A + (3.0 * GELU_A * GELU_B) * u2)
    return u * half, slope


def rows(start, size):
    return pl.ds(pl.multiple_of(start, size), size)


def block_kernel(
    tok, og, wq, wk, wv, wo, gain1, gain2, up_hbm, dn_hbm, table, ids, lengths, prompt,
    final, tgrad, gsum, small, x_all, g_all, cnt,
    wj, wjt, gath, qkv, att_snd, att, wo_full, up, dn, snd_a, snd_b, g_own, x_own, gc, xc,
    pack, ag, act, eacc, eg_rcv, out_rcv, disp, disp_t, hid, hgrad, mixed, agr_snd, agr,
    dq, dk, dv, jg, ng_snd, ng_rcv, wog_snd, wog_rcv, gfull, gpart, rs_core, rs_rcv, rs_pair,
    sm_x, sm_e, sm_d,
    load_sem, own_sem, nrm_s, nrm_r, wo_s, wo_r, gd_s, gd_r, xd_s, xd_r, eg_s, eg_r, out_s, out_r,
    att_s, att_r, agr_s, agr_r, ng_s, ng_r, wog_s, wog_r, tg_s, tg_r, tx_s, tx_r, ct_s, ct_r,
    ca_s, ca_r, a2_s, a2_r, a3_s, a3_r, a4_s, a4_r, sx_s, sx_r, se_s, se_r, sd_s, sd_r,
):
    h = lax.axis_index("head")
    e = lax.axis_index("expert")
    d = lax.axis_index("dp")
    right, left, across = lax.rem(h + 1, 4), lax.rem(h + 3, 4), lax.rem(h + 2, 4)
    x_peers = (right, left, across)
    x_from = (left, right, across)
    other = 1 - d
    twin = e + 1 - 2 * lax.rem(e, 2)

    def remote(src, dst, ss, rs, device):
        return pltpu.make_async_remote_copy(
            src_ref=src, dst_ref=dst, send_sem=ss, recv_sem=rs, device_id=device, device_id_type=MESH
        )

    def spread(snd, rcv, ss, rs):
        def step(k, carry):
            p = lax.rem(e + k, EXPERTS)
            remote(
                snd.at[rows(p * CAP, CAP)], rcv.at[rows(e * CAP, CAP)], ss.at[k], rs.at[k], (h, p, d)
            ).start()
            return carry

        lax.fori_loop(1, EXPERTS, step, 0)
        rcv[rows(e * CAP, CAP), :] = snd[rows(e * CAP, CAP), :]

    def spread_recv(snd, rcv, ss, rs):
        def step(k, carry):
            p = lax.rem(e + EXPERTS - k, EXPERTS)
            remote(
                snd.at[rows(p * CAP, CAP)], rcv.at[rows(p * CAP, CAP)], ss.at[k], rs.at[k], (h, p, d)
            ).wait_recv()
            return carry

        lax.fori_loop(1, EXPERTS, step, 0)

    def spread_sent(snd, rcv, ss, rs):
        def step(k, carry):
            p = lax.rem(e + k, EXPERTS)
            remote(
                snd.at[rows(p * CAP, CAP)], rcv.at[rows(e * CAP, CAP)], ss.at[k], rs.at[k], (h, p, d)
            ).wait_send()
            return carry

        lax.fori_loop(1, EXPERTS, step, 0)

    def cross(snd, rcv, ss, rs, only=None):
        view = (lambda r, i: r.at[i]) if only is None else (lambda r, i: r.at[i, pl.ds(0, only)])
        out = [
            remote(view(snd, p), view(rcv, h), ss.at[i], rs.at[i], (p, e, d))
            for i, p in enumerate(x_peers)
        ]
        into = [
            remote(view(snd, p), view(rcv, p), ss.at[i], rs.at[i], (p, e, d))
            for i, p in enumerate(x_from)
        ]
        return out, into

    def gather(buf, ss, rs, only=None):
        view = (lambda r, i: r.at[i]) if only is None else (lambda r, i: r.at[i, pl.ds(0, only)])
        out = [
            remote(view(buf, h), view(buf, h), ss.at[i], rs.at[i], (p, e, d))
            for i, p in enumerate(x_peers)
        ]
        into = [
            remote(view(buf, p), view(buf, p), ss.at[i], rs.at[i], (p, e, d))
            for i, p in enumerate(x_from)
        ]
        return out, into

    def token_copies(own, dst, ss, rs):
        def blk(hh, dd):
            return dd * 4 + hh

        half = pl.ds(0, 256)
        rest = pl.ds(256, 256)
        me = dst.at[blk(h, d)]
        out = [
            remote(own, me, ss.at[0], rs.at[0], (right, e, d)),
            remote(own, me, ss.at[1], rs.at[1], (left, e, d)),
            remote(own, me, ss.at[2], rs.at[2], (h, e, other)),
            remote(
                dst.at[blk(left, d), half], dst.at[blk(left, d), half], ss.at[3], rs.at[3], (right, e, d)
            ),
            remote(
                dst.at[blk(right, d), rest], dst.at[blk(right, d), rest], ss.at[4], rs.at[4], (left, e, d)
            ),
            remote(dst.at[blk(h, other)], dst.at[blk(h, other)], ss.at[5], rs.at[5], (right, e, d)),
            remote(dst.at[blk(h, other)], dst.at[blk(h, other)], ss.at[6], rs.at[6], (left, e, d)),
            remote(dst.at[blk(across, d)], dst.at[blk(across, d)], ss.at[7], rs.at[7], (h, e, other)),
        ]
        places = [
            dst.at[blk(left, d)],
            dst.at[blk(right, d)],
            dst.at[blk(h, other)],
            dst.at[blk(across, d), half],
            dst.at[blk(across, d), rest],
            dst.at[blk(left, other)],
            dst.at[blk(right, other)],
            dst.at[blk(across, other)],
        ]
        senders = [
            (left, e, d), (right, e, d), (h, e, other), (left, e, d),
            (right, e, d), (left, e, d), (right, e, d), (h, e, other),
        ]
        into = [
            remote(p, p, ss.at[i], rs.at[i], s) for i, (p, s) in enumerate(zip(places, senders))
        ]
        return out, into

    g_out, g_into = token_copies(gc, g_all, tg_s, tg_r)
    t_out, t_into = token_copies(xc, x_all, tx_s, tx_r)

    up_load = pltpu.make_async_copy(up_hbm, up, load_sem.at[0])
    dn_load = pltpu.make_async_copy(dn_hbm, dn, load_sem.at[1])
    up_load.start()
    dn_load.start()

    barrier = pltpu.get_barrier_semaphore()
    for p in x_peers:
        pl.semaphore_signal(barrier, inc=1, device_id=(p, e, d), device_id_type=MESH)
    pl.semaphore_signal(barrier, inc=1, device_id=(h, e, other), device_id_type=MESH)

    def greet(k, carry):
        pl.semaphore_signal(
            barrier, inc=1, device_id=(h, lax.rem(e + k, EXPERTS), d), device_id_type=MESH
        )
        return carry

    lax.fori_loop(1, EXPERTS, greet, 0)

    one, _ = norm_parts(tok[...].astype(f32))
    gath[h] = (one * gain1[...]).astype(bf16)
    wj[...] = jnp.zeros_like(wj)
    wj[:, 0:HEAD_COLS] = wq[...]
    wj[:, PAD_COLS : PAD_COLS + HEAD_COLS] = wk[...]
    wj[:, 2 * PAD_COLS : 2 * PAD_COLS + HEAD_COLS] = wv[...]
    for i in range(4):
        wo_full[i, HEAD_COLS:PAD_COLS, :] = jnp.zeros((PAD_COLS - HEAD_COLS, D), bf16)
    wo_full[h, 0:HEAD_COLS, :] = wo[...]

    pl.semaphore_wait(barrier, 3 + 1 + EXPERTS - 1)
    nrm_out, nrm_into = gather(gath, nrm_s, nrm_r)
    for c in nrm_out:
        c.start()

    eye = iota((TOK, TOK), 0) == iota((TOK, TOK), 1)
    id_col = jnp.sum(jnp.where(eye, ids[...].astype(f32), 0.0), axis=1, keepdims=True).astype(i32)
    high, low = lax.shift_right_logical(id_col, 7), lax.bitwise_and(id_col, 127)
    pick = jnp.where(iota((TOK, 256), 1) == high, 1.0, 0.0).astype(bf16)
    near = dot(pick, table[...].astype(f32).astype(bf16))
    lane = iota((TOK, 128), 1)
    chosen = jnp.sum(jnp.where(lane == low, near, 0.0), axis=1, keepdims=True)
    member = jnp.where(lane == chosen.astype(i32), 1.0, 0.0)
    before = jnp.where(iota((TOK, TOK), 1) < iota((TOK, TOK), 0), 1.0, 0.0).astype(bf16)
    rank = jnp.sum(dot(before, member.astype(bf16)) * member, axis=1, keepdims=True)
    slot = chosen * CAP + rank
    slot_row = jnp.sum(jnp.where(eye, slot, 0.0), axis=0, keepdims=True).astype(i32)
    disp_t[...] = jnp.where(iota((TOK, SLOTS), 1) == slot.astype(i32), 1.0, 0.0).astype(bf16)
    disp[...] = jnp.where(iota((SLOTS, TOK), 0) == slot_row, 1.0, 0.0).astype(bf16)
    sm_x[h] = jnp.zeros((8, D), f32)
    sm_x[h, 2:3, 0:128] = jnp.sum(member, axis=0, keepdims=True)

    snd_a[...] = dot(disp[...], og[...]).astype(bf16)
    spread(snd_a, g_own, gd_s, gd_r)

    column_scale = jnp.where(iota((1, D), 1) < PAD_COLS, 0.125, 1.0)

    def project(b):
        qkv[rows(b * TOK, TOK), :] = (dot(gath[b], wj[...]) * column_scale).astype(bf16)

    project(h)
    wo_out, wo_into = gather(wo_full, wo_s, wo_r, HEAD_COLS)
    for i, b in enumerate(x_from):
        nrm_into[i].wait_recv()
        if i == 2:
            for c in wo_out:
                c.start()
        project(b)

    ends = []
    total = 0
    for j in range(8):
        total = total + lengths[0, j]
        ends.append(total)

    def segment(pos):
        found = jnp.zeros(pos.shape, i32)
        for j in range(8):
            found = found + jnp.where(ends[j] <= pos, 1, 0)
        return found

    def window(b):
        first = jnp.minimum(jnp.maximum(b - 1, 0), 1) * TOK
        q_pos = b * TOK + iota((TOK, 1), 0)
        k_pos = first + iota((1, WIN), 1)
        said = prompt[:, pl.ds(pl.multiple_of(first, TOK), WIN)]
        k_least = jnp.where(said == 1, -1, k_pos)
        allowed = (segment(q_pos) == segment(k_pos)) & (k_least <= q_pos)
        return pl.ds(pl.multiple_of(first, TOK), WIN), allowed

    lane_low = iota((TOK, 128), 1) < 64

    def head_mask(head, x):
        if head == 2:
            return x
        return jnp.where(lane_low if head == 0 else jnp.logical_not(lane_low), x, jnp.zeros_like(x))

    def head_lanes(head, part):
        return pl.ds(part * PAD_COLS + (head // 2) * 128, 128)

    def attend(b, carry):
        keys, allowed = window(b)
        mine = rows(b * TOK, TOK)
        groups = [None, None]
        for head in range(3):
            q = head_mask(head, qkv[mine, head_lanes(head, 0)])
            s = dot(q, qkv[keys, head_lanes(head, 1)], NT)
            s = jnp.where(allowed, s, NEGATIVE)
            p = jnp.exp(s - jnp.max(s, axis=-1, keepdims=True))
            total = jnp.sum(p, axis=-1, keepdims=True)
            o = dot(p.astype(bf16), qkv[keys, head_lanes(head, 2)]) * (1.0 / total)
            o = head_mask(head, o)
            g = head // 2
            groups[g] = o if groups[g] is None else groups[g] + o
        att_snd[b, :, 0:128] = groups[0].astype(bf16)
        att_snd[b, :, 128:256] = groups[1].astype(bf16)
        return carry

    lax.fori_loop(0, 4, attend, 0)
    att_out, att_into = cross(att_snd, att, att_s, att_r)
    for c in att_out:
        c.start()
    att[h] = att_snd[h]

    spread_recv(snd_a, g_own, gd_s, gd_r)
    there = jnp.max(jnp.abs(g_own[...].astype(f32)), axis=1, keepdims=True) > 0.0
    there_f = jnp.where(there, 1.0, 0.0)
    earlier = jnp.where(iota((SLOTS, SLOTS), 1) < iota((SLOTS, SLOTS), 0), 1.0, 0.0).astype(bf16)
    place = dot(earlier, jnp.broadcast_to(there_f, (SLOTS, 128)).astype(bf16))[:, 0:1]
    place = jnp.where(there, place, -1.0).astype(i32)
    pack[...] = jnp.where(iota((SLOTS, SLOTS), 1) == place, 1.0, 0.0).astype(bf16)
    gc[...] = dot(pack[...], g_own[...], TN).astype(bf16)
    cnt[d, h] = jnp.broadcast_to(jnp.sum(there_f, axis=0, keepdims=True), (8, 128))
    for i in range(3):
        g_out[i].start()
    g_mine = pltpu.make_async_copy(gc, g_all.at[d * 4 + h], own_sem.at[0])
    g_mine.start()
    c_out = [
        remote(cnt.at[d, h], cnt.at[d, h], ct_s.at[i], ct_r.at[i], (p, e, d))
        for i, p in enumerate(x_peers)
    ]
    c_into = [
        remote(cnt.at[d, p], cnt.at[d, p], ct_s.at[i], ct_r.at[i], (p, e, d))
        for i, p in enumerate(x_from)
    ]
    c_pair = remote(cnt.at[d], cnt.at[d], ct_s.at[3], ct_r.at[3], (h, e, other))
    c_pair_in = remote(cnt.at[other], cnt.at[other], ct_s.at[3], ct_r.at[3], (h, e, other))
    for c in c_out:
        c.start()

    for c in wo_into:
        c.wait_recv()
    for c in att_into:
        c.wait_recv()
    for i in range(4):
        part = dot(att[i], wo_full[i])
        hid[...] = (tok[...].astype(f32) if i == 0 else hid[...]) + part
    two, _ = norm_parts(hid[...])
    snd_b[...] = dot(disp[...], (two * gain2[...]).astype(bf16)).astype(bf16)
    spread(snd_b, x_own, xd_s, xd_r)

    for c in c_into:
        c.wait_recv()
    c_pair.start()
    dn_load.wait()

    def back_down(c, carry):
        part = pl.ds(pl.multiple_of(c * FF_CHUNK, FF_CHUNK), FF_CHUNK)
        ag[:, part] = dot(g_own[...], dn[part, :], NT)
        return carry

    lax.fori_loop(0, FF // FF_CHUNK, back_down, 0)
    up_load.wait()
    for i in range(2):
        g_into[i].wait_recv()
    g_out[3].start()
    g_out[4].start()
    g_into[2].wait_recv()
    g_out[5].start()
    g_out[6].start()
    spread_sent(snd_a, g_own, gd_s, gd_r)
    spread_recv(snd_b, x_own, xd_s, xd_r)

    eacc[...] = jnp.zeros_like(eacc)

    def expert(c, carry):
        part = pl.ds(pl.multiple_of(c * FF_CHUNK, FF_CHUNK), FF_CHUNK)
        value, slope = gelu_pair(dot(x_own[...], up[:, part]))
        act[:, part] = value.astype(bf16)
        pre_grad = (ag[:, part] * slope).astype(bf16)
        eacc[...] += dot(pre_grad, up[:, part], NT)
        return carry

    lax.fori_loop(0, FF // FF_CHUNK, expert, 0)
    snd_a[...] = eacc[...].astype(bf16)
    spread(snd_a, eg_rcv, eg_s, eg_r)
    xc[...] = dot(pack[...], x_own[...], TN).astype(bf16)
    spread_sent(snd_b, x_own, xd_s, xd_r)
    eacc[...] = jnp.zeros_like(eacc)

    def produce(c, carry):
        part = pl.ds(pl.multiple_of(c * FF_CHUNK, FF_CHUNK), FF_CHUNK)
        eacc[...] += dot(act[:, part], dn[part, :])
        return carry

    lax.fori_loop(0, FF // FF_CHUNK, produce, 0)
    snd_b[...] = eacc[...].astype(bf16)
    spread(snd_b, out_rcv, out_s, out_r)
    for i in range(3):
        t_out[i].start()
    x_mine = pltpu.make_async_copy(xc, x_all.at[d * 4 + h], own_sem.at[1])
    x_mine.start()
    g_into[3].wait_recv()
    g_into[4].wait_recv()
    g_out[7].start()
    wjt[...] = wj[...].astype(f32).T
    spread_recv(snd_a, eg_rcv, eg_s, eg_r)

    two, scale2 = norm_parts(hid[...])
    back = dot(disp_t[...], eg_rcv[...])
    sm_x[h, 1:2, :] = jnp.sum(back * two, axis=0, keepdims=True)
    hgrad[...] = og[...].astype(f32) + norm_pull(back, two, scale2, gain2[...])
    mixed[...] = hgrad[...].astype(bf16)

    def back_output(i, carry):
        agr_snd[i] = dot(mixed[...], wo_full[i], NT).astype(bf16)
        return carry

    lax.fori_loop(0, 4, back_output, 0)
    agr_out, agr_into = cross(agr_snd, agr, agr_s, agr_r)
    for c in agr_out:
        c.start()
    agr[h] = agr_snd[h]

    def output_grad(i, carry):
        wog_snd[i] = dot(att[i], mixed[...], TN).astype(bf16)
        return carry

    lax.fori_loop(0, 4, output_grad, 0)
    wog_out, wog_into = cross(wog_snd, wog_rcv, wog_s, wog_r, HEAD_COLS)
    for c in wog_out:
        c.start()
    dq[...] = jnp.zeros_like(dq)
    dk[...] = jnp.zeros_like(dk)
    dv[...] = jnp.zeros_like(dv)
    for c in agr_into:
        c.wait_recv()

    def attend_back(b, carry):
        keys, allowed = window(b)
        mine = rows(b * TOK, TOK)
        for head in range(3):
            g = pl.ds((head // 2) * 128, 128)
            q = head_mask(head, qkv[mine, head_lanes(head, 0)])
            k = qkv[keys, head_lanes(head, 1)]
            v = qkv[keys, head_lanes(head, 2)]
            u = head_mask(head, agr[b, :, g])
            s = jnp.where(allowed, dot(q, k, NT), NEGATIVE)
            p = jnp.exp(s - jnp.max(s, axis=-1, keepdims=True))
            chances = p * (1.0 / jnp.sum(p, axis=-1, keepdims=True))
            chance_grad = dot(u, v, NT)
            inner = jnp.sum(chance_grad * chances, axis=-1, keepdims=True)
            score_grad = (chances * (chance_grad - inner)).astype(bf16)
            dq[mine, g] += head_mask(head, dot(score_grad, k)) * 0.125
            dk[keys, g] += dot(score_grad, q, TN)
            dv[keys, g] += dot(chances.astype(bf16), u, TN)
        return carry

    lax.fori_loop(0, 4, attend_back, 0)
    jg[:, 0:PAD_COLS] = dq[...].astype(bf16)
    jg[:, PAD_COLS : 2 * PAD_COLS] = dk[...].astype(bf16)
    jg[:, 2 * PAD_COLS : 3 * PAD_COLS] = dv[...].astype(bf16)

    ng_out, ng_into = cross(ng_snd, ng_rcv, ng_s, ng_r)
    for i, p in enumerate((across, right, left)):
        ng_snd[p] = dot(jg[rows(p * TOK, TOK), :], wj[...], NT).astype(bf16)
        ng_out[(2, 0, 1)[i]].start()

    for c in wog_into:
        c.wait_recv()
    wog = wog_snd[h, 0:HEAD_COLS, :].astype(f32)
    for p in x_from:
        wog = wog + wog_rcv[p, 0:HEAD_COLS, :].astype(f32)
    gfull[3 * HEAD_COLS : 4 * HEAD_COLS, :] = wog.astype(bf16)
    gain1_part = jnp.zeros((1, D), f32)
    for part in range(3):
        grad = jnp.zeros((PAD_COLS, D), f32)
        for b in range(4):
            grad = grad + dot(jg[b * TOK : (b + 1) * TOK, part * PAD_COLS : (part + 1) * PAD_COLS], gath[b], TN)
        gain1_part = gain1_part + jnp.sum(
            grad * wjt[part * PAD_COLS : (part + 1) * PAD_COLS, :], axis=0, keepdims=True
        )
        gfull[part * HEAD_COLS : (part + 1) * HEAD_COLS, :] = grad[0:HEAD_COLS, :].astype(bf16)
    sm_x[h, 0:1, :] = gain1_part / gain1[...]

    core = lax.rem(e, 2)
    mine_half = rows(core * 384, 384)
    twin_half = rows((1 - core) * 384, 384)
    ca_out = remote(gfull.at[twin_half], rs_core, ca_s.at[0], ca_r.at[0], (h, twin, d))
    ca_out.start()
    sx_out, sx_into = gather(sm_x, sx_s, sx_r)
    for c in sx_out:
        c.start()

    own_grad = dot(jg[rows(h * TOK, TOK), :], wj[...], NT)
    ca_out.wait_recv()
    gpart[...] = (gfull[mine_half, :].astype(f32) + rs_core[...].astype(f32)).astype(bf16)

    unit = lax.div(e, 2)

    def peer(k):
        return lax.rem(unit + k, 8)

    def a2_copy(k, where):
        p = peer(k)
        return remote(
            gpart.at[rows(p * 48, 48)], rs_rcv.at[where], a2_s.at[k], a2_r.at[k], (h, p * 2 + core, d)
        )

    for k in range(1, 8):
        a2_copy(k, unit).start()
    rs_rcv[unit] = gpart[rows(unit * 48, 48), :]
    for c in sx_into:
        c.wait_recv()
    sm_e[e] = (sm_x[0] + sm_x[1]) + (sm_x[2] + sm_x[3])

    def small_copy(k, p, where):
        return remote(sm_e.at[e], sm_e.at[where], se_s.at[k], se_r.at[k], (h, p, d))

    def small_start(k, carry):
        p = lax.rem(e + k, EXPERTS)
        small_copy(k, p, e).start()
        return carry

    lax.fori_loop(1, EXPERTS, small_start, 0)

    for c in ng_into:
        c.wait_recv()
    for p in x_from:
        own_grad = own_grad + ng_rcv[p].astype(f32)
    one, scale1 = norm_parts(tok[...].astype(f32))
    tgrad[...] = hgrad[...] + norm_pull(own_grad, one, scale1, gain1[...])

    for k in range(1, 8):
        a2_copy(k, peer(8 - k)).wait_recv()
    reduced = rs_rcv[0].astype(f32)
    for k in range(1, 8):
        reduced = reduced + rs_rcv[k].astype(f32)
    rs_pair[d] = reduced.astype(bf16)
    a3 = remote(rs_pair.at[d], rs_pair.at[d], a3_s.at[0], a3_r.at[0], (h, e, other))
    a3_in = remote(rs_pair.at[other], rs_pair.at[other], a3_s.at[0], a3_r.at[0], (h, e, other))
    a3.start()

    def small_recv(k, carry):
        p = lax.rem(e + EXPERTS - k, EXPERTS)
        small_copy(k, p, p).wait_recv()
        return carry

    lax.fori_loop(1, EXPERTS, small_recv, 0)
    gathered = sm_e[0]
    for k in range(1, EXPERTS):
        gathered = gathered + sm_e[k]
    sm_d[d] = gathered
    sd = remote(sm_d.at[d], sm_d.at[d], sd_s.at[0], sd_r.at[0], (h, e, other))
    sd_in = remote(sm_d.at[other], sm_d.at[other], sd_s.at[0], sd_r.at[0], (h, e, other))
    sd.start()

    spread_recv(snd_b, out_rcv, out_s, out_r)
    final[...] = hid[...] + dot(disp_t[...], out_rcv[...])

    a3_in.wait_recv()
    here = rows(core * 384 + unit * 48, 48)
    gsum[here, :] = (rs_pair[0].astype(f32) + rs_pair[1].astype(f32)).astype(bf16)

    def a4_copy(k, p, place):
        return remote(gsum.at[place], gsum.at[place], a4_s.at[k], a4_r.at[k], (h, p * 2 + core, d))

    for k in range(1, 8):
        a4_copy(k, peer(k), here).start()

    for i in range(2):
        t_into[i].wait_recv()
    t_out[3].start()
    t_out[4].start()
    t_into[2].wait_recv()
    t_out[5].start()
    t_out[6].start()
    sd_in.wait_recv()
    small[...] = sm_d[0] + sm_d[1]
    for k in range(1, 8):
        p = peer(8 - k)
        a4_copy(k, p, rows(core * 384 + p * 48, 48)).wait_recv()
    for k in range(1, 8):
        a4_copy(k, peer(k), here).wait_send()
    a5 = remote(gsum.at[mine_half], gsum.at[mine_half], ca_s.at[1], ca_r.at[1], (h, twin, d))
    a5_in = remote(gsum.at[twin_half], gsum.at[twin_half], ca_s.at[1], ca_r.at[1], (h, twin, d))
    a5.start()
    a5_in.wait_recv()
    t_into[3].wait_recv()
    t_into[4].wait_recv()
    t_out[7].start()
    for i in range(5, 8):
        g_into[i].wait_recv()
        t_into[i].wait_recv()
    c_pair_in.wait_recv()

    g_mine.wait()
    x_mine.wait()
    spread_sent(snd_a, eg_rcv, eg_s, eg_r)
    spread_sent(snd_b, out_rcv, out_s, out_r)

    def small_sent(k, carry):
        p = lax.rem(e + k, EXPERTS)
        small_copy(k, p, e).wait_send()
        return carry

    lax.fori_loop(1, EXPERTS, small_sent, 0)
    for k in range(1, 8):
        a2_copy(k, unit).wait_send()
    for c in (
        nrm_out + wo_out + att_out + g_out + t_out + c_out + [c_pair] + agr_out + wog_out + ng_out
        + sx_out + [ca_out, a5, a3, sd]
    ):
        c.wait_send()


def block_call(*args):
    vmem = pl.BlockSpec(memory_space=pltpu.VMEM)
    hbm = pl.BlockSpec(memory_space=pl.ANY)
    smem = pl.BlockSpec(memory_space=pltpu.SMEM)
    dma = pltpu.SemaphoreType.DMA

    def buf(*shape, dtype=bf16):
        return pltpu.VMEM(shape, dtype)

    scratch = [
        buf(D, D), buf(D, D, dtype=f32), buf(4, TOK, D), buf(ROW, D), buf(4, TOK, PAD_COLS), buf(4, TOK, PAD_COLS),
        buf(4, PAD_COLS, D), buf(D, FF), buf(FF, D), buf(SLOTS, D), buf(SLOTS, D), buf(SLOTS, D),
        buf(SLOTS, D), buf(SLOTS, D), buf(SLOTS, D),
        buf(SLOTS, SLOTS), buf(SLOTS, FF, dtype=f32), buf(SLOTS, FF), buf(SLOTS, D, dtype=f32),
        buf(SLOTS, D), buf(SLOTS, D), buf(SLOTS, TOK), buf(TOK, SLOTS),
        buf(TOK, D, dtype=f32), buf(TOK, D, dtype=f32), buf(TOK, D), buf(4, TOK, PAD_COLS), buf(4, TOK, PAD_COLS),
        buf(ROW, PAD_COLS, dtype=f32), buf(ROW, PAD_COLS, dtype=f32), buf(ROW, PAD_COLS, dtype=f32),
        buf(ROW, D), buf(4, TOK, D), buf(4, TOK, D), buf(4, PAD_COLS, D), buf(4, PAD_COLS, D),
        buf(D, D), buf(384, D), buf(384, D), buf(8, 48, D), buf(2, 48, D),
        buf(4, 8, D, dtype=f32), buf(EXPERTS, 8, D, dtype=f32), buf(2, 8, D, dtype=f32),
        dma((2,)), dma((2,)),
    ]
    for n in (3, 3, 16, 16, 16, 16, 3, 3, 3, 3, 8, 8, 4, 2, 8, 1, 8, 3, 16, 1):
        scratch += [dma((n,)), dma((n,))]
    return pl.pallas_call(
        block_kernel,
        out_shape=[
            jax.ShapeDtypeStruct((TOK, D), f32),
            jax.ShapeDtypeStruct((TOK, D), f32),
            jax.ShapeDtypeStruct((D, D), bf16),
            jax.ShapeDtypeStruct((8, D), f32),
            jax.ShapeDtypeStruct((8, SLOTS, D), bf16),
            jax.ShapeDtypeStruct((8, SLOTS, D), bf16),
            jax.ShapeDtypeStruct((2, 4, 8, 128), f32),
        ],
        in_specs=[vmem] * 8 + [hbm, hbm, vmem, vmem, smem, vmem],
        out_specs=[vmem] * 4 + [hbm, hbm, vmem],
        scratch_shapes=scratch,
        compiler_params=pltpu.CompilerParams(
            collective_id=1, has_side_effects=True, vmem_limit_bytes=64 * 2**20 - 2**16
        ),
    )(*args)


GRAD_TILE = 512
REST_TILE = 256


def expert_grad_kernel(n_ref, x_ref, g_ref, up_ref, dn_ref, du_ref, dd_ref, xs, gs):
    total = 0
    ends = []
    for b in range(8):
        ends.append(total)
        total = total + lax.div(n_ref[b] + 15, 16) * 16

    @pl.when(pl.program_id(0) == 0)
    def _():
        for b in range(8):
            there = pl.ds(pl.multiple_of(ends[b], 16), SLOTS)
            xs[there, :] = x_ref[b]
            gs[there, :] = g_ref[b]
        tail = pl.ds(pl.multiple_of(total, 16), SLOTS)
        xs[tail, :] = jnp.zeros((SLOTS, D), bf16)
        gs[tail, :] = jnp.zeros((SLOTS, D), bf16)

    du_ref[...] = jnp.zeros_like(du_ref)
    dd_ref[...] = jnp.zeros_like(dd_ref)

    def tile(start, size):
        r = pl.ds(pl.multiple_of(start, size), size)
        x, g = xs[r, :], gs[r, :]
        value, slope = gelu_pair(dot(x, up_ref[...]))
        pre_grad = (dot(g, dn_ref[...], NT) * slope).astype(bf16)
        du_ref[...] += dot(x, pre_grad, TN)
        dd_ref[...] += dot(value.astype(bf16), g, TN)

    def whole(i, carry):
        tile(i * GRAD_TILE, GRAD_TILE)
        return carry

    def rest(i, carry):
        tile(i * REST_TILE, REST_TILE)
        return carry

    full = lax.div(total, GRAD_TILE)
    lax.fori_loop(0, full, whole, 0)
    lax.fori_loop(full * (GRAD_TILE // REST_TILE), lax.div(total + REST_TILE - 1, REST_TILE), rest, 0)


def expert_grads(counts, x_all, g_all, up, dn):
    return pl.pallas_call(
        expert_grad_kernel,
        grid_spec=pltpu.PrefetchScalarGridSpec(
            num_scalar_prefetch=1,
            grid=(FF // FF_CHUNK,),
            in_specs=[
                pl.BlockSpec((8, SLOTS, D), lambda i, n: (0, 0, 0)),
                pl.BlockSpec((8, SLOTS, D), lambda i, n: (0, 0, 0)),
                pl.BlockSpec((D, FF_CHUNK), lambda i, n: (0, i)),
                pl.BlockSpec((FF_CHUNK, D), lambda i, n: (i, 0)),
            ],
            out_specs=[
                pl.BlockSpec((D, FF_CHUNK), lambda i, n: (0, i)),
                pl.BlockSpec((FF_CHUNK, D), lambda i, n: (i, 0)),
            ],
            scratch_shapes=[
                pltpu.VMEM((9 * SLOTS, D), bf16),
                pltpu.VMEM((9 * SLOTS, D), bf16),
            ],
        ),
        out_shape=[jax.ShapeDtypeStruct((D, FF), f32), jax.ShapeDtypeStruct((FF, D), f32)],
        compiler_params=pltpu.CompilerParams(vmem_limit_bytes=64 * 2**20 - 2**16),
    )(counts, x_all, g_all, up, dn)


def body(
    tokens, out_grad, w_query, w_key, w_value, w_output, gain_one, gain_two, expert_up, expert_down,
    hash_table, token_ids, doc_lengths, turn_mask,
):
    final, tokens_grad, gsum, small, x_all, g_all, cnt = block_call(
        tokens[0], out_grad[0], w_query, w_key, w_value, w_output,
        gain_one.reshape(1, D), gain_two.reshape(1, D), expert_up[0], expert_down[0],
        hash_table.reshape(256, 128), token_ids, doc_lengths, turn_mask,
    )
    counts = cnt[:, :, 0, 0].reshape(8).astype(i32)
    up_grad, down_grad = expert_grads(counts, x_all, g_all, expert_up[0], expert_down[0])
    grads = gsum.astype(f32)
    return (
        final[None],
        tokens_grad[None],
        grads[0:HEAD_COLS].T,
        grads[HEAD_COLS : 2 * HEAD_COLS].T,
        grads[2 * HEAD_COLS : 3 * HEAD_COLS].T,
        grads[3 * HEAD_COLS :],
        small[0],
        small[1],
        up_grad[None],
        down_grad[None],
        small[2, :EXPERTS].astype(i32),
    )


def solution(mesh):
    rows_spec = P(("expert", "dp"), "head", None)
    in_specs = (
        rows_spec, rows_spec, P(None, "head"), P(None, "head"), P(None, "head"), P("head", None),
        P(), P(), P("expert", None, None), P("expert", None, None), P(),
        P(("expert", "dp"), "head"), P(("expert", "dp"), None), P(("expert", "dp"), None),
    )
    out_specs = (
        rows_spec, rows_spec, P(None, "head"), P(None, "head"), P(None, "head"), P("head", None),
        P(), P(), P("expert", None, None), P("expert", None, None), P(),
    )
    return jax.shard_map(body, mesh=mesh, in_specs=in_specs, out_specs=out_specs, check_vma=False)
```

```python
import functools

import jax
import jax.numpy as jnp
from jax import lax
from jax.experimental import pallas as pl
from jax.experimental.pallas import tpu as pltpu
from jax.sharding import PartitionSpec as P

MESH = pl.DeviceIdType.MESH
f32 = jnp.float32
bf16 = jnp.bfloat16
i32 = jnp.int32

HEADS_X = 4
EXPERTS = 16
TOK = 256
ROW = 1024
D = 768
FF = 3072
CAP = 32
SLOTS = EXPERTS * CAP
WIN = 768
HEAD_COLS = 192
PAD_COLS = 256
FF_CHUNK = 512
HALF = SLOTS // 2
BLOCKS = 7
FILL_TILE = 448
EPSILON = 1e-05
NEGATIVE = -1e30
GELU_A = 0.7978845608028654
GELU_B = 0.044715

NN = (((1,), (0,)), ((), ()))
NT = (((1,), (1,)), ((), ()))
TN = (((0,), (0,)), ((), ()))


def dot(a, b, dims=NN):
    return lax.dot_general(a, b, dims, preferred_element_type=f32)


def iota(shape, dim):
    return lax.broadcasted_iota(i32, shape, dim)


def norm_parts(x):
    average = jnp.mean(x, axis=-1, keepdims=True)
    centred = x - average
    variance = jnp.mean(centred * centred, axis=-1, keepdims=True)
    scale = lax.rsqrt(variance + EPSILON)
    return centred * scale, scale


def norm_pull(upstream, normed, scale, gain):
    m = upstream * gain
    first = jnp.mean(m, axis=-1, keepdims=True)
    second = jnp.mean(m * normed, axis=-1, keepdims=True)
    return scale * (m - first - normed * second)


def gelu_pair(u):
    u2 = u * u
    half = 0.5 + 0.5 * jnp.tanh(u * (GELU_A + (GELU_A * GELU_B) * u2))
    slope = half + (u + u) * (half * (1.0 - half)) * (GELU_A + (3.0 * GELU_A * GELU_B) * u2)
    return u * half, slope


def rows(start, size):
    return pl.ds(pl.multiple_of(start, size), size)


def block_kernel(
    tok, og, wqt, wkt, wvt, wo, gain1_in, gain2_in, up_hbm, dn_hbm, table, ids, lengths, prompt,
    final, tgrad, gsum, small, x_hi, g_hi, cnt, du_hbm, dd_hbm,
    count, wjt, gath, qkv, att_snd, att, wo_full, up, dn, snd_a, snd_b, g_own, x_own, gc, xc,
    pack, ag, act, eacc, eg_rcv, out_rcv, disp, disp_t, hid, hgrad, mixed, agr_snd, agr,
    lse, x_lo, g_lo, du, dk, dv, jg, wog_snd, wog_pair, wog_rcv, gfull, gpart, rs_core, rs_rcv, rs_pair,
    sm_x, sm_e, sm_d,
    load_sem, fill_sem, nrm_s, nrm_r, wo_s, wo_r, gd_s, gd_r, xd_s, xd_r, eg_s, eg_r, out_s, out_r,
    att_s, att_r, agr_s, agr_r, ng_s, ng_r, wog_s, wog_r, gl_s, gl_r, gh_s, gh_r, xl_s, xl_r, xh_s, xh_r, ct_s, ct_r,
    ca_s, ca_r, a2_s, a2_r, a3_s, a3_r, a4_s, a4_r, sx_s, sx_r, se_s, se_r, sd_s, sd_r,
):
    h = lax.axis_index("head")
    e = lax.axis_index("expert")
    d = lax.axis_index("dp")
    right, left, across = lax.rem(h + 1, 4), lax.rem(h + 3, 4), lax.rem(h + 2, 4)
    x_peers = (right, left, across)
    x_from = (left, right, across)
    other = 1 - d
    twin = e + 1 - 2 * lax.rem(e, 2)

    def remote(src, dst, ss, rs, device):
        return pltpu.make_async_remote_copy(
            src_ref=src, dst_ref=dst, send_sem=ss, recv_sem=rs, device_id=device, device_id_type=MESH
        )

    def spread(snd, rcv, ss, rs):
        def step(k, carry):
            p = lax.rem(e + k, EXPERTS)
            remote(
                snd.at[rows(p * CAP, CAP)], rcv.at[rows(e * CAP, CAP)], ss.at[k], rs.at[k], (h, p, d)
            ).start()
            return carry

        lax.fori_loop(1, EXPERTS, step, 0)
        rcv[rows(e * CAP, CAP), :] = snd[rows(e * CAP, CAP), :]

    def spread_recv(snd, rcv, ss, rs):
        def step(k, carry):
            p = lax.rem(e + EXPERTS - k, EXPERTS)
            remote(
                snd.at[rows(p * CAP, CAP)], rcv.at[rows(p * CAP, CAP)], ss.at[k], rs.at[k], (h, p, d)
            ).wait_recv()
            return carry

        lax.fori_loop(1, EXPERTS, step, 0)

    def spread_sent(snd, rcv, ss, rs):
        def step(k, carry):
            p = lax.rem(e + k, EXPERTS)
            remote(
                snd.at[rows(p * CAP, CAP)], rcv.at[rows(e * CAP, CAP)], ss.at[k], rs.at[k], (h, p, d)
            ).wait_send()
            return carry

        lax.fori_loop(1, EXPERTS, step, 0)

    def cross(snd, rcv, ss, rs, only=None):
        view = (lambda r, i: r.at[i]) if only is None else (lambda r, i: r.at[i, pl.ds(0, only)])
        out = [
            remote(view(snd, p), view(rcv, h), ss.at[i], rs.at[i], (p, e, d))
            for i, p in enumerate(x_peers)
        ]
        into = [
            remote(view(snd, p), view(rcv, p), ss.at[i], rs.at[i], (p, e, d))
            for i, p in enumerate(x_from)
        ]
        return out, into

    def gather(buf, ss, rs, only=None):
        view = (lambda r, i: r.at[i]) if only is None else (lambda r, i: r.at[i, pl.ds(0, only)])
        out = [
            remote(view(buf, h), view(buf, h), ss.at[i], rs.at[i], (p, e, d))
            for i, p in enumerate(x_peers)
        ]
        into = [
            remote(view(buf, p), view(buf, p), ss.at[i], rs.at[i], (p, e, d))
            for i, p in enumerate(x_from)
        ]
        return out, into

    def relay_gather(buf, ss, rs):
        low, high = pl.ds(0, TOK // 2), pl.ds(TOK // 2, TOK // 2)

        def pair(i, there, view):
            return remote(view, view, ss.at[i], rs.at[i], (there, e, d))

        out = [
            pair(0, right, buf.at[h]),
            pair(1, left, buf.at[h]),
            pair(2, right, buf.at[left, low]),
            pair(3, left, buf.at[right, high]),
        ]
        into = [
            pair(0, left, buf.at[left]),
            pair(1, right, buf.at[right]),
            pair(2, left, buf.at[across, low]),
            pair(3, right, buf.at[across, high]),
        ]
        return out, into

    def token_copies(own, dst, ss, rs):
        def at(i, part=None):
            return dst.at[rows(i * HALF, HALF)] if part is None else dst.at[pl.ds(i * HALF + part, HALF // 2)]

        moves = [
            (own, at(2), right, d),
            (own, at(0), left, d),
            (own, at(3), h, other),
            (at(2, 0), at(1, 0), right, d),
            (at(0, HALF // 2), at(1, HALF // 2), left, d),
            (at(3), at(6), right, d),
            (at(3), at(4), left, d),
            (at(1), at(5), h, other),
        ]
        return [
            remote(src, to, ss.at[i], rs.at[i], (hh, e, dd)) for i, (src, to, hh, dd) in enumerate(moves)
        ]

    g_low = token_copies(gc.at[pl.ds(0, HALF)], g_lo, gl_s, gl_r)
    g_high = token_copies(gc.at[pl.ds(HALF, HALF)], g_hi, gh_s, gh_r)
    x_low = token_copies(xc.at[pl.ds(0, HALF)], x_lo, xl_s, xl_r)
    x_high = token_copies(xc.at[pl.ds(HALF, HALF)], x_hi, xh_s, xh_r)

    def start(copies, *which):
        for i in which:
            copies[i].start()

    def arrive(copies, *which):
        for i in which:
            copies[i].wait_recv()

    up_load = pltpu.make_async_copy(up_hbm, up, load_sem.at[0])
    dn_load = pltpu.make_async_copy(dn_hbm, dn, load_sem.at[1])
    up_load.start()
    dn_load.start()

    barrier = pltpu.get_barrier_semaphore()
    for p in x_peers:
        pl.semaphore_signal(barrier, inc=1, device_id=(p, e, d), device_id_type=MESH)
    pl.semaphore_signal(barrier, inc=1, device_id=(h, e, other), device_id_type=MESH)

    def greet(k, carry):
        pl.semaphore_signal(
            barrier, inc=1, device_id=(h, lax.rem(e + k, EXPERTS), d), device_id_type=MESH
        )
        return carry

    lax.fori_loop(1, EXPERTS, greet, 0)

    gain1 = gain1_in[...].reshape(1, D)
    gain2 = gain2_in[...].reshape(1, D)
    one, _ = norm_parts(tok[...].astype(f32))
    gath[h] = (one * gain1).astype(bf16)
    for i, w in enumerate((wqt, wkt, wvt)):
        wjt[i * PAD_COLS : i * PAD_COLS + HEAD_COLS, :] = w[...]
        wjt[i * PAD_COLS + HEAD_COLS : (i + 1) * PAD_COLS, :] = jnp.zeros(
            (PAD_COLS - HEAD_COLS, D), bf16
        )
    for i in range(4):
        wo_full[i, HEAD_COLS:PAD_COLS, :] = jnp.zeros((PAD_COLS - HEAD_COLS, D), bf16)
    wo_full[h, 0:HEAD_COLS, :] = wo[...]

    pl.semaphore_wait(barrier, 3 + 1 + EXPERTS - 1)
    nrm_out, nrm_into = relay_gather(gath, nrm_s, nrm_r)
    nrm_out[0].start()
    nrm_out[1].start()

    eye = iota((TOK, TOK), 0) == iota((TOK, TOK), 1)
    id_col = jnp.sum(jnp.where(eye, ids[...].astype(f32), 0.0), axis=1, keepdims=True).astype(i32)
    high, low = lax.shift_right_logical(id_col, 7), lax.bitwise_and(id_col, 127)
    pick = jnp.where(iota((TOK, 256), 1) == high, 1.0, 0.0).astype(bf16)
    near = dot(pick, table[...].astype(f32).astype(bf16))
    lane = iota((TOK, 128), 1)
    chosen = jnp.sum(jnp.where(lane == low, near, 0.0), axis=1, keepdims=True)
    member = jnp.where(lane == chosen.astype(i32), 1.0, 0.0)
    before = jnp.where(iota((TOK, TOK), 1) < iota((TOK, TOK), 0), 1.0, 0.0).astype(bf16)
    rank = jnp.sum(dot(before, member.astype(bf16)) * member, axis=1, keepdims=True)
    slot = chosen * CAP + rank
    slot_row = jnp.sum(jnp.where(eye, slot, 0.0), axis=0, keepdims=True).astype(i32)
    disp_t[...] = jnp.where(iota((TOK, SLOTS), 1) == slot.astype(i32), 1.0, 0.0).astype(bf16)
    disp[...] = jnp.where(iota((SLOTS, TOK), 0) == slot_row, 1.0, 0.0).astype(bf16)
    sm_x[h] = jnp.zeros((8, D), f32)
    sm_x[h, 2:3, 0:128] = jnp.sum(member, axis=0, keepdims=True)

    snd_a[...] = dot(disp[...], og[...]).astype(bf16)
    spread(snd_a, g_own, gd_s, gd_r)

    column_scale = jnp.where(iota((1, D), 1) < PAD_COLS, 0.125, 1.0)

    def project(b):
        qkv[rows(b * TOK, TOK), :] = (dot(gath[b], wjt[...], NT) * column_scale).astype(bf16)

    core = lax.rem(e, 2)
    wo_mine = pl.ds(pl.multiple_of(core * 96, 96), 96)
    wo_twin = pl.ds(pl.multiple_of((1 - core) * 96, 96), 96)

    def wo_copy(i, block, part, device):
        view = wo_full.at[block, part]
        return remote(view, view, wo_s.at[i], wo_r.at[i], device)

    wo_out = [wo_copy(i, h, wo_mine, (p, e, d)) for i, p in enumerate(x_peers)]
    wo_into = [wo_copy(i, p, wo_mine, (p, e, d)) for i, p in enumerate(x_from)]
    wo_out2 = [wo_copy(3 + i, p, wo_mine, (h, twin, d)) for i, p in enumerate(x_from)]
    wo_into2 = [wo_copy(3 + i, p, wo_twin, (h, twin, d)) for i, p in enumerate(x_from)]
    project(h)
    nrm_into[0].wait_recv()
    nrm_out[2].start()
    nrm_into[1].wait_recv()
    nrm_out[3].start()
    for c in wo_out:
        c.start()
    project(left)
    project(right)
    nrm_into[2].wait_recv()
    nrm_into[3].wait_recv()
    project(across)

    spread_recv(snd_a, g_own, gd_s, gd_r)
    there = jnp.max(jnp.abs(g_own[...].astype(f32)), axis=1, keepdims=True) > 0.0
    there_f = jnp.where(there, 1.0, 0.0)
    earlier = jnp.where(iota((SLOTS, SLOTS), 1) < iota((SLOTS, SLOTS), 0), 1.0, 0.0).astype(bf16)
    place = dot(earlier, jnp.broadcast_to(there_f, (SLOTS, 128)).astype(bf16))[:, 0:1]
    place = jnp.where(there, place, -1.0).astype(i32)
    pack[...] = jnp.where(iota((SLOTS, SLOTS), 1) == place, 1.0, 0.0).astype(bf16)
    gc[...] = dot(pack[...], g_own[...], TN).astype(bf16)
    count[...] = jnp.broadcast_to(jnp.sum(there_f, axis=0, keepdims=True), (8, 128))
    c_out = [
        remote(count, cnt.at[slot_at], ct_s.at[i], ct_r.at[i], device)
        for i, (slot_at, device) in enumerate(
            ((2, (right, e, d)), (0, (left, e, d)), (1, (across, e, d)), (3, (h, e, other)))
        )
    ]
    c_pair = remote(cnt.at[pl.ds(0, 3)], cnt.at[pl.ds(4, 3)], ct_s.at[4], ct_r.at[4], (h, e, other))
    start(g_low, 0, 1, 2)
    start(c_out, 0, 1, 2, 3)

    ends = []
    total = 0
    for j in range(8):
        total = total + lengths[0, j]
        ends.append(total)

    def segment(pos):
        found = jnp.zeros(pos.shape, i32)
        for j in range(8):
            found = found + jnp.where(ends[j] <= pos, 1, 0)
        return found

    def window(b):
        first = jnp.minimum(jnp.maximum(b - 1, 0), 1) * TOK
        q_pos = b * TOK + iota((TOK, 1), 0)
        k_pos = first + iota((1, WIN), 1)
        said = prompt[:, pl.ds(pl.multiple_of(first, TOK), WIN)]
        k_least = jnp.where(said == 1, -1, k_pos)
        allowed = (segment(q_pos) == segment(k_pos)) & (k_least <= q_pos)
        return pl.ds(pl.multiple_of(first, TOK), WIN), allowed

    lane_low = iota((TOK, 128), 1) < 64

    def head_mask(head, x):
        if head == 2:
            return x
        return jnp.where(lane_low if head == 0 else jnp.logical_not(lane_low), x, jnp.zeros_like(x))

    def head_lanes(head, part):
        return pl.ds(part * PAD_COLS + (head // 2) * 128, 128)

    def attend(b, carry):
        keys, allowed = window(b)
        mine = rows(b * TOK, TOK)
        groups = [None, None]
        for head in range(3):
            q = head_mask(head, qkv[mine, head_lanes(head, 0)])
            s = dot(q, qkv[keys, head_lanes(head, 1)], NT)
            s = jnp.where(allowed, s, NEGATIVE)
            top = jnp.max(s, axis=-1, keepdims=True)
            p = jnp.exp(s - top)
            total = jnp.sum(p, axis=-1, keepdims=True)
            lse[mine, head : head + 1] = top + jnp.log(total)
            o = dot(p.astype(bf16), qkv[keys, head_lanes(head, 2)]) * (1.0 / total)
            o = head_mask(head, o)
            g = head // 2
            groups[g] = o if groups[g] is None else groups[g] + o
        att_snd[b, :, 0:128] = groups[0].astype(bf16)
        att_snd[b, :, 128:256] = groups[1].astype(bf16)
        return carry

    lax.fori_loop(0, 4, attend, 0)
    att_out, att_into = cross(att_snd, att, att_s, att_r)
    for c in att_out:
        c.start()
    att[h] = att_snd[h]

    for i in range(3):
        wo_into[i].wait_recv()
        wo_out2[i].start()
    for c in att_into:
        c.wait_recv()
    arrive(g_low, 0, 1)
    start(g_low, 3, 4)
    arrive(g_low, 2)
    start(g_low, 5, 6)
    start(g_high, 0, 1)
    for c in wo_into2:
        c.wait_recv()
    for i in range(4):
        part = dot(att[i], wo_full[i])
        hid[...] = (tok[...].astype(f32) if i == 0 else hid[...]) + part
    two, _ = norm_parts(hid[...])
    snd_b[...] = dot(disp[...], (two * gain2).astype(bf16)).astype(bf16)
    spread(snd_b, x_own, xd_s, xd_r)

    arrive(c_out, 0, 1, 2, 3)
    c_pair.start()
    dn_load.wait()

    def back_down(c, carry):
        part = pl.ds(pl.multiple_of(c * FF_CHUNK, FF_CHUNK), FF_CHUNK)
        ag[:, part] = dot(g_own[...], dn[part, :], NT).astype(bf16)
        return carry

    lax.fori_loop(0, FF // FF_CHUNK, back_down, 0)
    up_load.wait()
    spread_sent(snd_a, g_own, gd_s, gd_r)
    spread_recv(snd_b, x_own, xd_s, xd_r)

    xc[...] = dot(pack[...], x_own[...], TN).astype(bf16)
    start(x_low, 0, 1, 2)
    arrive(g_low, 3, 4)
    start(g_low, 7)
    eacc[...] = jnp.zeros_like(eacc)

    def expert(c, carry):
        part = pl.ds(pl.multiple_of(c * FF_CHUNK, FF_CHUNK), FF_CHUNK)
        value, slope = gelu_pair(dot(x_own[...], up[:, part]))
        act[:, part] = value.astype(bf16)
        pre_grad = (ag[:, part].astype(f32) * slope).astype(bf16)
        ag[:, part] = pre_grad
        eacc[...] += dot(pre_grad, up[:, part], NT)
        return carry

    lax.fori_loop(0, FF // FF_CHUNK, expert, 0)
    snd_a[...] = eacc[...].astype(bf16)
    spread(snd_a, eg_rcv, eg_s, eg_r)
    spread_sent(snd_b, x_own, xd_s, xd_r)
    eacc[...] = jnp.zeros_like(eacc)

    def produce(c, carry):
        part = pl.ds(pl.multiple_of(c * FF_CHUNK, FF_CHUNK), FF_CHUNK)
        eacc[...] += dot(act[:, part], dn[part, :])
        return carry

    lax.fori_loop(0, FF // FF_CHUNK, produce, 0)
    snd_b[...] = eacc[...].astype(bf16)
    arrive(x_low, 0, 1)
    start(x_low, 3, 4)
    arrive(x_low, 2)
    start(x_low, 5, 6)
    spread_recv(snd_a, eg_rcv, eg_s, eg_r)

    two, scale2 = norm_parts(hid[...])
    back = dot(disp_t[...], eg_rcv[...])
    sm_x[h, 1:2, :] = jnp.sum(back * two, axis=0, keepdims=True)
    hgrad[...] = og[...].astype(f32) + norm_pull(back, two, scale2, gain2)
    mixed[...] = hgrad[...].astype(bf16)

    def back_output(i, carry):
        agr_snd[i] = dot(mixed[...], wo_full[i], NT).astype(bf16)
        return carry

    lax.fori_loop(0, 4, back_output, 0)
    for c in wo_out + wo_out2:
        c.wait_send()
    agr_out, agr_into = cross(agr_snd, agr, agr_s, agr_r)
    for c in agr_out:
        c.start()
    agr[h] = agr_snd[h]
    spread(snd_b, out_rcv, out_s, out_r)
    start(g_high, 2)

    def output_grad(i, carry):
        wog_snd[i] = dot(att[i], mixed[...], TN).astype(bf16)
        return carry

    lax.fori_loop(0, 4, output_grad, 0)
    wog_twin = [
        remote(wog_snd.at[i, wo_twin], wog_pair.at[i], wog_s.at[3 + i], wog_r.at[3 + i], (h, twin, d))
        for i in range(4)
    ]
    for c in wog_twin:
        c.start()
    dk[...] = jnp.zeros_like(dk)
    dv[...] = jnp.zeros_like(dv)
    for c in agr_into:
        c.wait_recv()
    arrive(g_high, 0, 1)
    start(g_high, 3, 4)
    arrive(x_low, 3, 4)
    start(x_low, 7)

    def attend_back(b, carry):
        keys, allowed = window(b)
        mine = rows(b * TOK, TOK)
        groups = [None, None]
        for head in range(3):
            lanes = pl.ds((head // 2) * 128, 128)
            q = head_mask(head, qkv[mine, head_lanes(head, 0)])
            k = qkv[keys, head_lanes(head, 1)]
            v = qkv[keys, head_lanes(head, 2)]
            u = head_mask(head, agr[b, :, lanes])
            inner = jnp.sum(u.astype(f32) * att_snd[b, :, lanes].astype(f32), axis=-1, keepdims=True)
            s = jnp.where(allowed, dot(q, k, NT), NEGATIVE)
            chances = jnp.exp(s - lse[mine, head : head + 1])
            score_grad = (chances * (dot(u, v, NT) - inner)).astype(bf16)
            part = head_mask(head, dot(score_grad, k)) * 0.125
            g = head // 2
            groups[g] = part if groups[g] is None else groups[g] + part
            dk[keys, lanes] += dot(score_grad, q, TN)
            dv[keys, lanes] += dot(chances.astype(bf16), u, TN)
        jg[mine, 0:128] = groups[0].astype(bf16)
        jg[mine, 128:256] = groups[1].astype(bf16)
        return carry

    for i in range(4):
        wog_twin[i].wait_recv()
        wog_pair[i] = (wog_snd[i, wo_mine, :].astype(f32) + wog_pair[i].astype(f32)).astype(bf16)
    wog_out, wog_into = cross(wog_pair, wog_rcv, wog_s, wog_r)
    start(wog_out, 0, 1, 2)
    arrive(g_high, 2)
    start(g_high, 5, 6)
    lax.fori_loop(0, 4, attend_back, 0)
    jg[:, PAD_COLS : 2 * PAD_COLS] = dk[...].astype(bf16)
    jg[:, 2 * PAD_COLS : 3 * PAD_COLS] = dv[...].astype(bf16)

    def fill_copies(c):
        part = pl.ds(c * FF_CHUNK, FF_CHUNK)
        return (
            pltpu.make_async_copy(du, du_hbm.at[:, part], fill_sem.at[0]),
            pltpu.make_async_copy(eacc, dd_hbm.at[part], fill_sem.at[1]),
        )

    def fill(c):
        part = pl.ds(c * FF_CHUNK, FF_CHUNK)
        if c > 0:
            for copy in fill_copies(c - 1):
                copy.wait()
        du[...] = dot(x_own[...], ag[:, part], TN)
        eacc[...] = dot(act[:, part], g_own[...], TN)

        def tile(i, carry):
            r = rows(i * FILL_TILE, FILL_TILE)
            x, g = x_lo[r, :], g_lo[r, :]
            value, slope = gelu_pair(dot(x, up[:, part]))
            pre_grad = (dot(g, dn[part, :], NT) * slope).astype(bf16)
            du[...] += dot(x, pre_grad, TN)
            eacc[...] += dot(value.astype(bf16), g, TN)
            return carry

        lax.fori_loop(0, BLOCKS * HALF // FILL_TILE, tile, 0)
        for copy in fill_copies(c):
            copy.start()

    for c in wog_twin:
        c.wait_send()
    ng_out, ng_into = cross(wog_snd, wo_full, ng_s, ng_r)
    for i, p in enumerate((across, right, left)):
        wog_snd[p] = dot(jg[rows(p * TOK, TOK), :], wjt[...]).astype(bf16)
        ng_out[(2, 0, 1)[i]].start()

    for c in wog_into:
        c.wait_recv()
    wog = wog_pair[h].astype(f32)
    for p in x_from:
        wog = wog + wog_rcv[p].astype(f32)
    gpart[288:384, :] = wog.astype(bf16)
    gain1_part = jnp.zeros((1, D), f32)
    for part in range(3):
        grad = jnp.zeros((PAD_COLS, D), f32)
        for b in range(4):
            grad = grad + dot(jg[b * TOK : (b + 1) * TOK, part * PAD_COLS : (part + 1) * PAD_COLS], gath[b], TN)
        gain1_part = gain1_part + jnp.sum(
            grad * wjt[part * PAD_COLS : (part + 1) * PAD_COLS, :].astype(f32), axis=0, keepdims=True
        )
        gfull[part * HEAD_COLS : (part + 1) * HEAD_COLS, :] = grad[0:HEAD_COLS, :].astype(bf16)
    sm_x[h, 0:1, :] = gain1_part / gain1

    mine_half = rows(core * 384, 384)
    twin_half = rows((1 - core) * 384, 384)
    mine_part = pl.ds(pl.multiple_of(core * 288, 288), 288)
    twin_part = pl.ds(pl.multiple_of((1 - core) * 288, 288), 288)
    ca_out = remote(gfull.at[twin_part], rs_core, ca_s.at[0], ca_r.at[0], (h, twin, d))
    ca_out.start()
    sx_out, sx_into = gather(sm_x, sx_s, sx_r)
    for c in sx_out:
        c.start()

    own_grad = dot(jg[rows(h * TOK, TOK), :], wjt[...])
    arrive(g_low, 5, 6, 7)
    arrive(x_low, 5, 6, 7)
    fill(0)
    ca_out.wait_recv()
    gpart[0:288, :] = (gfull[mine_part, :].astype(f32) + rs_core[...].astype(f32)).astype(bf16)

    unit = lax.div(e, 2)

    def peer(k):
        return lax.rem(unit + k, 8)

    def a2_copy(k, where):
        p = peer(k)
        return remote(
            gpart.at[rows(p * 48, 48)], rs_rcv.at[where], a2_s.at[k], a2_r.at[k], (h, p * 2 + core, d)
        )

    for k in range(1, 8):
        a2_copy(k, unit).start()
    rs_rcv[unit] = gpart[rows(unit * 48, 48), :]
    for c in sx_into:
        c.wait_recv()
    sm_e[e] = (sm_x[0] + sm_x[1]) + (sm_x[2] + sm_x[3])

    def small_copy(k, p, where):
        return remote(sm_e.at[e], sm_e.at[where], se_s.at[k], se_r.at[k], (h, p, d))

    def small_start(k, carry):
        p = lax.rem(e + k, EXPERTS)
        small_copy(k, p, e).start()
        return carry

    lax.fori_loop(1, EXPERTS, small_start, 0)
    arrive(g_high, 3, 4)
    start(g_high, 7)
    fill(1)

    for c in ng_into:
        c.wait_recv()
    for p in x_from:
        own_grad = own_grad + wo_full[p].astype(f32)
    one, scale1 = norm_parts(tok[...].astype(f32))
    tgrad[...] = hgrad[...] + norm_pull(own_grad, one, scale1, gain1)
    start(x_high, 0, 1, 2)
    fill(2)

    for k in range(1, 8):
        a2_copy(k, peer(8 - k)).wait_recv()
    reduced = rs_rcv[0].astype(f32)
    for k in range(1, 8):
        reduced = reduced + rs_rcv[k].astype(f32)
    rs_pair[d] = reduced.astype(bf16)
    a3 = remote(rs_pair.at[d], rs_pair.at[d], a3_s.at[0], a3_r.at[0], (h, e, other))
    a3_in = remote(rs_pair.at[other], rs_pair.at[other], a3_s.at[0], a3_r.at[0], (h, e, other))
    a3.start()

    def small_recv(k, carry):
        p = lax.rem(e + EXPERTS - k, EXPERTS)
        small_copy(k, p, p).wait_recv()
        return carry

    lax.fori_loop(1, EXPERTS, small_recv, 0)
    gathered = sm_e[0]
    for k in range(1, EXPERTS):
        gathered = gathered + sm_e[k]
    sm_d[d] = gathered
    sd = remote(sm_d.at[d], sm_d.at[d], sd_s.at[0], sd_r.at[0], (h, e, other))
    sd_in = remote(sm_d.at[other], sm_d.at[other], sd_s.at[0], sd_r.at[0], (h, e, other))
    sd.start()
    fill(3)
    arrive(x_high, 0, 1)
    start(x_high, 3, 4)
    arrive(x_high, 2)
    start(x_high, 5, 6)

    spread_recv(snd_b, out_rcv, out_s, out_r)
    final[...] = hid[...] + dot(disp_t[...], out_rcv[...])

    a3_in.wait_recv()
    here = rows(core * 384 + unit * 48, 48)
    gsum[here, :] = (rs_pair[0].astype(f32) + rs_pair[1].astype(f32)).astype(bf16)

    def a4_copy(k, p, place):
        return remote(gsum.at[place], gsum.at[place], a4_s.at[k], a4_r.at[k], (h, p * 2 + core, d))

    for k in range(1, 8):
        a4_copy(k, peer(k), here).start()
    fill(4)
    arrive(x_high, 3, 4)
    start(x_high, 7)

    sd_in.wait_recv()
    small[...] = sm_d[0] + sm_d[1]
    for k in range(1, 8):
        p = peer(8 - k)
        a4_copy(k, p, rows(core * 384 + p * 48, 48)).wait_recv()
    for k in range(1, 8):
        a4_copy(k, peer(k), here).wait_send()
    a5 = remote(gsum.at[mine_half], gsum.at[mine_half], ca_s.at[1], ca_r.at[1], (h, twin, d))
    a5_in = remote(gsum.at[twin_half], gsum.at[twin_half], ca_s.at[1], ca_r.at[1], (h, twin, d))
    a5.start()
    fill(5)
    a5_in.wait_recv()
    arrive(g_high, 5, 6, 7)
    arrive(x_high, 5, 6, 7)
    c_pair.wait_recv()
    for copy in fill_copies(5):
        copy.wait()

    spread_sent(snd_a, eg_rcv, eg_s, eg_r)
    spread_sent(snd_b, out_rcv, out_s, out_r)

    def small_sent(k, carry):
        p = lax.rem(e + k, EXPERTS)
        small_copy(k, p, e).wait_send()
        return carry

    lax.fori_loop(1, EXPERTS, small_sent, 0)
    for k in range(1, 8):
        a2_copy(k, unit).wait_send()
    for c in (
        nrm_out + att_out + g_low + g_high + x_low + x_high + c_out + [c_pair] + agr_out + wog_out + ng_out
        + sx_out + [ca_out, a5, a3, sd]
    ):
        c.wait_send()


def block_call(*args):
    vmem = pl.BlockSpec(memory_space=pltpu.VMEM)
    hbm = pl.BlockSpec(memory_space=pl.ANY)
    smem = pl.BlockSpec(memory_space=pltpu.SMEM)
    dma = pltpu.SemaphoreType.DMA

    def buf(*shape, dtype=bf16):
        return pltpu.VMEM(shape, dtype)

    scratch = [
        buf(8, 128, dtype=f32), buf(D, D), buf(4, TOK, D), buf(ROW, D), buf(4, TOK, PAD_COLS), buf(4, TOK, PAD_COLS),
        buf(4, PAD_COLS, D), buf(D, FF), buf(FF, D), buf(SLOTS, D), buf(SLOTS, D), buf(SLOTS, D),
        buf(SLOTS, D), buf(SLOTS, D), buf(SLOTS, D),
        buf(SLOTS, SLOTS), buf(SLOTS, FF), buf(SLOTS, FF), buf(SLOTS, D, dtype=f32),
        buf(SLOTS, D), buf(SLOTS, D), buf(SLOTS, TOK), buf(TOK, SLOTS),
        buf(TOK, D, dtype=f32), buf(TOK, D, dtype=f32), buf(TOK, D), buf(4, TOK, PAD_COLS), buf(4, TOK, PAD_COLS),
        buf(ROW, 128, dtype=f32), buf(BLOCKS * HALF, D), buf(BLOCKS * HALF, D), buf(D, FF_CHUNK, dtype=f32),
        buf(ROW, PAD_COLS, dtype=f32), buf(ROW, PAD_COLS, dtype=f32),
        buf(ROW, D), buf(4, PAD_COLS, D), buf(4, 96, D), buf(4, 96, D),
        buf(3 * HEAD_COLS, D), buf(384, D), buf(288, D), buf(8, 48, D), buf(2, 48, D),
        buf(4, 8, D, dtype=f32), buf(EXPERTS, 8, D, dtype=f32), buf(2, 8, D, dtype=f32),
        dma((2,)), dma((2,)),
    ]
    for n in (4, 6, 16, 16, 16, 16, 3, 3, 3, 7, 8, 8, 8, 8, 5, 2, 8, 1, 8, 3, 16, 1):
        scratch += [dma((n,)), dma((n,))]
    return pl.pallas_call(
        block_kernel,
        out_shape=[
            jax.ShapeDtypeStruct((TOK, D), f32),
            jax.ShapeDtypeStruct((TOK, D), f32),
            jax.ShapeDtypeStruct((D, D), bf16),
            jax.ShapeDtypeStruct((8, D), f32),
            jax.ShapeDtypeStruct((BLOCKS * HALF, D), bf16),
            jax.ShapeDtypeStruct((BLOCKS * HALF, D), bf16),
            jax.ShapeDtypeStruct((BLOCKS, 8, 128), f32),
            jax.ShapeDtypeStruct((D, FF), f32),
            jax.ShapeDtypeStruct((FF, D), f32),
        ],
        in_specs=[vmem] * 8 + [hbm, hbm, vmem, vmem, smem, vmem],
        out_specs=[vmem] * 4 + [hbm, hbm, vmem, hbm, hbm],
        scratch_shapes=scratch,
        compiler_params=pltpu.CompilerParams(
            collective_id=1, has_side_effects=True, vmem_limit_bytes=64 * 2**20 - 2**16
        ),
    )(*args)


GRAD_TILE = 512
REST_TILE = 256


def finish_kernel(
    cnt, x_ref, g_ref, up_ref, dn_ref, du0, dd0, gsum, small, final_in, tgrad_in,
    du_ref, dd_ref, final, tgrad, wq, wk, wv, wo, gain1, gain2, loads,
    xs, gs, total_ref,
):
    step = pl.program_id(0)
    final[...] = final_in[...]
    tgrad[...] = tgrad_in[...]

    @pl.when(step == 0)
    def _():
        total = 0
        for b in range(BLOCKS):
            there = pl.ds(pl.multiple_of(total, 16), HALF)
            xs[there, :] = x_ref[b * HALF : (b + 1) * HALF, :]
            gs[there, :] = g_ref[b * HALF : (b + 1) * HALF, :]
            more = jnp.maximum(jnp.max(cnt[b]).astype(i32) - HALF, 0)
            total = total + lax.div(more + 15, 16) * 16
        tail = pl.ds(pl.multiple_of(total, 16), GRAD_TILE)
        xs[tail, :] = jnp.zeros((GRAD_TILE, D), bf16)
        gs[tail, :] = jnp.zeros((GRAD_TILE, D), bf16)
        total_ref[0] = total
        for i, w in enumerate((wq, wk, wv)):
            first = i * HEAD_COLS
            for piece in range(12):
                r = first + piece * 16
                at = r if r < 288 else r + 96
                w[piece * 16 : piece * 16 + 16, :] = gsum[at : at + 16, :].astype(f32)
        wo[0:96, :] = gsum[288:384, :].astype(f32)
        wo[96:192, :] = gsum[672:768, :].astype(f32)
        gain1[...] = small[0:1, :].reshape(D)
        gain2[...] = small[1:2, :].reshape(D)
        loads[...] = small[2:3, 0:128].astype(i32).reshape(128)

    total = total_ref[0]
    du_ref[...] = du0[...]
    dd_ref[...] = dd0[...]

    def tile(start, size):
        r = pl.ds(pl.multiple_of(start, size), size)
        x, g = xs[r, :], gs[r, :]
        value, slope = gelu_pair(dot(x, up_ref[...]))
        pre_grad = (dot(g, dn_ref[...], NT) * slope).astype(bf16)
        du_ref[...] += dot(x, pre_grad, TN)
        dd_ref[...] += dot(value.astype(bf16), g, TN)

    def whole(i, carry):
        tile(i * GRAD_TILE, GRAD_TILE)
        return carry

    def rest(i, carry):
        tile(i * REST_TILE, REST_TILE)
        return carry

    full = lax.div(total, GRAD_TILE)
    lax.fori_loop(0, full, whole, 0)
    lax.fori_loop(full * (GRAD_TILE // REST_TILE), lax.div(total + REST_TILE - 1, REST_TILE), rest, 0)


def finish_call(cnt, x_hi, g_hi, up, dn, du0, dd0, gsum, small, final, tgrad):
    def whole(*shape):
        return pl.BlockSpec(shape, lambda i: (0,) * len(shape))

    share = pl.BlockSpec((TOK, D // 6), lambda i: (0, i))
    columns = pl.BlockSpec((D, FF_CHUNK), lambda i: (0, i))
    lines = pl.BlockSpec((FF_CHUNK, D), lambda i: (i, 0))
    return pl.pallas_call(
        finish_kernel,
        grid=(FF // FF_CHUNK,),
        in_specs=[
            whole(BLOCKS, 8, 128), whole(BLOCKS * HALF, D), whole(BLOCKS * HALF, D),
            columns, lines, columns, lines, whole(D, D), whole(8, D), share, share,
        ],
        out_specs=[columns, lines, share, share] + [whole(HEAD_COLS, D)] * 4 + [whole(D), whole(D), whole(128)],
        out_shape=[
            jax.ShapeDtypeStruct((D, FF), f32),
            jax.ShapeDtypeStruct((FF, D), f32),
            jax.ShapeDtypeStruct((TOK, D), f32),
            jax.ShapeDtypeStruct((TOK, D), f32),
        ]
        + [jax.ShapeDtypeStruct((HEAD_COLS, D), f32)] * 4
        + [
            jax.ShapeDtypeStruct((D,), f32),
            jax.ShapeDtypeStruct((D,), f32),
            jax.ShapeDtypeStruct((128,), i32),
        ],
        scratch_shapes=[
            pltpu.VMEM((BLOCKS * HALF + GRAD_TILE, D), bf16),
            pltpu.VMEM((BLOCKS * HALF + GRAD_TILE, D), bf16),
            pltpu.SMEM((1,), i32),
        ],
        compiler_params=pltpu.CompilerParams(vmem_limit_bytes=64 * 2**20 - 2**16),
    )(cnt, x_hi, g_hi, up, dn, du0, dd0, gsum, small, final, tgrad)


def body(
    tokens, out_grad, w_query, w_key, w_value, w_output, gain_one, gain_two, expert_up, expert_down,
    hash_table, token_ids, doc_lengths, turn_mask,
):
    final, tokens_grad, gsum, small, x_hi, g_hi, cnt, du0, dd0 = block_call(
        tokens[0], out_grad[0], w_query.T, w_key.T, w_value.T, w_output, gain_one, gain_two,
        expert_up[0], expert_down[0], hash_table.reshape(256, 128), token_ids, doc_lengths, turn_mask,
    )
    up_grad, down_grad, final, tokens_grad, wq, wk, wv, wo, gain1, gain2, loads = finish_call(
        cnt, x_hi, g_hi, expert_up[0], expert_down[0], du0, dd0, gsum, small, final, tokens_grad
    )
    return (
        final[None], tokens_grad[None], wq.T, wk.T, wv.T, wo, gain1, gain2, up_grad[None], down_grad[None],
        loads[:EXPERTS],
    )


def solution(mesh):
    rows_spec = P(("expert", "dp"), "head", None)
    in_specs = (
        rows_spec, rows_spec, P(None, "head"), P(None, "head"), P(None, "head"), P("head", None),
        P(), P(), P("expert", None, None), P("expert", None, None), P(),
        P(("expert", "dp"), "head"), P(("expert", "dp"), None), P(("expert", "dp"), None),
    )
    out_specs = (
        rows_spec, rows_spec, P(None, "head"), P(None, "head"), P(None, "head"), P("head", None),
        P(), P(), P("expert", None, None), P("expert", None, None), P(),
    )
    return jax.shard_map(body, mesh=mesh, in_specs=in_specs, out_specs=out_specs, check_vma=False)
```

```python
import functools

import jax
import jax.numpy as jnp
from jax import lax
from jax.experimental import pallas as pl
from jax.experimental.pallas import tpu as pltpu
from jax.sharding import PartitionSpec as P

MESH = pl.DeviceIdType.MESH
f32 = jnp.float32
bf16 = jnp.bfloat16
i32 = jnp.int32

HEADS_X = 4
EXPERTS = 16
TOK = 256
ROW = 1024
D = 768
FF = 3072
CAP = 32
SLOTS = EXPERTS * CAP
WIN = 768
HEAD_COLS = 192
PAD_COLS = 256
FF_CHUNK = 512
HALF = SLOTS // 2
BLOCKS = 7
FILL_TILE = 448
EPSILON = 1e-05
NEGATIVE = -1e30
GELU_A = 0.7978845608028654
GELU_B = 0.044715

NN = (((1,), (0,)), ((), ()))
NT = (((1,), (1,)), ((), ()))
TN = (((0,), (0,)), ((), ()))


def dot(a, b, dims=NN):
    return lax.dot_general(a, b, dims, preferred_element_type=f32)


def iota(shape, dim):
    return lax.broadcasted_iota(i32, shape, dim)


def norm_parts(x):
    average = jnp.mean(x, axis=-1, keepdims=True)
    centred = x - average
    variance = jnp.mean(centred * centred, axis=-1, keepdims=True)
    scale = lax.rsqrt(variance + EPSILON)
    return centred * scale, scale


def norm_pull(upstream, normed, scale, gain):
    m = upstream * gain
    first = jnp.mean(m, axis=-1, keepdims=True)
    second = jnp.mean(m * normed, axis=-1, keepdims=True)
    return scale * (m - first - normed * second)


def gelu_pair(u):
    u2 = u * u
    half = 0.5 + 0.5 * jnp.tanh(u * (GELU_A + (GELU_A * GELU_B) * u2))
    slope = half + (u + u) * (half * (1.0 - half)) * (GELU_A + (3.0 * GELU_A * GELU_B) * u2)
    return u * half, slope


def rows(start, size):
    return pl.ds(pl.multiple_of(start, size), size)


def block_kernel(
    tok, og, wqt, wkt, wvt, wo, gain1_in, gain2_in, up_hbm, dn_hbm, table, ids, lengths, prompt,
    final, tgrad, gsum, small, x_hi, g_hi, cnt, du_hbm, dd_hbm,
    count, wjt, gath, qkv, att_snd, att, wo_full, up, dn, snd_a, snd_b, g_own, x_own, gc, xc,
    pack, ag, act, eacc, eg_rcv, out_rcv, disp, disp_t, hid, hgrad, mixed, agr_snd, agr,
    lse, x_lo, g_lo, du, du_out, dd_out, dk, dv, jg, wog_snd, wog_pair, wog_rcv, wog_sum, wog_x, gfull, gpart, rs_core, rs_rcv, rs_pair,
    sm_x, sm_e, sm_d,
    load_sem, fill_sem, nrm_s, nrm_r, wo_s, wo_r, gd_s, gd_r, xd_s, xd_r, eg_s, eg_r, out_s, out_r,
    att_s, att_r, agr_s, agr_r, ng_s, ng_r, wog_s, wog_r, wox_s, wox_r, gl_s, gl_r, gh_s, gh_r, xl_s, xl_r, xh_s, xh_r, ct_s, ct_r,
    ca_s, ca_r, a2_s, a2_r, a3_s, a3_r, a4_s, a4_r, sx_s, sx_r, se_s, se_r, sd_s, sd_r,
):
    h = lax.axis_index("head")
    e = lax.axis_index("expert")
    d = lax.axis_index("dp")
    right, left, across = lax.rem(h + 1, 4), lax.rem(h + 3, 4), lax.rem(h + 2, 4)
    x_peers = (right, left, across)
    x_from = (left, right, across)
    other = 1 - d
    twin = e + 1 - 2 * lax.rem(e, 2)

    def remote(src, dst, ss, rs, device):
        return pltpu.make_async_remote_copy(
            src_ref=src, dst_ref=dst, send_sem=ss, recv_sem=rs, device_id=device, device_id_type=MESH
        )

    def spread_copy(snd, rcv, ss, rs, k, back):
        p = lax.rem(e + (EXPERTS - k if back else k), EXPERTS)
        return remote(
            snd.at[rows(k * CAP, CAP)], rcv.at[rows(k * CAP, CAP)], ss.at[k], rs.at[k], (h, p, d)
        )

    def spread(snd, rcv, ss, rs, back=False, first=1, last=EXPERTS):
        def step(k, carry):
            spread_copy(snd, rcv, ss, rs, k, back).start()
            return carry

        lax.fori_loop(first, last, step, 0)
        if first == 1:
            rcv[0:CAP, :] = snd[0:CAP, :]

    def spread_recv(snd, rcv, ss, rs, back=False, first=1, last=EXPERTS):
        def step(k, carry):
            spread_copy(snd, rcv, ss, rs, k, back).wait_recv()
            return carry

        lax.fori_loop(first, last, step, 0)

    def spread_sent(snd, rcv, ss, rs, back=False):
        def step(k, carry):
            spread_copy(snd, rcv, ss, rs, k, back).wait_send()
            return carry

        lax.fori_loop(1, EXPERTS, step, 0)

    def cross(snd, rcv, ss, rs, only=None):
        view = (lambda r, i: r.at[i]) if only is None else (lambda r, i: r.at[i, pl.ds(0, only)])
        out = [
            remote(view(snd, p), view(rcv, h), ss.at[i], rs.at[i], (p, e, d))
            for i, p in enumerate(x_peers)
        ]
        into = [
            remote(view(snd, p), view(rcv, p), ss.at[i], rs.at[i], (p, e, d))
            for i, p in enumerate(x_from)
        ]
        return out, into

    def gather(buf, ss, rs, only=None):
        view = (lambda r, i: r.at[i]) if only is None else (lambda r, i: r.at[i, pl.ds(0, only)])
        out = [
            remote(view(buf, h), view(buf, h), ss.at[i], rs.at[i], (p, e, d))
            for i, p in enumerate(x_peers)
        ]
        into = [
            remote(view(buf, p), view(buf, p), ss.at[i], rs.at[i], (p, e, d))
            for i, p in enumerate(x_from)
        ]
        return out, into

    def relay_gather(buf, ss, rs):
        low, high = pl.ds(0, TOK // 2), pl.ds(TOK // 2, TOK // 2)

        def pair(i, there, view):
            return remote(view, view, ss.at[i], rs.at[i], (there, e, d))

        out = [
            pair(0, right, buf.at[h]),
            pair(1, left, buf.at[h]),
            pair(2, right, buf.at[left, low]),
            pair(3, left, buf.at[right, high]),
        ]
        into = [
            pair(0, left, buf.at[left]),
            pair(1, right, buf.at[right]),
            pair(2, left, buf.at[across, low]),
            pair(3, right, buf.at[across, high]),
        ]
        return out, into

    def token_copies(own, dst, ss, rs):
        def at(i, part=None):
            return dst.at[rows(i * HALF, HALF)] if part is None else dst.at[pl.ds(i * HALF + part, HALF // 2)]

        moves = [
            (own, at(2), right, d),
            (own, at(0), left, d),
            (own, at(3), h, other),
            (at(2, 0), at(1, 0), right, d),
            (at(0, HALF // 2), at(1, HALF // 2), left, d),
            (at(3), at(6), right, d),
            (at(3), at(4), left, d),
            (at(1), at(5), h, other),
        ]
        return [
            remote(src, to, ss.at[i], rs.at[i], (hh, e, dd)) for i, (src, to, hh, dd) in enumerate(moves)
        ]

    g_low = token_copies(gc.at[pl.ds(0, HALF)], g_lo, gl_s, gl_r)
    g_high = token_copies(gc.at[pl.ds(HALF, HALF)], g_hi, gh_s, gh_r)
    x_low = token_copies(xc.at[pl.ds(0, HALF)], x_lo, xl_s, xl_r)
    x_high = token_copies(xc.at[pl.ds(HALF, HALF)], x_hi, xh_s, xh_r)

    def start(copies, *which):
        for i in which:
            copies[i].start()

    def arrive(copies, *which):
        for i in which:
            copies[i].wait_recv()

    up_load = pltpu.make_async_copy(up_hbm, up, load_sem.at[0])
    dn_load = pltpu.make_async_copy(dn_hbm, dn, load_sem.at[1])
    up_load.start()
    dn_load.start()

    barrier = pltpu.get_barrier_semaphore()
    for p in x_peers:
        pl.semaphore_signal(barrier, inc=1, device_id=(p, e, d), device_id_type=MESH)
    pl.semaphore_signal(barrier, inc=1, device_id=(h, e, other), device_id_type=MESH)

    def greet(k, carry):
        pl.semaphore_signal(
            barrier, inc=1, device_id=(h, lax.rem(e + k, EXPERTS), d), device_id_type=MESH
        )
        return carry

    lax.fori_loop(1, EXPERTS, greet, 0)

    gain1 = gain1_in[...].reshape(1, D)
    gain2 = gain2_in[...].reshape(1, D)
    one, _ = norm_parts(tok[...].astype(f32))
    gath[h] = (one * gain1).astype(bf16)
    for i, w in enumerate((wqt, wkt, wvt)):
        wjt[i * PAD_COLS : i * PAD_COLS + HEAD_COLS, :] = w[...]
        wjt[i * PAD_COLS + HEAD_COLS : (i + 1) * PAD_COLS, :] = jnp.zeros(
            (PAD_COLS - HEAD_COLS, D), bf16
        )
    for i in range(4):
        wo_full[i, HEAD_COLS:PAD_COLS, :] = jnp.zeros((PAD_COLS - HEAD_COLS, D), bf16)
    wo_full[h, 0:HEAD_COLS, :] = wo[...]

    pl.semaphore_wait(barrier, 3 + 1 + EXPERTS - 1)
    nrm_out, nrm_into = relay_gather(gath, nrm_s, nrm_r)
    nrm_out[0].start()
    nrm_out[1].start()

    eye = iota((TOK, TOK), 0) == iota((TOK, TOK), 1)
    id_col = jnp.sum(jnp.where(eye, ids[...].astype(f32), 0.0), axis=1, keepdims=True).astype(i32)
    high, low = lax.shift_right_logical(id_col, 7), lax.bitwise_and(id_col, 127)
    pick = jnp.where(iota((TOK, 256), 1) == high, 1.0, 0.0).astype(bf16)
    near = dot(pick, table[...].astype(f32).astype(bf16))
    lane = iota((TOK, 128), 1)
    chosen = jnp.sum(jnp.where(lane == low, near, 0.0), axis=1, keepdims=True)
    member = jnp.where(lane == chosen.astype(i32), 1.0, 0.0)
    before = jnp.where(iota((TOK, TOK), 1) < iota((TOK, TOK), 0), 1.0, 0.0).astype(bf16)
    rank = jnp.sum(dot(before, member.astype(bf16)) * member, axis=1, keepdims=True)
    ahead = chosen - e.astype(f32)
    slot = jnp.where(ahead < 0.0, ahead + EXPERTS, ahead) * CAP + rank
    slot_row = jnp.sum(jnp.where(eye, slot, 0.0), axis=0, keepdims=True).astype(i32)
    disp_t[...] = jnp.where(iota((TOK, SLOTS), 1) == slot.astype(i32), 1.0, 0.0).astype(bf16)
    disp[...] = jnp.where(iota((SLOTS, TOK), 0) == slot_row, 1.0, 0.0).astype(bf16)
    sm_x[h] = jnp.zeros((8, D), f32)
    sm_x[h, 2:3, 0:128] = jnp.sum(member, axis=0, keepdims=True)

    snd_a[...] = dot(disp[...], og[...]).astype(bf16)
    spread(snd_a, g_own, gd_s, gd_r)

    column_scale = jnp.where(iota((1, D), 1) < PAD_COLS, 0.125, 1.0)

    def project(b):
        qkv[rows(b * TOK, TOK), :] = (dot(gath[b], wjt[...], NT) * column_scale).astype(bf16)

    core = lax.rem(e, 2)
    wo_mine = pl.ds(pl.multiple_of(core * 96, 96), 96)
    wo_twin = pl.ds(pl.multiple_of((1 - core) * 96, 96), 96)

    def wo_copy(i, block, part, device):
        view = wo_full.at[block, part]
        return remote(view, view, wo_s.at[i], wo_r.at[i], device)

    wo_out = [wo_copy(i, h, wo_mine, (p, e, d)) for i, p in enumerate(x_peers)]
    wo_into = [wo_copy(i, p, wo_mine, (p, e, d)) for i, p in enumerate(x_from)]
    wo_out2 = [wo_copy(3 + i, p, wo_mine, (h, twin, d)) for i, p in enumerate(x_from)]
    wo_into2 = [wo_copy(3 + i, p, wo_twin, (h, twin, d)) for i, p in enumerate(x_from)]
    project(h)
    nrm_into[0].wait_recv()
    nrm_out[2].start()
    nrm_into[1].wait_recv()
    nrm_out[3].start()
    start(wo_out, 0, 1, 2)
    project(left)
    project(right)
    nrm_into[2].wait_recv()
    nrm_into[3].wait_recv()
    project(across)

    spread_recv(snd_a, g_own, gd_s, gd_r)
    there = jnp.max(jnp.abs(g_own[...].astype(f32)), axis=1, keepdims=True) > 0.0
    there_f = jnp.where(there, 1.0, 0.0)
    earlier = jnp.where(iota((SLOTS, SLOTS), 1) < iota((SLOTS, SLOTS), 0), 1.0, 0.0).astype(bf16)
    place = dot(earlier, jnp.broadcast_to(there_f, (SLOTS, 128)).astype(bf16))[:, 0:1]
    place = jnp.where(there, place, -1.0).astype(i32)
    pack[...] = jnp.where(iota((SLOTS, SLOTS), 1) == place, 1.0, 0.0).astype(bf16)
    gc[...] = dot(pack[...], g_own[...], TN).astype(bf16)
    count[...] = jnp.broadcast_to(jnp.sum(there_f, axis=0, keepdims=True), (8, 128))
    c_out = [
        remote(count, cnt.at[slot_at], ct_s.at[i], ct_r.at[i], device)
        for i, (slot_at, device) in enumerate(
            ((2, (right, e, d)), (0, (left, e, d)), (1, (across, e, d)), (3, (h, e, other)))
        )
    ]
    c_pair = remote(cnt.at[pl.ds(0, 3)], cnt.at[pl.ds(4, 3)], ct_s.at[4], ct_r.at[4], (h, e, other))
    start(c_out, 0, 1, 2, 3)
    start(g_low, 2)

    ends = []
    total = 0
    for j in range(8):
        total = total + lengths[0, j]
        ends.append(total)

    def segment(pos):
        found = jnp.zeros(pos.shape, i32)
        for j in range(8):
            found = found + jnp.where(ends[j] <= pos, 1, 0)
        return found

    def window(b):
        first = jnp.minimum(jnp.maximum(b - 1, 0), 1) * TOK
        q_pos = b * TOK + iota((TOK, 1), 0)
        k_pos = first + iota((1, WIN), 1)
        said = prompt[:, pl.ds(pl.multiple_of(first, TOK), WIN)]
        k_least = jnp.where(said == 1, -1, k_pos)
        allowed = (segment(q_pos) == segment(k_pos)) & (k_least <= q_pos)
        return pl.ds(pl.multiple_of(first, TOK), WIN), allowed

    lane_low = iota((TOK, 128), 1) < 64

    def head_mask(head, x):
        if head == 2:
            return x
        return jnp.where(lane_low if head == 0 else jnp.logical_not(lane_low), x, jnp.zeros_like(x))

    def head_lanes(head, part):
        return pl.ds(part * PAD_COLS + (head // 2) * 128, 128)

    def attend(b):
        keys, allowed = window(b)
        mine = rows(b * TOK, TOK)
        groups = [None, None]
        for head in range(3):
            q = head_mask(head, qkv[mine, head_lanes(head, 0)])
            s = dot(q, qkv[keys, head_lanes(head, 1)], NT)
            s = jnp.where(allowed, s, NEGATIVE)
            top = jnp.max(s, axis=-1, keepdims=True)
            p = jnp.exp(s - top)
            total = jnp.sum(p, axis=-1, keepdims=True)
            lse[mine, head : head + 1] = top + jnp.log(total)
            o = dot(p.astype(bf16), qkv[keys, head_lanes(head, 2)]) * (1.0 / total)
            o = head_mask(head, o)
            g = head // 2
            groups[g] = o if groups[g] is None else groups[g] + o
        att_snd[b, :, 0:128] = groups[0].astype(bf16)
        att_snd[b, :, 128:256] = groups[1].astype(bf16)

    def att_copy(i):
        p = lax.rem(h + 1 + i, 4)
        return remote(att_snd.at[p], att.at[h], att_s.at[i], att_r.at[i], (p, e, d))

    def attend_away(i, carry):
        attend(lax.rem(h + 1 + i, 4))
        att_copy(i).start()
        return carry

    lax.fori_loop(0, 3, attend_away, 0)
    attend(h)
    start(g_low, 0, 1)
    att_out = [att_copy(i) for i in range(3)]
    att[h] = att_snd[h]

    for i in range(3):
        wo_into[i].wait_recv()
        wo_out2[i].start()
    arrive(att_out, 0, 1, 2)
    for c in wo_into2:
        c.wait_recv()
    for i in range(4):
        part = dot(att[i], wo_full[i])
        hid[...] = (tok[...].astype(f32) if i == 0 else hid[...]) + part
    two, _ = norm_parts(hid[...])
    snd_b[...] = dot(disp[...], (two * gain2).astype(bf16)).astype(bf16)
    spread(snd_b, x_own, xd_s, xd_r)

    arrive(c_out, 0, 1, 2, 3)
    c_pair.start()
    arrive(g_low, 2)
    start(g_low, 5, 6)
    dn_load.wait()

    def back_down(c, carry):
        part = pl.ds(pl.multiple_of(c * FF_CHUNK, FF_CHUNK), FF_CHUNK)
        ag[:, part] = dot(g_own[...], dn[part, :], NT).astype(bf16)
        return carry

    lax.fori_loop(0, FF // FF_CHUNK, back_down, 0)
    up_load.wait()
    spread_sent(snd_a, g_own, gd_s, gd_r)
    arrive(g_low, 0, 1)
    start(g_low, 3, 4)
    start(g_high, 0, 1)
    spread_recv(snd_b, x_own, xd_s, xd_r, last=8)

    eacc[...] = jnp.zeros_like(eacc)

    def expert(r):
        def step(c, carry):
            part = pl.ds(pl.multiple_of(c * FF_CHUNK, FF_CHUNK), FF_CHUNK)
            value, slope = gelu_pair(dot(x_own[r, :], up[:, part]))
            act[r, part] = value.astype(bf16)
            pre_grad = (ag[r, part].astype(f32) * slope).astype(bf16)
            ag[r, part] = pre_grad
            eacc[r, :] += dot(pre_grad, up[:, part], NT)
            return carry

        lax.fori_loop(0, FF // FF_CHUNK, step, 0)
        snd_a[r, :] = eacc[r, :].astype(bf16)

    expert(pl.ds(0, HALF))
    spread(snd_a, eg_rcv, eg_s, eg_r, True, last=8)
    spread_recv(snd_b, x_own, xd_s, xd_r, first=8)
    xc[...] = dot(pack[...], x_own[...], TN).astype(bf16)
    start(x_low, 0, 1)
    expert(pl.ds(HALF, HALF))
    spread(snd_a, eg_rcv, eg_s, eg_r, True, first=8)
    start(x_low, 2)
    arrive(g_low, 3, 4)
    start(g_low, 7)
    spread_sent(snd_b, x_own, xd_s, xd_r)
    eacc[...] = jnp.zeros_like(eacc)

    def produce(c, carry):
        part = pl.ds(pl.multiple_of(c * FF_CHUNK, FF_CHUNK), FF_CHUNK)
        eacc[...] += dot(act[:, part], dn[part, :])
        return carry

    lax.fori_loop(0, FF // FF_CHUNK, produce, 0)
    snd_b[...] = eacc[...].astype(bf16)
    arrive(x_low, 0, 1)
    start(x_low, 3, 4)
    spread_recv(snd_a, eg_rcv, eg_s, eg_r, True)

    two, scale2 = norm_parts(hid[...])
    back = dot(disp_t[...], eg_rcv[...])
    sm_x[h, 1:2, :] = jnp.sum(back * two, axis=0, keepdims=True)
    hgrad[...] = og[...].astype(f32) + norm_pull(back, two, scale2, gain2)
    mixed[...] = hgrad[...].astype(bf16)

    def back_output(i, carry):
        agr_snd[i] = dot(mixed[...], wo_full[i], NT).astype(bf16)
        return carry

    lax.fori_loop(0, 4, back_output, 0)
    for c in wo_out + wo_out2:
        c.wait_send()
    agr_out, agr_into = cross(agr_snd, agr, agr_s, agr_r)
    for c in agr_out:
        c.start()
    agr[h] = agr_snd[h]
    arrive(x_low, 3, 4)
    start(x_low, 7)
    start(g_high, 2)

    def output_grad(i, carry):
        wog_snd[i] = dot(att[i], mixed[...], TN).astype(bf16)
        return carry

    lax.fori_loop(0, 4, output_grad, 0)
    wog_twin = [
        remote(wog_snd.at[i, wo_twin], wog_pair.at[i], wog_s.at[3 + i], wog_r.at[3 + i], (h, twin, d))
        for i in range(4)
    ]
    for c in wog_twin:
        c.start()
    dk[...] = jnp.zeros_like(dk)
    dv[...] = jnp.zeros_like(dv)
    for c in agr_into:
        c.wait_recv()

    def attend_back(b, carry):
        keys, allowed = window(b)
        mine = rows(b * TOK, TOK)
        groups = [None, None]
        for head in range(3):
            lanes = pl.ds((head // 2) * 128, 128)
            q = head_mask(head, qkv[mine, head_lanes(head, 0)])
            k = qkv[keys, head_lanes(head, 1)]
            v = qkv[keys, head_lanes(head, 2)]
            u = head_mask(head, agr[b, :, lanes])
            inner = jnp.sum(u.astype(f32) * att_snd[b, :, lanes].astype(f32), axis=-1, keepdims=True)
            s = jnp.where(allowed, dot(q, k, NT), NEGATIVE)
            chances = jnp.exp(s - lse[mine, head : head + 1])
            score_grad = (chances * (dot(u, v, NT) - inner)).astype(bf16)
            part = head_mask(head, dot(score_grad, k)) * 0.125
            g = head // 2
            groups[g] = part if groups[g] is None else groups[g] + part
            dk[keys, lanes] += dot(score_grad, q, TN)
            dv[keys, lanes] += dot(chances.astype(bf16), u, TN)
        jg[mine, 0:128] = groups[0].astype(bf16)
        jg[mine, 128:256] = groups[1].astype(bf16)
        return carry

    for i in range(4):
        wog_twin[i].wait_recv()
        wog_pair[i] = (wog_snd[i, wo_mine, :].astype(f32) + wog_pair[i].astype(f32)).astype(bf16)
    y = lax.div(e, 4)
    over_y = [
        remote(
            wog_pair.at[lax.rem(y + i, 4)], wog_rcv.at[i], wog_s.at[i - 1], wog_r.at[i - 1],
            (h, lax.rem(e + 4 * i, EXPERTS), d),
        )
        for i in range(1, 4)
    ]
    for c in over_y:
        c.start()
    lax.fori_loop(0, 2, attend_back, 0)
    arrive(over_y, 0, 1, 2)
    wog_sum[...] = (
        wog_pair[y].astype(f32) + wog_rcv[1].astype(f32) + wog_rcv[2].astype(f32) + wog_rcv[3].astype(f32)
    ).astype(bf16)
    over_x = [
        remote(wog_sum, wog_x.at[i], wox_s.at[i], wox_r.at[i], (lax.rem(h + i, 4), e, d)) for i in range(1, 4)
    ]
    for i in range(1, 4):

        @pl.when(lax.rem(h + i, 4) == y)
        def _(i=i):
            over_x[i - 1].start()

    arrive(x_low, 2)
    start(x_low, 5, 6)
    arrive(g_high, 0, 1)
    start(g_high, 3, 4)
    lax.fori_loop(2, 4, attend_back, 0)
    jg[:, PAD_COLS : 2 * PAD_COLS] = dk[...].astype(bf16)
    jg[:, 2 * PAD_COLS : 3 * PAD_COLS] = dv[...].astype(bf16)

    def fill_copies(c):
        part = pl.ds(c * FF_CHUNK, FF_CHUNK)
        return (
            pltpu.make_async_copy(du_out, du_hbm.at[:, part], fill_sem.at[0]),
            pltpu.make_async_copy(dd_out, dd_hbm.at[part], fill_sem.at[1]),
        )

    def fill(c, between=None):
        part = pl.ds(c * FF_CHUNK, FF_CHUNK)
        du[...] = dot(x_own[...], ag[:, part], TN)
        eacc[...] = dot(act[:, part], g_own[...], TN)

        def tile(i, carry):
            r = rows(i * FILL_TILE, FILL_TILE)
            x, g = x_lo[r, :], g_lo[r, :]
            value, slope = gelu_pair(dot(x, up[:, part]))
            pre_grad = (dot(g, dn[part, :], NT) * slope).astype(bf16)
            du[...] += dot(x, pre_grad, TN)
            eacc[...] += dot(value.astype(bf16), g, TN)
            return carry

        if between is None:
            lax.fori_loop(0, BLOCKS * HALF // FILL_TILE, tile, 0)
        else:
            lax.fori_loop(0, 2, tile, 0)
            between()
            lax.fori_loop(2, 4, tile, 0)
        if c > 0:
            for copy in fill_copies(c - 1):
                copy.wait()
        du_out[...] = du[...].astype(bf16)
        dd_out[...] = eacc[...].astype(bf16)
        for copy in fill_copies(c):
            copy.start()

    for c in wog_twin:
        c.wait_send()
    ng_out, ng_into = cross(wog_snd, wo_full, ng_s, ng_r)
    for i, p in enumerate((across, right, left)):
        wog_snd[p] = dot(jg[rows(p * TOK, TOK), :], wjt[...]).astype(bf16)
        ng_out[(2, 0, 1)[i]].start()
    spread(snd_b, out_rcv, out_s, out_r, True)

    gain1_part = jnp.zeros((1, D), f32)
    for part in range(3):
        grad = jnp.zeros((PAD_COLS, D), f32)
        for b in range(4):
            grad = grad + dot(jg[b * TOK : (b + 1) * TOK, part * PAD_COLS : (part + 1) * PAD_COLS], gath[b], TN)
        gain1_part = gain1_part + jnp.sum(
            grad * wjt[part * PAD_COLS : (part + 1) * PAD_COLS, :].astype(f32), axis=0, keepdims=True
        )
        gfull[part * HEAD_COLS : (part + 1) * HEAD_COLS, :] = grad[0:HEAD_COLS, :].astype(bf16)
    sm_x[h, 0:1, :] = gain1_part / gain1

    mine_half = rows(core * 384, 384)
    twin_half = rows((1 - core) * 384, 384)
    mine_part = pl.ds(pl.multiple_of(core * 288, 288), 288)
    twin_part = pl.ds(pl.multiple_of((1 - core) * 288, 288), 288)
    ca_out = remote(gfull.at[twin_part], rs_core, ca_s.at[0], ca_r.at[0], (h, twin, d))
    ca_out.start()
    sx_out, sx_into = gather(sm_x, sx_s, sx_r)
    for c in sx_out:
        c.start()
    start(x_high, 0, 1, 2)
    arrive(g_high, 2)
    start(g_high, 5, 6)

    own_grad = dot(jg[rows(h * TOK, TOK), :], wjt[...])

    def far_blocks():
        arrive(g_low, 5, 6, 7)
        arrive(x_low, 5, 6, 7)

    fill(0, far_blocks)
    ca_out.wait_recv()
    gpart[288:384, :] = jnp.zeros((96, D), bf16)

    @pl.when(y == h)
    def _():
        wog = wog_sum[...].astype(f32)
        for i in range(1, 4):
            over_x[i - 1].wait_recv()
            wog = wog + wog_x[i].astype(f32)
        gpart[288:384, :] = wog.astype(bf16)

    for i in range(1, 4):

        @pl.when(lax.rem(h + i, 4) == y)
        def _(i=i):
            over_x[i - 1].wait_send()

    gpart[0:288, :] = (gfull[mine_part, :].astype(f32) + rs_core[...].astype(f32)).astype(bf16)

    unit = lax.div(e, 2)

    def peer(k):
        return lax.rem(unit + k, 8)

    def a2_copy(k, where):
        p = peer(k)
        return remote(
            gpart.at[rows(p * 48, 48)], rs_rcv.at[where], a2_s.at[k], a2_r.at[k], (h, p * 2 + core, d)
        )

    for k in range(1, 8):
        a2_copy(k, unit).start()
    rs_rcv[unit] = gpart[rows(unit * 48, 48), :]
    def small_copy(k, p, where):
        return remote(sm_e.at[e], sm_e.at[where], se_s.at[k], se_r.at[k], (h, p, d))

    def small_start(k, carry):
        p = lax.rem(e + k, EXPERTS)
        small_copy(k, p, e).start()
        return carry

    fill(1)

    fill(2)
    for c in sx_into:
        c.wait_recv()
    sm_e[e] = (sm_x[0] + sm_x[1]) + (sm_x[2] + sm_x[3])
    lax.fori_loop(1, EXPERTS, small_start, 0)

    for k in range(1, 8):
        a2_copy(k, peer(8 - k)).wait_recv()
    reduced = rs_rcv[0].astype(f32)
    for k in range(1, 8):
        reduced = reduced + rs_rcv[k].astype(f32)
    rs_pair[d] = reduced.astype(bf16)
    a3 = remote(rs_pair.at[d], rs_pair.at[d], a3_s.at[0], a3_r.at[0], (h, e, other))
    a3_in = remote(rs_pair.at[other], rs_pair.at[other], a3_s.at[0], a3_r.at[0], (h, e, other))
    a3.start()

    fill(3)

    for c in ng_into:
        c.wait_recv()
    for p in x_from:
        own_grad = own_grad + wo_full[p].astype(f32)
    one, scale1 = norm_parts(tok[...].astype(f32))
    tgrad[...] = hgrad[...] + norm_pull(own_grad, one, scale1, gain1)
    arrive(x_high, 0, 1)
    start(x_high, 3, 4)
    arrive(x_high, 2)
    start(x_high, 5, 6)
    arrive(g_high, 3, 4)
    start(g_high, 7)

    spread_recv(snd_b, out_rcv, out_s, out_r, True)
    final[...] = hid[...] + dot(disp_t[...], out_rcv[...])

    a3_in.wait_recv()
    here = rows(core * 384 + unit * 48, 48)
    gsum[here, :] = (rs_pair[0].astype(f32) + rs_pair[1].astype(f32)).astype(bf16)

    def a4_copy(k, p, place):
        return remote(gsum.at[place], gsum.at[place], a4_s.at[k], a4_r.at[k], (h, p * 2 + core, d))

    for k in range(1, 8):
        a4_copy(k, peer(k), here).start()

    def small_recv(k, carry):
        p = lax.rem(e + EXPERTS - k, EXPERTS)
        small_copy(k, p, p).wait_recv()
        return carry

    lax.fori_loop(1, EXPERTS, small_recv, 0)
    gathered = sm_e[0]
    for k in range(1, EXPERTS):
        gathered = gathered + sm_e[k]
    sm_d[d] = gathered
    sd = remote(sm_d.at[d], sm_d.at[d], sd_s.at[0], sd_r.at[0], (h, e, other))
    sd_in = remote(sm_d.at[other], sm_d.at[other], sd_s.at[0], sd_r.at[0], (h, e, other))
    sd.start()
    fill(4)
    arrive(x_high, 3, 4)
    start(x_high, 7)

    for k in range(1, 8):
        p = peer(8 - k)
        a4_copy(k, p, rows(core * 384 + p * 48, 48)).wait_recv()
    for k in range(1, 8):
        a4_copy(k, peer(k), here).wait_send()
    a5 = remote(gsum.at[mine_half], gsum.at[mine_half], ca_s.at[1], ca_r.at[1], (h, twin, d))
    a5_in = remote(gsum.at[twin_half], gsum.at[twin_half], ca_s.at[1], ca_r.at[1], (h, twin, d))
    a5.start()
    fill(5)
    sd_in.wait_recv()
    small[...] = sm_d[0] + sm_d[1]
    a5_in.wait_recv()
    arrive(g_high, 5, 6, 7)
    arrive(x_high, 5, 6, 7)
    c_pair.wait_recv()
    for copy in fill_copies(5):
        copy.wait()

    spread_sent(snd_a, eg_rcv, eg_s, eg_r, True)
    spread_sent(snd_b, out_rcv, out_s, out_r, True)

    def small_sent(k, carry):
        p = lax.rem(e + k, EXPERTS)
        small_copy(k, p, e).wait_send()
        return carry

    lax.fori_loop(1, EXPERTS, small_sent, 0)
    for k in range(1, 8):
        a2_copy(k, unit).wait_send()
    for c in (
        nrm_out + att_out + g_low + g_high + x_low + x_high + c_out + [c_pair] + agr_out + over_y + ng_out
        + sx_out + [ca_out, a5, a3, sd]
    ):
        c.wait_send()


def block_call(*args):
    vmem = pl.BlockSpec(memory_space=pltpu.VMEM)
    hbm = pl.BlockSpec(memory_space=pl.ANY)
    smem = pl.BlockSpec(memory_space=pltpu.SMEM)
    dma = pltpu.SemaphoreType.DMA

    def buf(*shape, dtype=bf16):
        return pltpu.VMEM(shape, dtype)

    scratch = [
        buf(8, 128, dtype=f32), buf(D, D), buf(4, TOK, D), buf(ROW, D), buf(4, TOK, PAD_COLS), buf(4, TOK, PAD_COLS),
        buf(4, PAD_COLS, D), buf(D, FF), buf(FF, D), buf(SLOTS, D), buf(SLOTS, D), buf(SLOTS, D),
        buf(SLOTS, D), buf(SLOTS, D), buf(SLOTS, D),
        buf(SLOTS, SLOTS), buf(SLOTS, FF), buf(SLOTS, FF), buf(SLOTS, D, dtype=f32),
        buf(SLOTS, D), buf(SLOTS, D), buf(SLOTS, TOK), buf(TOK, SLOTS),
        buf(TOK, D, dtype=f32), buf(TOK, D, dtype=f32), buf(TOK, D), buf(4, TOK, PAD_COLS), buf(4, TOK, PAD_COLS),
        buf(ROW, 128, dtype=f32), buf(BLOCKS * HALF, D), buf(BLOCKS * HALF, D), buf(D, FF_CHUNK, dtype=f32), buf(D, FF_CHUNK), buf(FF_CHUNK, D),
        buf(ROW, PAD_COLS, dtype=f32), buf(ROW, PAD_COLS, dtype=f32),
        buf(ROW, D), buf(4, PAD_COLS, D), buf(4, 96, D), buf(4, 96, D), buf(96, D), buf(4, 96, D),
        buf(3 * HEAD_COLS, D), buf(384, D), buf(288, D), buf(8, 48, D), buf(2, 48, D),
        buf(4, 8, D, dtype=f32), buf(EXPERTS, 8, D, dtype=f32), buf(2, 8, D, dtype=f32),
        dma((2,)), dma((2,)),
    ]
    for n in (4, 6, 16, 16, 16, 16, 3, 3, 3, 7, 4, 8, 8, 8, 8, 5, 2, 8, 1, 8, 3, 16, 1):
        scratch += [dma((n,)), dma((n,))]
    return pl.pallas_call(
        block_kernel,
        out_shape=[
            jax.ShapeDtypeStruct((TOK, D), f32),
            jax.ShapeDtypeStruct((TOK, D), f32),
            jax.ShapeDtypeStruct((D, D), bf16),
            jax.ShapeDtypeStruct((8, D), f32),
            jax.ShapeDtypeStruct((BLOCKS * HALF, D), bf16),
            jax.ShapeDtypeStruct((BLOCKS * HALF, D), bf16),
            jax.ShapeDtypeStruct((BLOCKS, 8, 128), f32),
            jax.ShapeDtypeStruct((D, FF), bf16),
            jax.ShapeDtypeStruct((FF, D), bf16),
        ],
        in_specs=[vmem] * 8 + [hbm, hbm, vmem, vmem, smem, vmem],
        out_specs=[vmem] * 4 + [hbm, hbm, vmem, hbm, hbm],
        scratch_shapes=scratch,
        compiler_params=pltpu.CompilerParams(
            collective_id=1, has_side_effects=True, vmem_limit_bytes=64 * 2**20 - 2**16
        ),
    )(*args)


GRAD_TILE = 512
REST_TILE = 256


def finish_kernel(
    cnt, x_ref, g_ref, up_ref, dn_ref, du0, dd0, gsum, small, final_in, tgrad_in,
    du_ref, dd_ref, final, tgrad, wq, wk, wv, wo, gain1, gain2, loads,
    xs, gs, total_ref,
):
    step = pl.program_id(0)
    final[...] = final_in[...]
    tgrad[...] = tgrad_in[...]

    @pl.when(step == 0)
    def _():
        total = 0
        for b in range(BLOCKS):
            there = pl.ds(pl.multiple_of(total, 16), HALF)
            xs[there, :] = x_ref[b * HALF : (b + 1) * HALF, :]
            gs[there, :] = g_ref[b * HALF : (b + 1) * HALF, :]
            more = jnp.maximum(jnp.max(cnt[b]).astype(i32) - HALF, 0)
            total = total + lax.div(more + 15, 16) * 16
        tail = pl.ds(pl.multiple_of(total, 16), GRAD_TILE)
        xs[tail, :] = jnp.zeros((GRAD_TILE, D), bf16)
        gs[tail, :] = jnp.zeros((GRAD_TILE, D), bf16)
        total_ref[0] = total
        for i, w in enumerate((wq, wk, wv)):
            first = i * HEAD_COLS
            for piece in range(12):
                r = first + piece * 16
                at = r if r < 288 else r + 96
                w[piece * 16 : piece * 16 + 16, :] = gsum[at : at + 16, :].astype(f32)
        wo[0:96, :] = gsum[288:384, :].astype(f32)
        wo[96:192, :] = gsum[672:768, :].astype(f32)
        gain1[...] = small[0:1, :].reshape(D)
        gain2[...] = small[1:2, :].reshape(D)
        loads[...] = small[2:3, 0:128].astype(i32).reshape(128)

    total = total_ref[0]
    du_ref[...] = du0[...].astype(f32)
    dd_ref[...] = dd0[...].astype(f32)

    def tile(start, size):
        r = pl.ds(pl.multiple_of(start, size), size)
        x, g = xs[r, :], gs[r, :]
        value, slope = gelu_pair(dot(x, up_ref[...]))
        pre_grad = (dot(g, dn_ref[...], NT) * slope).astype(bf16)
        du_ref[...] += dot(x, pre_grad, TN)
        dd_ref[...] += dot(value.astype(bf16), g, TN)

    def whole(i, carry):
        tile(i * GRAD_TILE, GRAD_TILE)
        return carry

    def rest(i, carry):
        tile(i * REST_TILE, REST_TILE)
        return carry

    full = lax.div(total, GRAD_TILE)
    lax.fori_loop(0, full, whole, 0)
    lax.fori_loop(full * (GRAD_TILE // REST_TILE), lax.div(total + REST_TILE - 1, REST_TILE), rest, 0)


def finish_call(cnt, x_hi, g_hi, up, dn, du0, dd0, gsum, small, final, tgrad):
    def whole(*shape):
        return pl.BlockSpec(shape, lambda i: (0,) * len(shape))

    share = pl.BlockSpec((TOK, D // 6), lambda i: (0, i))
    columns = pl.BlockSpec((D, FF_CHUNK), lambda i: (0, i))
    lines = pl.BlockSpec((FF_CHUNK, D), lambda i: (i, 0))
    return pl.pallas_call(
        finish_kernel,
        grid=(FF // FF_CHUNK,),
        in_specs=[
            whole(BLOCKS, 8, 128), whole(BLOCKS * HALF, D), whole(BLOCKS * HALF, D),
            columns, lines, columns, lines, whole(D, D), whole(8, D), share, share,
        ],
        out_specs=[columns, lines, share, share] + [whole(HEAD_COLS, D)] * 4 + [whole(D), whole(D), whole(128)],
        out_shape=[
            jax.ShapeDtypeStruct((D, FF), f32),
            jax.ShapeDtypeStruct((FF, D), f32),
            jax.ShapeDtypeStruct((TOK, D), f32),
            jax.ShapeDtypeStruct((TOK, D), f32),
        ]
        + [jax.ShapeDtypeStruct((HEAD_COLS, D), f32)] * 4
        + [
            jax.ShapeDtypeStruct((D,), f32),
            jax.ShapeDtypeStruct((D,), f32),
            jax.ShapeDtypeStruct((128,), i32),
        ],
        scratch_shapes=[
            pltpu.VMEM((BLOCKS * HALF + GRAD_TILE, D), bf16),
            pltpu.VMEM((BLOCKS * HALF + GRAD_TILE, D), bf16),
            pltpu.SMEM((1,), i32),
        ],
        compiler_params=pltpu.CompilerParams(vmem_limit_bytes=64 * 2**20 - 2**16),
    )(cnt, x_hi, g_hi, up, dn, du0, dd0, gsum, small, final, tgrad)


def body(
    tokens, out_grad, w_query, w_key, w_value, w_output, gain_one, gain_two, expert_up, expert_down,
    hash_table, token_ids, doc_lengths, turn_mask,
):
    final, tokens_grad, gsum, small, x_hi, g_hi, cnt, du0, dd0 = block_call(
        tokens[0], out_grad[0], w_query.T, w_key.T, w_value.T, w_output, gain_one, gain_two,
        expert_up[0], expert_down[0], hash_table.reshape(256, 128), token_ids, doc_lengths, turn_mask,
    )
    up_grad, down_grad, final, tokens_grad, wq, wk, wv, wo, gain1, gain2, loads = finish_call(
        cnt, x_hi, g_hi, expert_up[0], expert_down[0], du0, dd0, gsum, small, final, tokens_grad
    )
    return (
        final[None], tokens_grad[None], wq.T, wk.T, wv.T, wo, gain1, gain2, up_grad[None], down_grad[None],
        loads[:EXPERTS],
    )


def solution(mesh):
    rows_spec = P(("expert", "dp"), "head", None)
    in_specs = (
        rows_spec, rows_spec, P(None, "head"), P(None, "head"), P(None, "head"), P("head", None),
        P(), P(), P("expert", None, None), P("expert", None, None), P(),
        P(("expert", "dp"), "head"), P(("expert", "dp"), None), P(("expert", "dp"), None),
    )
    out_specs = (
        rows_spec, rows_spec, P(None, "head"), P(None, "head"), P(None, "head"), P("head", None),
        P(), P(), P("expert", None, None), P("expert", None, None), P(),
    )
    return jax.shard_map(body, mesh=mesh, in_specs=in_specs, out_specs=out_specs, check_vma=False)
```

```python
import functools

import jax
import jax.numpy as jnp
from jax import lax
from jax.experimental import pallas as pl
from jax.experimental.pallas import tpu as pltpu
from jax.sharding import PartitionSpec as P

MESH = pl.DeviceIdType.MESH
f32 = jnp.float32
bf16 = jnp.bfloat16
i32 = jnp.int32

HEADS_X = 4
EXPERTS = 16
TOK = 256
ROW = 1024
D = 768
FF = 3072
CAP = 32
SLOTS = EXPERTS * CAP
WIN = 768
HEAD_COLS = 192
PAD_COLS = 256
FF_CHUNK = 512
HALF = SLOTS // 2
BLOCKS = 7
FILL_TILE = 896
EPSILON = 1e-05
NEGATIVE = -1e30
GELU_A = 0.7978845608028654
GELU_B = 0.044715

NN = (((1,), (0,)), ((), ()))
NT = (((1,), (1,)), ((), ()))
TN = (((0,), (0,)), ((), ()))


def dot(a, b, dims=NN):
    return lax.dot_general(a, b, dims, preferred_element_type=f32)


def iota(shape, dim):
    return lax.broadcasted_iota(i32, shape, dim)


def norm_parts(x):
    average = jnp.mean(x, axis=-1, keepdims=True)
    centred = x - average
    variance = jnp.mean(centred * centred, axis=-1, keepdims=True)
    scale = lax.rsqrt(variance + EPSILON)
    return centred * scale, scale


def norm_pull(upstream, normed, scale, gain):
    m = upstream * gain
    first = jnp.mean(m, axis=-1, keepdims=True)
    second = jnp.mean(m * normed, axis=-1, keepdims=True)
    return scale * (m - first - normed * second)


def gelu_pair(u):
    u2 = u * u
    half = 0.5 + 0.5 * jnp.tanh(u * (GELU_A + (GELU_A * GELU_B) * u2))
    slope = half + (u + u) * (half * (1.0 - half)) * (GELU_A + (3.0 * GELU_A * GELU_B) * u2)
    return u * half, slope


def rows(start, size):
    return pl.ds(pl.multiple_of(start, size), size)


def block_kernel(
    tok, og, wqt, wkt, wvt, wo, gain1_in, gain2_in, up_hbm, dn_hbm, table, ids, lengths, prompt,
    final, tgrad, gsum, small, x_hi, g_hi, cnt, du_hbm, dd_hbm,
    count, wjt, gath, qkv, att_snd, att, wo_full, up, dn, snd_a, snd_b, g_own, x_own, gc, xc,
    pack, ag, act, eacc, eg_rcv, out_rcv, disp, disp_t, hid, hgrad, mixed, agr_snd, agr,
    lse, x_lo, g_lo, du, dk, dv, jg, wog_snd, wog_pair, wog_rcv, wog_sum, wog_x, gfull, gpart, rs_core, rs_rcv, rs_pair,
    sm_x, sm_e, sm_d,
    load_sem, fill_sem, nrm_s, nrm_r, wo_s, wo_r, gd_s, gd_r, xd_s, xd_r, eg_s, eg_r, out_s, out_r,
    att_s, att_r, agr_s, agr_r, ng_s, ng_r, wog_s, wog_r, wox_s, wox_r, gl_s, gl_r, gh_s, gh_r, xl_s, xl_r, xh_s, xh_r, ct_s, ct_r,
    ca_s, ca_r, a2_s, a2_r, a3_s, a3_r, a4_s, a4_r, sx_s, sx_r, se_s, se_r, sd_s, sd_r,
):
    h = lax.axis_index("head")
    e = lax.axis_index("expert")
    d = lax.axis_index("dp")
    right, left, across = lax.rem(h + 1, 4), lax.rem(h + 3, 4), lax.rem(h + 2, 4)
    x_peers = (right, left, across)
    x_from = (left, right, across)
    other = 1 - d
    twin = e + 1 - 2 * lax.rem(e, 2)

    def remote(src, dst, ss, rs, device):
        return pltpu.make_async_remote_copy(
            src_ref=src, dst_ref=dst, send_sem=ss, recv_sem=rs, device_id=device, device_id_type=MESH
        )

    def spread_copy(snd, rcv, ss, rs, k, back):
        p = lax.rem(e + (EXPERTS - k if back else k), EXPERTS)
        return remote(
            snd.at[rows(k * CAP, CAP)], rcv.at[rows(k * CAP, CAP)], ss.at[k], rs.at[k], (h, p, d)
        )

    def spread(snd, rcv, ss, rs, back=False, first=1, last=EXPERTS):
        def step(k, carry):
            spread_copy(snd, rcv, ss, rs, k, back).start()
            return carry

        lax.fori_loop(first, last, step, 0)
        if first == 1:
            rcv[0:CAP, :] = snd[0:CAP, :]

    def spread_recv(snd, rcv, ss, rs, back=False, first=1, last=EXPERTS):
        def step(k, carry):
            spread_copy(snd, rcv, ss, rs, k, back).wait_recv()
            return carry

        lax.fori_loop(first, last, step, 0)

    def spread_sent(snd, rcv, ss, rs, back=False):
        def step(k, carry):
            spread_copy(snd, rcv, ss, rs, k, back).wait_send()
            return carry

        lax.fori_loop(1, EXPERTS, step, 0)

    def cross(snd, rcv, ss, rs, only=None):
        view = (lambda r, i: r.at[i]) if only is None else (lambda r, i: r.at[i, pl.ds(0, only)])
        out = [
            remote(view(snd, p), view(rcv, h), ss.at[i], rs.at[i], (p, e, d))
            for i, p in enumerate(x_peers)
        ]
        into = [
            remote(view(snd, p), view(rcv, p), ss.at[i], rs.at[i], (p, e, d))
            for i, p in enumerate(x_from)
        ]
        return out, into

    def gather(buf, ss, rs, only=None):
        view = (lambda r, i: r.at[i]) if only is None else (lambda r, i: r.at[i, pl.ds(0, only)])
        out = [
            remote(view(buf, h), view(buf, h), ss.at[i], rs.at[i], (p, e, d))
            for i, p in enumerate(x_peers)
        ]
        into = [
            remote(view(buf, p), view(buf, p), ss.at[i], rs.at[i], (p, e, d))
            for i, p in enumerate(x_from)
        ]
        return out, into

    def relay_gather(buf, ss, rs):
        low, high = pl.ds(0, TOK // 2), pl.ds(TOK // 2, TOK // 2)

        def pair(i, there, view):
            return remote(view, view, ss.at[i], rs.at[i], (there, e, d))

        out = [
            pair(0, right, buf.at[h]),
            pair(1, left, buf.at[h]),
            pair(2, right, buf.at[left, low]),
            pair(3, left, buf.at[right, high]),
        ]
        into = [
            pair(0, left, buf.at[left]),
            pair(1, right, buf.at[right]),
            pair(2, left, buf.at[across, low]),
            pair(3, right, buf.at[across, high]),
        ]
        return out, into

    def token_copies(own, dst, ss, rs):
        def at(i, part=None):
            return dst.at[rows(i * HALF, HALF)] if part is None else dst.at[pl.ds(i * HALF + part, HALF // 2)]

        moves = [
            (own, at(2), right, d),
            (own, at(0), left, d),
            (own, at(3), h, other),
            (at(2, 0), at(1, 0), right, d),
            (at(0, HALF // 2), at(1, HALF // 2), left, d),
            (at(3), at(6), right, d),
            (at(3), at(4), left, d),
            (at(1), at(5), h, other),
        ]
        return [
            remote(src, to, ss.at[i], rs.at[i], (hh, e, dd)) for i, (src, to, hh, dd) in enumerate(moves)
        ]

    g_low = token_copies(gc.at[pl.ds(0, HALF)], g_lo, gl_s, gl_r)
    g_high = token_copies(gc.at[pl.ds(HALF, HALF)], g_hi, gh_s, gh_r)
    x_low = token_copies(xc.at[pl.ds(0, HALF)], x_lo, xl_s, xl_r)
    x_high = token_copies(xc.at[pl.ds(HALF, HALF)], x_hi, xh_s, xh_r)

    def start(copies, *which):
        for i in which:
            copies[i].start()

    def arrive(copies, *which):
        for i in which:
            copies[i].wait_recv()

    up_load = pltpu.make_async_copy(up_hbm, up, load_sem.at[0])
    dn_load = pltpu.make_async_copy(dn_hbm, dn, load_sem.at[1])
    up_load.start()
    dn_load.start()

    barrier = pltpu.get_barrier_semaphore()
    for p in x_peers:
        pl.semaphore_signal(barrier, inc=1, device_id=(p, e, d), device_id_type=MESH)
    pl.semaphore_signal(barrier, inc=1, device_id=(h, e, other), device_id_type=MESH)

    def greet(k, carry):
        pl.semaphore_signal(
            barrier, inc=1, device_id=(h, lax.rem(e + k, EXPERTS), d), device_id_type=MESH
        )
        return carry

    lax.fori_loop(1, EXPERTS, greet, 0)

    gain1 = gain1_in[...].reshape(1, D)
    gain2 = gain2_in[...].reshape(1, D)
    one, _ = norm_parts(tok[...].astype(f32))
    gath[h] = (one * gain1).astype(bf16)
    for i, w in enumerate((wqt, wkt, wvt)):
        wjt[i * PAD_COLS : i * PAD_COLS + HEAD_COLS, :] = w[...]
        wjt[i * PAD_COLS + HEAD_COLS : (i + 1) * PAD_COLS, :] = jnp.zeros(
            (PAD_COLS - HEAD_COLS, D), bf16
        )
    for i in range(4):
        wo_full[i, HEAD_COLS:PAD_COLS, :] = jnp.zeros((PAD_COLS - HEAD_COLS, D), bf16)
    wo_full[h, 0:HEAD_COLS, :] = wo[...]

    pl.semaphore_wait(barrier, 3 + 1 + EXPERTS - 1)
    nrm_out, nrm_into = relay_gather(gath, nrm_s, nrm_r)
    nrm_out[0].start()
    nrm_out[1].start()

    eye = iota((TOK, TOK), 0) == iota((TOK, TOK), 1)
    id_col = jnp.sum(jnp.where(eye, ids[...].astype(f32), 0.0), axis=1, keepdims=True).astype(i32)
    high, low = lax.shift_right_logical(id_col, 7), lax.bitwise_and(id_col, 127)
    pick = jnp.where(iota((TOK, 256), 1) == high, 1.0, 0.0).astype(bf16)
    near = dot(pick, table[...].astype(f32).astype(bf16))
    lane = iota((TOK, 128), 1)
    chosen = jnp.sum(jnp.where(lane == low, near, 0.0), axis=1, keepdims=True)
    member = jnp.where(lane == chosen.astype(i32), 1.0, 0.0)
    before = jnp.where(iota((TOK, TOK), 1) < iota((TOK, TOK), 0), 1.0, 0.0).astype(bf16)
    rank = jnp.sum(dot(before, member.astype(bf16)) * member, axis=1, keepdims=True)
    ahead = chosen - e.astype(f32)
    slot = jnp.where(ahead < 0.0, ahead + EXPERTS, ahead) * CAP + rank
    slot_row = jnp.sum(jnp.where(eye, slot, 0.0), axis=0, keepdims=True).astype(i32)
    disp_t[...] = jnp.where(iota((TOK, SLOTS), 1) == slot.astype(i32), 1.0, 0.0).astype(bf16)
    disp[...] = jnp.where(iota((SLOTS, TOK), 0) == slot_row, 1.0, 0.0).astype(bf16)
    sm_x[h] = jnp.zeros((8, D), f32)
    sm_x[h, 2:3, 0:128] = jnp.sum(member, axis=0, keepdims=True)

    snd_a[...] = dot(disp[...], og[...]).astype(bf16)
    spread(snd_a, g_own, gd_s, gd_r)

    column_scale = jnp.where(iota((1, D), 1) < PAD_COLS, 0.125, 1.0)

    def project(b):
        qkv[rows(b * TOK, TOK), :] = (dot(gath[b], wjt[...], NT) * column_scale).astype(bf16)

    core = lax.rem(e, 2)
    wo_mine = pl.ds(pl.multiple_of(core * 96, 96), 96)
    wo_twin = pl.ds(pl.multiple_of((1 - core) * 96, 96), 96)

    def wo_copy(i, block, part, device):
        view = wo_full.at[block, part]
        return remote(view, view, wo_s.at[i], wo_r.at[i], device)

    wo_out = [wo_copy(i, h, wo_mine, (p, e, d)) for i, p in enumerate(x_peers)]
    wo_into = [wo_copy(i, p, wo_mine, (p, e, d)) for i, p in enumerate(x_from)]
    wo_out2 = [wo_copy(3 + i, p, wo_mine, (h, twin, d)) for i, p in enumerate(x_from)]
    wo_into2 = [wo_copy(3 + i, p, wo_twin, (h, twin, d)) for i, p in enumerate(x_from)]
    project(h)
    nrm_into[0].wait_recv()
    nrm_out[2].start()
    nrm_into[1].wait_recv()
    nrm_out[3].start()
    start(wo_out, 0, 1, 2)
    project(left)
    project(right)
    spread_recv(snd_a, g_own, gd_s, gd_r)
    there = jnp.max(jnp.abs(g_own[...].astype(f32)), axis=1, keepdims=True) > 0.0
    there_f = jnp.where(there, 1.0, 0.0)
    earlier = jnp.where(iota((SLOTS, SLOTS), 1) < iota((SLOTS, SLOTS), 0), 1.0, 0.0).astype(bf16)
    place = dot(earlier, jnp.broadcast_to(there_f, (SLOTS, 128)).astype(bf16))[:, 0:1]
    place = jnp.where(there, place, -1.0).astype(i32)
    pack[...] = jnp.where(iota((SLOTS, SLOTS), 1) == place, 1.0, 0.0).astype(bf16)
    gc[...] = dot(pack[...], g_own[...], TN).astype(bf16)
    count[...] = jnp.broadcast_to(jnp.sum(there_f, axis=0, keepdims=True), (8, 128))
    c_out = [
        remote(count, cnt.at[slot_at], ct_s.at[i], ct_r.at[i], device)
        for i, (slot_at, device) in enumerate(
            ((2, (right, e, d)), (0, (left, e, d)), (1, (across, e, d)), (3, (h, e, other)))
        )
    ]
    c_pair = remote(cnt.at[pl.ds(0, 3)], cnt.at[pl.ds(4, 3)], ct_s.at[4], ct_r.at[4], (h, e, other))
    start(c_out, 0, 1, 2, 3)
    start(g_low, 2)

    nrm_into[2].wait_recv()
    nrm_into[3].wait_recv()
    project(across)


    ends = []
    total = 0
    for j in range(8):
        total = total + lengths[0, j]
        ends.append(total)

    def segment(pos):
        found = jnp.zeros(pos.shape, i32)
        for j in range(8):
            found = found + jnp.where(ends[j] <= pos, 1, 0)
        return found

    def window(b):
        first = jnp.minimum(jnp.maximum(b - 1, 0), 1) * TOK
        q_pos = b * TOK + iota((TOK, 1), 0)
        k_pos = first + iota((1, WIN), 1)
        said = prompt[:, pl.ds(pl.multiple_of(first, TOK), WIN)]
        k_least = jnp.where(said == 1, -1, k_pos)
        allowed = (segment(q_pos) == segment(k_pos)) & (k_least <= q_pos)
        return pl.ds(pl.multiple_of(first, TOK), WIN), allowed

    lane_low = iota((TOK, 128), 1) < 64

    def head_mask(head, x):
        if head == 2:
            return x
        return jnp.where(lane_low if head == 0 else jnp.logical_not(lane_low), x, jnp.zeros_like(x))

    def head_lanes(head, part):
        return pl.ds(part * PAD_COLS + (head // 2) * 128, 128)

    def attend(b):
        keys, allowed = window(b)
        mine = rows(b * TOK, TOK)
        groups = [None, None]
        for head in range(3):
            q = head_mask(head, qkv[mine, head_lanes(head, 0)])
            s = dot(q, qkv[keys, head_lanes(head, 1)], NT)
            s = jnp.where(allowed, s, NEGATIVE)
            top = jnp.max(s, axis=-1, keepdims=True)
            p = jnp.exp(s - top)
            total = jnp.sum(p, axis=-1, keepdims=True)
            lse[mine, head : head + 1] = top + jnp.log(total)
            o = dot(p.astype(bf16), qkv[keys, head_lanes(head, 2)]) * (1.0 / total)
            o = head_mask(head, o)
            g = head // 2
            groups[g] = o if groups[g] is None else groups[g] + o
        att_snd[b, :, 0:128] = groups[0].astype(bf16)
        att_snd[b, :, 128:256] = groups[1].astype(bf16)

    def att_copy(i):
        p = lax.rem(h + 1 + i, 4)
        return remote(att_snd.at[p], att.at[h], att_s.at[i], att_r.at[i], (p, e, d))

    def attend_away(i, carry):
        attend(lax.rem(h + 1 + i, 4))
        att_copy(i).start()
        return carry

    lax.fori_loop(0, 3, attend_away, 0)
    attend(h)
    start(g_low, 0, 1)
    att_out = [att_copy(i) for i in range(3)]
    att[h] = att_snd[h]

    for i in range(3):
        wo_into[i].wait_recv()
        wo_out2[i].start()
    arrive(att_out, 0, 1, 2)
    for c in wo_into2:
        c.wait_recv()
    for i in range(4):
        part = dot(att[i], wo_full[i])
        hid[...] = (tok[...].astype(f32) if i == 0 else hid[...]) + part
    two, _ = norm_parts(hid[...])
    snd_b[...] = dot(disp[...], (two * gain2).astype(bf16)).astype(bf16)
    spread(snd_b, x_own, xd_s, xd_r)

    arrive(c_out, 0, 1, 2, 3)
    c_pair.start()
    arrive(g_low, 2)
    start(g_low, 5, 6)
    dn_load.wait()

    def back_down(c, carry):
        part = pl.ds(pl.multiple_of(c * FF_CHUNK, FF_CHUNK), FF_CHUNK)
        ag[:, part] = dot(g_own[...], dn[part, :], NT).astype(bf16)
        return carry

    lax.fori_loop(0, FF // FF_CHUNK, back_down, 0)
    up_load.wait()
    spread_sent(snd_a, g_own, gd_s, gd_r)
    arrive(g_low, 0, 1)
    start(g_low, 3, 4)
    start(g_high, 0, 1)
    spread_recv(snd_b, x_own, xd_s, xd_r, last=8)

    eacc[...] = jnp.zeros_like(eacc)

    def expert(r):
        def step(c, carry):
            part = pl.ds(pl.multiple_of(c * FF_CHUNK, FF_CHUNK), FF_CHUNK)
            value, slope = gelu_pair(dot(x_own[r, :], up[:, part]))
            act[r, part] = value.astype(bf16)
            pre_grad = (ag[r, part].astype(f32) * slope).astype(bf16)
            ag[r, part] = pre_grad
            eacc[r, :] += dot(pre_grad, up[:, part], NT)
            return carry

        lax.fori_loop(0, FF // FF_CHUNK, step, 0)
        snd_a[r, :] = eacc[r, :].astype(bf16)

    expert(pl.ds(0, HALF))
    spread(snd_a, eg_rcv, eg_s, eg_r, True, last=8)
    spread_recv(snd_b, x_own, xd_s, xd_r, first=8)
    xc[...] = dot(pack[...], x_own[...], TN).astype(bf16)
    start(x_low, 0, 1)
    expert(pl.ds(HALF, HALF))
    spread(snd_a, eg_rcv, eg_s, eg_r, True, first=8)
    start(x_low, 2)
    arrive(g_low, 3, 4)
    start(g_low, 7)
    spread_sent(snd_b, x_own, xd_s, xd_r)
    eacc[...] = jnp.zeros_like(eacc)

    def produce(c, carry):
        part = pl.ds(pl.multiple_of(c * FF_CHUNK, FF_CHUNK), FF_CHUNK)
        eacc[...] += dot(act[:, part], dn[part, :])
        return carry

    lax.fori_loop(0, FF // FF_CHUNK, produce, 0)
    snd_b[...] = eacc[...].astype(bf16)
    arrive(x_low, 0, 1)
    start(x_low, 3, 4)
    spread_recv(snd_a, eg_rcv, eg_s, eg_r, True)

    two, scale2 = norm_parts(hid[...])
    back = dot(disp_t[...], eg_rcv[...])
    sm_x[h, 1:2, :] = jnp.sum(back * two, axis=0, keepdims=True)
    hgrad[...] = og[...].astype(f32) + norm_pull(back, two, scale2, gain2)
    mixed[...] = hgrad[...].astype(bf16)

    def back_output(i, carry):
        agr_snd[i] = dot(mixed[...], wo_full[i], NT).astype(bf16)
        return carry

    lax.fori_loop(0, 4, back_output, 0)
    for c in wo_out + wo_out2:
        c.wait_send()
    agr_out, agr_into = cross(agr_snd, agr, agr_s, agr_r)
    for c in agr_out:
        c.start()
    agr[h] = agr_snd[h]
    arrive(x_low, 3, 4)
    start(x_low, 7)
    start(g_high, 2)

    def output_grad(i, carry):
        wog_snd[i] = dot(att[i], mixed[...], TN).astype(bf16)
        return carry

    lax.fori_loop(0, 4, output_grad, 0)
    wog_twin = [
        remote(wog_snd.at[i, wo_twin], wog_pair.at[i], wog_s.at[3 + i], wog_r.at[3 + i], (h, twin, d))
        for i in range(4)
    ]
    for c in wog_twin:
        c.start()
    dk[...] = jnp.zeros_like(dk)
    dv[...] = jnp.zeros_like(dv)
    for c in agr_into:
        c.wait_recv()

    def attend_back(b, carry):
        keys, allowed = window(b)
        mine = rows(b * TOK, TOK)
        groups = [None, None]
        for head in range(3):
            lanes = pl.ds((head // 2) * 128, 128)
            q = head_mask(head, qkv[mine, head_lanes(head, 0)])
            k = qkv[keys, head_lanes(head, 1)]
            v = qkv[keys, head_lanes(head, 2)]
            u = head_mask(head, agr[b, :, lanes])
            inner = jnp.sum(u.astype(f32) * att_snd[b, :, lanes].astype(f32), axis=-1, keepdims=True)
            s = jnp.where(allowed, dot(q, k, NT), NEGATIVE)
            chances = jnp.exp(s - lse[mine, head : head + 1])
            score_grad = (chances * (dot(u, v, NT) - inner)).astype(bf16)
            part = head_mask(head, dot(score_grad, k)) * 0.125
            g = head // 2
            groups[g] = part if groups[g] is None else groups[g] + part
            dk[keys, lanes] += dot(score_grad, q, TN)
            dv[keys, lanes] += dot(chances.astype(bf16), u, TN)
        jg[mine, 0:128] = groups[0].astype(bf16)
        jg[mine, 128:256] = groups[1].astype(bf16)
        return carry

    for i in range(4):
        wog_twin[i].wait_recv()
        wog_pair[i] = (wog_snd[i, wo_mine, :].astype(f32) + wog_pair[i].astype(f32)).astype(bf16)
    y = lax.div(e, 4)
    over_y = [
        remote(
            wog_pair.at[lax.rem(y + i, 4)], wog_rcv.at[i], wog_s.at[i - 1], wog_r.at[i - 1],
            (h, lax.rem(e + 4 * i, EXPERTS), d),
        )
        for i in range(1, 4)
    ]
    for c in over_y:
        c.start()
    lax.fori_loop(0, 2, attend_back, 0)
    arrive(over_y, 0, 1, 2)
    wog_sum[...] = (
        wog_pair[y].astype(f32) + wog_rcv[1].astype(f32) + wog_rcv[2].astype(f32) + wog_rcv[3].astype(f32)
    ).astype(bf16)
    over_x = [
        remote(wog_sum, wog_x.at[i], wox_s.at[i], wox_r.at[i], (lax.rem(h + i, 4), e, d)) for i in range(1, 4)
    ]
    for i in range(1, 4):

        @pl.when(lax.rem(h + i, 4) == y)
        def _(i=i):
            over_x[i - 1].start()

    arrive(x_low, 2)
    start(x_low, 5, 6)
    arrive(g_high, 0, 1)
    start(g_high, 3, 4)
    lax.fori_loop(2, 4, attend_back, 0)
    jg[:, PAD_COLS : 2 * PAD_COLS] = dk[...].astype(bf16)
    jg[:, 2 * PAD_COLS : 3 * PAD_COLS] = dv[...].astype(bf16)

    du_out = jg.at[pl.ds(0, D), pl.ds(0, FF_CHUNK)]
    dd_out = eg_rcv

    def fill_copies(c):
        part = rows(c * FF_CHUNK, FF_CHUNK)
        return (
            pltpu.make_async_copy(du_out, du_hbm.at[:, part], fill_sem.at[0]),
            pltpu.make_async_copy(dd_out, dd_hbm.at[part], fill_sem.at[1]),
        )

    def fill(c):
        part = rows(c * FF_CHUNK, FF_CHUNK)
        du[...] = dot(x_own[...], ag[:, part], TN)
        eacc[...] = dot(act[:, part], g_own[...], TN)

        def tile(i, carry):
            @pl.when(jnp.logical_and(c == 0, i == 1))
            def _():
                arrive(g_low, 5, 6, 7)
                arrive(x_low, 5, 6, 7)

            r = rows(i * FILL_TILE, FILL_TILE)
            x, g = x_lo[r, :], g_lo[r, :]
            value, slope = gelu_pair(dot(x, up[:, part]))
            pre_grad = (dot(g, dn[part, :], NT) * slope).astype(bf16)
            du[...] += dot(x, pre_grad, TN)
            eacc[...] += dot(value.astype(bf16), g, TN)
            return carry

        lax.fori_loop(0, BLOCKS * HALF // FILL_TILE, tile, 0)

        @pl.when(c > 0)
        def _():
            for copy in fill_copies(c - 1):
                copy.wait()

        du_out[...] = du[...].astype(bf16)
        dd_out[...] = eacc[...].astype(bf16)
        for copy in fill_copies(c):
            copy.start()

    for c in wog_twin:
        c.wait_send()
    ng_out, ng_into = cross(wog_snd, wo_full, ng_s, ng_r)
    for i, p in enumerate((across, right, left)):
        wog_snd[p] = dot(jg[rows(p * TOK, TOK), :], wjt[...]).astype(bf16)
        ng_out[(2, 0, 1)[i]].start()
    spread(snd_b, out_rcv, out_s, out_r, True)

    gain1_part = jnp.zeros((1, D), f32)
    for part in range(3):
        grad = jnp.zeros((PAD_COLS, D), f32)
        for b in range(4):
            grad = grad + dot(jg[b * TOK : (b + 1) * TOK, part * PAD_COLS : (part + 1) * PAD_COLS], gath[b], TN)
        gain1_part = gain1_part + jnp.sum(
            grad * wjt[part * PAD_COLS : (part + 1) * PAD_COLS, :].astype(f32), axis=0, keepdims=True
        )
        gfull[part * HEAD_COLS : (part + 1) * HEAD_COLS, :] = grad[0:HEAD_COLS, :].astype(bf16)
    sm_x[h, 0:1, :] = gain1_part / gain1

    mine_half = rows(core * 384, 384)
    twin_half = rows((1 - core) * 384, 384)
    mine_part = pl.ds(pl.multiple_of(core * 288, 288), 288)
    twin_part = pl.ds(pl.multiple_of((1 - core) * 288, 288), 288)
    ca_out = remote(gfull.at[twin_part], rs_core, ca_s.at[0], ca_r.at[0], (h, twin, d))
    ca_out.start()
    sx_out, sx_into = gather(sm_x, sx_s, sx_r)
    for c in sx_out:
        c.start()
    start(x_high, 0, 1, 2)
    arrive(g_high, 2)
    start(g_high, 5, 6)

    tgrad[...] = dot(jg[rows(h * TOK, TOK), :], wjt[...])
    unit = lax.div(e, 2)
    here = rows(core * 384 + unit * 48, 48)

    def peer(k):
        return lax.rem(unit + k, 8)

    def a2_copy(k, where):
        p = peer(k)
        return remote(
            gpart.at[rows(p * 48, 48)], rs_rcv.at[where], a2_s.at[k], a2_r.at[k], (h, p * 2 + core, d)
        )

    def small_copy(k, p, where):
        return remote(sm_e.at[e], sm_e.at[where], se_s.at[k], se_r.at[k], (h, p, d))

    def small_start(k, carry):
        p = lax.rem(e + k, EXPERTS)
        small_copy(k, p, e).start()
        return carry

    a3 = remote(rs_pair.at[d], rs_pair.at[d], a3_s.at[0], a3_r.at[0], (h, e, other))
    a3_in = remote(rs_pair.at[other], rs_pair.at[other], a3_s.at[0], a3_r.at[0], (h, e, other))
    def a4_copy(k, p, place):
        return remote(gsum.at[place], gsum.at[place], a4_s.at[k], a4_r.at[k], (h, p * 2 + core, d))


    def small_recv(k, carry):
        p = lax.rem(e + EXPERTS - k, EXPERTS)
        small_copy(k, p, p).wait_recv()
        return carry

    sd = remote(sm_d.at[d], sm_d.at[d], sd_s.at[0], sd_r.at[0], (h, e, other))
    sd_in = remote(sm_d.at[other], sm_d.at[other], sd_s.at[0], sd_r.at[0], (h, e, other))
    a5 = remote(gsum.at[mine_half], gsum.at[mine_half], ca_s.at[1], ca_r.at[1], (h, twin, d))
    a5_in = remote(gsum.at[twin_half], gsum.at[twin_half], ca_s.at[1], ca_r.at[1], (h, twin, d))

    def chunk(c, carry):
        @pl.when(c == 1)
        def _():
            ca_out.wait_recv()
            gpart[288:384, :] = jnp.zeros((96, D), bf16)

            @pl.when(y == h)
            def _():
                wog = wog_sum[...].astype(f32)
                for i in range(1, 4):
                    over_x[i - 1].wait_recv()
                    wog = wog + wog_x[i].astype(f32)
                gpart[288:384, :] = wog.astype(bf16)

            for i in range(1, 4):

                @pl.when(lax.rem(h + i, 4) == y)
                def _(i=i):
                    over_x[i - 1].wait_send()

            gpart[0:288, :] = (gfull[mine_part, :].astype(f32) + rs_core[...].astype(f32)).astype(bf16)

            for k in range(1, 8):
                a2_copy(k, unit).start()
            rs_rcv[unit] = gpart[rows(unit * 48, 48), :]

        @pl.when(c == 3)
        def _():
            for c in sx_into:
                c.wait_recv()
            sm_e[e] = (sm_x[0] + sm_x[1]) + (sm_x[2] + sm_x[3])
            lax.fori_loop(1, EXPERTS, small_start, 0)

            for k in range(1, 8):
                a2_copy(k, peer(8 - k)).wait_recv()
            reduced = rs_rcv[0].astype(f32)
            for k in range(1, 8):
                reduced = reduced + rs_rcv[k].astype(f32)
            rs_pair[d] = reduced.astype(bf16)
            a3.start()

        @pl.when(c == 4)
        def _():
            for c in ng_into:
                c.wait_recv()
            own_grad = tgrad[...]
            for p in x_from:
                own_grad = own_grad + wo_full[p].astype(f32)
            one, scale1 = norm_parts(tok[...].astype(f32))
            tgrad[...] = hgrad[...] + norm_pull(own_grad, one, scale1, gain1)
            arrive(x_high, 0, 1)
            start(x_high, 3, 4)
            arrive(x_high, 2)
            start(x_high, 5, 6)
            arrive(g_high, 3, 4)
            start(g_high, 7)

            spread_recv(snd_b, out_rcv, out_s, out_r, True)
            final[...] = hid[...] + dot(disp_t[...], out_rcv[...])

            a3_in.wait_recv()
            gsum[here, :] = (rs_pair[0].astype(f32) + rs_pair[1].astype(f32)).astype(bf16)

            for k in range(1, 8):
                a4_copy(k, peer(k), here).start()

            lax.fori_loop(1, EXPERTS, small_recv, 0)
            gathered = sm_e[0]
            for k in range(1, EXPERTS):
                gathered = gathered + sm_e[k]
            sm_d[d] = gathered
            sd.start()

        @pl.when(c == 5)
        def _():
            arrive(x_high, 3, 4)
            start(x_high, 7)
            for k in range(1, 8):
                p = peer(8 - k)
                a4_copy(k, p, rows(core * 384 + p * 48, 48)).wait_recv()
            for k in range(1, 8):
                a4_copy(k, peer(k), here).wait_send()
            a5.start()

        fill(c)
        return carry

    lax.fori_loop(0, FF // FF_CHUNK, chunk, 0)

    spread_sent(snd_a, eg_rcv, eg_s, eg_r, True)
    spread_sent(snd_b, out_rcv, out_s, out_r, True)

    def small_sent(k, carry):
        p = lax.rem(e + k, EXPERTS)
        small_copy(k, p, e).wait_send()
        return carry

    lax.fori_loop(1, EXPERTS, small_sent, 0)
    for k in range(1, 8):
        a2_copy(k, unit).wait_send()
    for c in (
        nrm_out + att_out + g_low + g_high + x_low + x_high[:7] + c_out + [c_pair] + agr_out + over_y + ng_out
        + sx_out + [ca_out, a3, sd]
    ):
        c.wait_send()

    sd_in.wait_recv()
    small[...] = sm_d[0] + sm_d[1]
    a5_in.wait_recv()
    arrive(g_high, 5, 6, 7)
    arrive(x_high, 5, 6, 7)
    c_pair.wait_recv()
    for copy in fill_copies(5):
        copy.wait()
    x_high[7].wait_send()
    a5.wait_send()


def block_call(*args):
    vmem = pl.BlockSpec(memory_space=pltpu.VMEM)
    hbm = pl.BlockSpec(memory_space=pl.ANY)
    smem = pl.BlockSpec(memory_space=pltpu.SMEM)
    dma = pltpu.SemaphoreType.DMA

    def buf(*shape, dtype=bf16):
        return pltpu.VMEM(shape, dtype)

    scratch = [
        buf(8, 128, dtype=f32), buf(D, D), buf(4, TOK, D), buf(ROW, D), buf(4, TOK, PAD_COLS), buf(4, TOK, PAD_COLS),
        buf(4, PAD_COLS, D), buf(D, FF), buf(FF, D), buf(SLOTS, D), buf(SLOTS, D), buf(SLOTS, D),
        buf(SLOTS, D), buf(SLOTS, D), buf(SLOTS, D),
        buf(SLOTS, SLOTS), buf(SLOTS, FF), buf(SLOTS, FF), buf(SLOTS, D, dtype=f32),
        buf(SLOTS, D), buf(SLOTS, D), buf(SLOTS, TOK), buf(TOK, SLOTS),
        buf(TOK, D, dtype=f32), buf(TOK, D, dtype=f32), buf(TOK, D), buf(4, TOK, PAD_COLS), buf(4, TOK, PAD_COLS),
        buf(ROW, 128, dtype=f32), buf(BLOCKS * HALF, D), buf(BLOCKS * HALF, D), buf(D, FF_CHUNK, dtype=f32),
        buf(ROW, PAD_COLS, dtype=f32), buf(ROW, PAD_COLS, dtype=f32),
        buf(ROW, D), buf(4, PAD_COLS, D), buf(4, 96, D), buf(4, 96, D), buf(96, D), buf(4, 96, D),
        buf(3 * HEAD_COLS, D), buf(384, D), buf(288, D), buf(8, 48, D), buf(2, 48, D),
        buf(4, 8, D, dtype=f32), buf(EXPERTS, 8, D, dtype=f32), buf(2, 8, D, dtype=f32),
        dma((2,)), dma((2,)),
    ]
    for n in (4, 6, 16, 16, 16, 16, 3, 3, 3, 7, 4, 8, 8, 8, 8, 5, 2, 8, 1, 8, 3, 16, 1):
        scratch += [dma((n,)), dma((n,))]
    return pl.pallas_call(
        block_kernel,
        out_shape=[
            jax.ShapeDtypeStruct((TOK, D), f32),
            jax.ShapeDtypeStruct((TOK, D), f32),
            jax.ShapeDtypeStruct((D, D), bf16),
            jax.ShapeDtypeStruct((8, D), f32),
            jax.ShapeDtypeStruct((BLOCKS * HALF, D), bf16),
            jax.ShapeDtypeStruct((BLOCKS * HALF, D), bf16),
            jax.ShapeDtypeStruct((BLOCKS, 8, 128), f32),
            jax.ShapeDtypeStruct((D, FF), bf16),
            jax.ShapeDtypeStruct((FF, D), bf16),
        ],
        in_specs=[vmem] * 8 + [hbm, hbm, vmem, vmem, smem, vmem],
        out_specs=[vmem] * 4 + [hbm, hbm, vmem, hbm, hbm],
        scratch_shapes=scratch,
        compiler_params=pltpu.CompilerParams(
            collective_id=1, has_side_effects=True, vmem_limit_bytes=64 * 2**20 - 2**16
        ),
    )(*args)


GRAD_TILE = 512
REST_TILE = 256


def finish_kernel(
    cnt, x_ref, g_ref, up_ref, dn_ref, du0, dd0, gsum, small, final_in, tgrad_in,
    du_ref, dd_ref, final, tgrad, wq, wk, wv, wo, gain1, gain2, loads,
    xs, gs, total_ref,
):
    step = pl.program_id(0)
    final[...] = final_in[...]
    tgrad[...] = tgrad_in[...]

    @pl.when(step == 0)
    def _():
        total = 0
        for b in range(BLOCKS):
            there = pl.ds(pl.multiple_of(total, 16), HALF)
            more = jnp.maximum(cnt[b, 0, 0].astype(i32) - HALF, 0)

            @pl.when(more > 0)
            def _(b=b, there=there):
                xs[there, :] = x_ref[b * HALF : (b + 1) * HALF, :]
                gs[there, :] = g_ref[b * HALF : (b + 1) * HALF, :]

            total = total + lax.div(more + 15, 16) * 16
        tail = pl.ds(pl.multiple_of(total, 16), GRAD_TILE)
        xs[tail, :] = jnp.zeros((GRAD_TILE, D), bf16)
        gs[tail, :] = jnp.zeros((GRAD_TILE, D), bf16)
        total_ref[0] = total
        for i, w in enumerate((wq, wk, wv)):
            first = i * HEAD_COLS
            for piece in range(12):
                r = first + piece * 16
                at = r if r < 288 else r + 96
                w[piece * 16 : piece * 16 + 16, :] = gsum[at : at + 16, :].astype(f32)
        wo[0:96, :] = gsum[288:384, :].astype(f32)
        wo[96:192, :] = gsum[672:768, :].astype(f32)
        gain1[...] = small[0:1, :].reshape(D)
        gain2[...] = small[1:2, :].reshape(D)
        loads[...] = small[2:3, 0:128].astype(i32).reshape(128)

    total = total_ref[0]
    du_ref[...] = du0[...].astype(f32)
    dd_ref[...] = dd0[...].astype(f32)

    for count in range(1, BLOCKS * HALF // REST_TILE + 1):

        @pl.when(lax.div(total + REST_TILE - 1, REST_TILE) == count)
        def _(size=count * REST_TILE):
            x, g = xs[0:size, :], gs[0:size, :]
            value, slope = gelu_pair(dot(x, up_ref[...]))
            pre_grad = (dot(g, dn_ref[...], NT) * slope).astype(bf16)
            du_ref[...] += dot(x, pre_grad, TN)
            dd_ref[...] += dot(value.astype(bf16), g, TN)


def finish_call(cnt, x_hi, g_hi, up, dn, du0, dd0, gsum, small, final, tgrad):
    def whole(*shape):
        return pl.BlockSpec(shape, lambda i: (0,) * len(shape))

    share = pl.BlockSpec((TOK, D // 6), lambda i: (0, i))
    columns = pl.BlockSpec((D, FF_CHUNK), lambda i: (0, i))
    lines = pl.BlockSpec((FF_CHUNK, D), lambda i: (i, 0))
    return pl.pallas_call(
        finish_kernel,
        grid=(FF // FF_CHUNK,),
        in_specs=[
            pl.BlockSpec((BLOCKS, 8, 128), lambda i: (0, 0, 0), memory_space=pltpu.SMEM), whole(BLOCKS * HALF, D), whole(BLOCKS * HALF, D),
            columns, lines, columns, lines, whole(D, D), whole(8, D), share, share,
        ],
        out_specs=[columns, lines, share, share] + [whole(HEAD_COLS, D)] * 4 + [whole(D), whole(D), whole(128)],
        out_shape=[
            jax.ShapeDtypeStruct((D, FF), f32),
            jax.ShapeDtypeStruct((FF, D), f32),
            jax.ShapeDtypeStruct((TOK, D), f32),
            jax.ShapeDtypeStruct((TOK, D), f32),
        ]
        + [jax.ShapeDtypeStruct((HEAD_COLS, D), f32)] * 4
        + [
            jax.ShapeDtypeStruct((D,), f32),
            jax.ShapeDtypeStruct((D,), f32),
            jax.ShapeDtypeStruct((128,), i32),
        ],
        scratch_shapes=[
            pltpu.VMEM((BLOCKS * HALF + GRAD_TILE, D), bf16),
            pltpu.VMEM((BLOCKS * HALF + GRAD_TILE, D), bf16),
            pltpu.SMEM((1,), i32),
        ],
        compiler_params=pltpu.CompilerParams(vmem_limit_bytes=64 * 2**20 - 2**16),
    )(cnt, x_hi, g_hi, up, dn, du0, dd0, gsum, small, final, tgrad)


def body(
    tokens, out_grad, w_query, w_key, w_value, w_output, gain_one, gain_two, expert_up, expert_down,
    hash_table, token_ids, doc_lengths, turn_mask,
):
    final, tokens_grad, gsum, small, x_hi, g_hi, cnt, du0, dd0 = block_call(
        tokens[0], out_grad[0], w_query.T, w_key.T, w_value.T, w_output, gain_one, gain_two,
        expert_up[0], expert_down[0], hash_table.reshape(256, 128), token_ids, doc_lengths, turn_mask,
    )
    up_grad, down_grad, final, tokens_grad, wq, wk, wv, wo, gain1, gain2, loads = finish_call(
        cnt, x_hi, g_hi, expert_up[0], expert_down[0], du0, dd0, gsum, small, final, tokens_grad
    )
    return (
        final[None], tokens_grad[None], wq.T, wk.T, wv.T, wo, gain1, gain2, up_grad[None], down_grad[None],
        loads[:EXPERTS],
    )


def solution(mesh):
    rows_spec = P(("expert", "dp"), "head", None)
    in_specs = (
        rows_spec, rows_spec, P(None, "head"), P(None, "head"), P(None, "head"), P("head", None),
        P(), P(), P("expert", None, None), P("expert", None, None), P(),
        P(("expert", "dp"), "head"), P(("expert", "dp"), None), P(("expert", "dp"), None),
    )
    out_specs = (
        rows_spec, rows_spec, P(None, "head"), P(None, "head"), P(None, "head"), P("head", None),
        P(), P(), P("expert", None, None), P("expert", None, None), P(),
    )
    return jax.shard_map(body, mesh=mesh, in_specs=in_specs, out_specs=out_specs, check_vma=False)
```

```python
import functools

import jax
import jax.numpy as jnp
from jax import lax
from jax.experimental import pallas as pl
from jax.experimental.pallas import tpu as pltpu
from jax.sharding import PartitionSpec as P

MESH = pl.DeviceIdType.MESH
f32 = jnp.float32
bf16 = jnp.bfloat16
i32 = jnp.int32

HEADS_X = 4
EXPERTS = 16
TOK = 256
ROW = 1024
D = 768
FF = 3072
CAP = 32
SLOTS = EXPERTS * CAP
WIN = 768
HEAD_COLS = 192
PAD_COLS = 256
FF_CHUNK = 512
WIDE_CHUNK = 1024
HALF = SLOTS // 2
BLOCKS = 7
FILL_TILE = 896
EPSILON = 1e-05
NEGATIVE = -1e30
GELU_A = 0.7978845608028654
GELU_B = 0.044715

NN = (((1,), (0,)), ((), ()))
NT = (((1,), (1,)), ((), ()))
TN = (((0,), (0,)), ((), ()))


def dot(a, b, dims=NN):
    return lax.dot_general(a, b, dims, preferred_element_type=f32)


def iota(shape, dim):
    return lax.broadcasted_iota(i32, shape, dim)


def norm_parts(x):
    average = jnp.mean(x, axis=-1, keepdims=True)
    centred = x - average
    variance = jnp.mean(centred * centred, axis=-1, keepdims=True)
    scale = lax.rsqrt(variance + EPSILON)
    return centred * scale, scale


def norm_pull(upstream, normed, scale, gain):
    m = upstream * gain
    first = jnp.mean(m, axis=-1, keepdims=True)
    second = jnp.mean(m * normed, axis=-1, keepdims=True)
    return scale * (m - first - normed * second)


def gelu_pair(u):
    u2 = u * u
    half = 0.5 + 0.5 * jnp.tanh(u * (GELU_A + (GELU_A * GELU_B) * u2))
    slope = half + (u + u) * (half * (1.0 - half)) * (GELU_A + (3.0 * GELU_A * GELU_B) * u2)
    return u * half, slope


def rows(start, size):
    return pl.ds(pl.multiple_of(start, size), size)


def block_kernel(
    tok, og, wqt, wkt, wvt, wo, gain1_in, gain2_in, up_hbm, dn_hbm, table, ids, lengths, prompt,
    final, tgrad, gsum, small, x_hi, g_hi, cnt, du_hbm, dd_hbm,
    count, wjt, gath, qkv, att_snd, att, wo_full, up, dn, snd_a, snd_b, g_own, x_own, gc, xc,
    pack, ag, act, eacc, eg_rcv, out_rcv, disp, disp_t, hid, hgrad, mixed, agr_snd, agr,
    lse, x_lo, g_lo, du, dk, dv, jg, wog_snd, wog_pair, wog_rcv, wog_sum, wog_x, gfull, gpart, rs_core, rs_rcv, rs_pair,
    sm_x, sm_e, sm_d,
    load_sem, fill_sem, nrm_s, nrm_r, wo_s, wo_r, gd_s, gd_r, xd_s, xd_r, eg_s, eg_r, out_s, out_r,
    att_s, att_r, agr_s, agr_r, ng_s, ng_r, wog_s, wog_r, wox_s, wox_r, gl_s, gl_r, gh_s, gh_r, xl_s, xl_r, xh_s, xh_r, ct_s, ct_r,
    ca_s, ca_r, a2_s, a2_r, a3_s, a3_r, a4_s, a4_r, sx_s, sx_r, se_s, se_r, sd_s, sd_r,
):
    h = lax.axis_index("head")
    e = lax.axis_index("expert")
    d = lax.axis_index("dp")
    right, left, across = lax.rem(h + 1, 4), lax.rem(h + 3, 4), lax.rem(h + 2, 4)
    x_peers = (right, left, across)
    x_from = (left, right, across)
    other = 1 - d
    twin = e + 1 - 2 * lax.rem(e, 2)

    def remote(src, dst, ss, rs, device):
        return pltpu.make_async_remote_copy(
            src_ref=src, dst_ref=dst, send_sem=ss, recv_sem=rs, device_id=device, device_id_type=MESH
        )

    def spread_copy(snd, rcv, ss, rs, k, back):
        p = lax.rem(e + (EXPERTS - k if back else k), EXPERTS)
        return remote(
            snd.at[rows(k * CAP, CAP)], rcv.at[rows(k * CAP, CAP)], ss.at[k], rs.at[k], (h, p, d)
        )

    def spread(snd, rcv, ss, rs, back=False, first=1, last=EXPERTS):
        def step(k, carry):
            spread_copy(snd, rcv, ss, rs, k, back).start()
            return carry

        lax.fori_loop(first, last, step, 0)
        if first == 1:
            rcv[0:CAP, :] = snd[0:CAP, :]

    def spread_recv(snd, rcv, ss, rs, back=False, first=1, last=EXPERTS):
        def step(k, carry):
            spread_copy(snd, rcv, ss, rs, k, back).wait_recv()
            return carry

        lax.fori_loop(first, last, step, 0)

    def spread_sent(snd, rcv, ss, rs, back=False):
        def step(k, carry):
            spread_copy(snd, rcv, ss, rs, k, back).wait_send()
            return carry

        lax.fori_loop(1, EXPERTS, step, 0)

    def cross(snd, rcv, ss, rs, only=None):
        view = (lambda r, i: r.at[i]) if only is None else (lambda r, i: r.at[i, pl.ds(0, only)])
        out = [
            remote(view(snd, p), view(rcv, h), ss.at[i], rs.at[i], (p, e, d))
            for i, p in enumerate(x_peers)
        ]
        into = [
            remote(view(snd, p), view(rcv, p), ss.at[i], rs.at[i], (p, e, d))
            for i, p in enumerate(x_from)
        ]
        return out, into

    def gather(buf, ss, rs, only=None):
        view = (lambda r, i: r.at[i]) if only is None else (lambda r, i: r.at[i, pl.ds(0, only)])
        out = [
            remote(view(buf, h), view(buf, h), ss.at[i], rs.at[i], (p, e, d))
            for i, p in enumerate(x_peers)
        ]
        into = [
            remote(view(buf, p), view(buf, p), ss.at[i], rs.at[i], (p, e, d))
            for i, p in enumerate(x_from)
        ]
        return out, into

    def relay_gather(buf, ss, rs):
        low, high = pl.ds(0, TOK // 2), pl.ds(TOK // 2, TOK // 2)

        def pair(i, there, view):
            return remote(view, view, ss.at[i], rs.at[i], (there, e, d))

        out = [
            pair(0, right, buf.at[h]),
            pair(1, left, buf.at[h]),
            pair(2, right, buf.at[left, low]),
            pair(3, left, buf.at[right, high]),
        ]
        into = [
            pair(0, left, buf.at[left]),
            pair(1, right, buf.at[right]),
            pair(2, left, buf.at[across, low]),
            pair(3, right, buf.at[across, high]),
        ]
        return out, into

    def token_copies(own, dst, ss, rs):
        def at(i, part=None):
            return dst.at[rows(i * HALF, HALF)] if part is None else dst.at[pl.ds(i * HALF + part, HALF // 2)]

        moves = [
            (own, at(2), right, d),
            (own, at(0), left, d),
            (own, at(3), h, other),
            (at(2, 0), at(1, 0), right, d),
            (at(0, HALF // 2), at(1, HALF // 2), left, d),
            (at(3), at(6), right, d),
            (at(3), at(4), left, d),
            (at(1), at(5), h, other),
        ]
        return [
            remote(src, to, ss.at[i], rs.at[i], (hh, e, dd)) for i, (src, to, hh, dd) in enumerate(moves)
        ]

    g_low = token_copies(gc.at[pl.ds(0, HALF)], g_lo, gl_s, gl_r)
    g_high = token_copies(gc.at[pl.ds(HALF, HALF)], g_hi, gh_s, gh_r)
    x_low = token_copies(xc.at[pl.ds(0, HALF)], x_lo, xl_s, xl_r)
    x_high = token_copies(xc.at[pl.ds(HALF, HALF)], x_hi, xh_s, xh_r)

    def start(copies, *which):
        for i in which:
            copies[i].start()

    def arrive(copies, *which):
        for i in which:
            copies[i].wait_recv()

    up_load = pltpu.make_async_copy(up_hbm, up, load_sem.at[0])
    dn_load = pltpu.make_async_copy(dn_hbm, dn, load_sem.at[1])
    up_load.start()
    dn_load.start()

    barrier = pltpu.get_barrier_semaphore()
    for p in x_peers:
        pl.semaphore_signal(barrier, inc=1, device_id=(p, e, d), device_id_type=MESH)
    pl.semaphore_signal(barrier, inc=1, device_id=(h, e, other), device_id_type=MESH)

    def greet(k, carry):
        pl.semaphore_signal(
            barrier, inc=1, device_id=(h, lax.rem(e + k, EXPERTS), d), device_id_type=MESH
        )
        return carry

    lax.fori_loop(1, EXPERTS, greet, 0)

    gain1 = gain1_in[...].reshape(1, D)
    gain2 = gain2_in[...].reshape(1, D)
    one, _ = norm_parts(tok[...].astype(f32))
    gath[h] = (one * gain1).astype(bf16)
    for i, w in enumerate((wqt, wkt, wvt)):
        wjt[i * PAD_COLS : i * PAD_COLS + HEAD_COLS, :] = w[...]
        wjt[i * PAD_COLS + HEAD_COLS : (i + 1) * PAD_COLS, :] = jnp.zeros(
            (PAD_COLS - HEAD_COLS, D), bf16
        )
    for i in range(4):
        wo_full[i, HEAD_COLS:PAD_COLS, :] = jnp.zeros((PAD_COLS - HEAD_COLS, D), bf16)
    wo_full[h, 0:HEAD_COLS, :] = wo[...]

    pl.semaphore_wait(barrier, 3 + 1 + EXPERTS - 1)
    nrm_out, nrm_into = relay_gather(gath, nrm_s, nrm_r)
    nrm_out[0].start()
    nrm_out[1].start()

    eye = iota((TOK, TOK), 0) == iota((TOK, TOK), 1)
    id_col = jnp.sum(jnp.where(eye, ids[...].astype(f32), 0.0), axis=1, keepdims=True).astype(i32)
    high, low = lax.shift_right_logical(id_col, 7), lax.bitwise_and(id_col, 127)
    pick = jnp.where(iota((TOK, 256), 1) == high, 1.0, 0.0).astype(bf16)
    near = dot(pick, table[...].astype(f32).astype(bf16))
    lane = iota((TOK, 128), 1)
    chosen = jnp.sum(jnp.where(lane == low, near, 0.0), axis=1, keepdims=True)
    member = jnp.where(lane == chosen.astype(i32), 1.0, 0.0)
    before = jnp.where(iota((TOK, TOK), 1) < iota((TOK, TOK), 0), 1.0, 0.0).astype(bf16)
    rank = jnp.sum(dot(before, member.astype(bf16)) * member, axis=1, keepdims=True)
    ahead = chosen - e.astype(f32)
    slot = jnp.where(ahead < 0.0, ahead + EXPERTS, ahead) * CAP + rank
    slot_row = jnp.sum(jnp.where(eye, slot, 0.0), axis=0, keepdims=True).astype(i32)
    disp_t[...] = jnp.where(iota((TOK, SLOTS), 1) == slot.astype(i32), 1.0, 0.0).astype(bf16)
    disp[...] = jnp.where(iota((SLOTS, TOK), 0) == slot_row, 1.0, 0.0).astype(bf16)
    sm_x[h] = jnp.zeros((8, D), f32)
    sm_x[h, 2:3, 0:128] = jnp.sum(member, axis=0, keepdims=True)

    snd_a[...] = dot(disp[...], og[...]).astype(bf16)
    spread(snd_a, g_own, gd_s, gd_r)

    column_scale = jnp.where(iota((1, D), 1) < PAD_COLS, 0.125, 1.0)

    def project(b):
        qkv[rows(b * TOK, TOK), :] = (dot(gath[b], wjt[...], NT) * column_scale).astype(bf16)

    core = lax.rem(e, 2)
    wo_mine = pl.ds(pl.multiple_of(core * 96, 96), 96)
    wo_twin = pl.ds(pl.multiple_of((1 - core) * 96, 96), 96)

    def wo_copy(i, block, part, device):
        view = wo_full.at[block, part]
        return remote(view, view, wo_s.at[i], wo_r.at[i], device)

    wo_out = [wo_copy(i, h, wo_mine, (p, e, d)) for i, p in enumerate(x_peers)]
    wo_into = [wo_copy(i, p, wo_mine, (p, e, d)) for i, p in enumerate(x_from)]
    wo_out2 = [wo_copy(3 + i, p, wo_mine, (h, twin, d)) for i, p in enumerate(x_from)]
    wo_into2 = [wo_copy(3 + i, p, wo_twin, (h, twin, d)) for i, p in enumerate(x_from)]
    project(h)
    nrm_into[0].wait_recv()
    nrm_out[2].start()
    nrm_into[1].wait_recv()
    nrm_out[3].start()
    start(wo_out, 0, 1, 2)
    project(left)
    project(right)
    spread_recv(snd_a, g_own, gd_s, gd_r)
    there = jnp.max(jnp.abs(g_own[...].astype(f32)), axis=1, keepdims=True) > 0.0
    there_f = jnp.where(there, 1.0, 0.0)
    earlier = jnp.where(iota((SLOTS, SLOTS), 1) < iota((SLOTS, SLOTS), 0), 1.0, 0.0).astype(bf16)
    place = dot(earlier, jnp.broadcast_to(there_f, (SLOTS, 128)).astype(bf16))[:, 0:1]
    place = jnp.where(there, place, -1.0).astype(i32)
    pack[...] = jnp.where(iota((SLOTS, SLOTS), 1) == place, 1.0, 0.0).astype(bf16)
    gc[...] = dot(pack[...], g_own[...], TN).astype(bf16)
    count[...] = jnp.broadcast_to(jnp.sum(there_f, axis=0, keepdims=True), (8, 128))
    c_out = [
        remote(count, cnt.at[slot_at], ct_s.at[i], ct_r.at[i], device)
        for i, (slot_at, device) in enumerate(
            ((2, (right, e, d)), (0, (left, e, d)), (1, (across, e, d)), (3, (h, e, other)))
        )
    ]
    c_pair = remote(cnt.at[pl.ds(0, 3)], cnt.at[pl.ds(4, 3)], ct_s.at[4], ct_r.at[4], (h, e, other))
    start(c_out, 0, 1, 2, 3)
    start(g_low, 2)

    nrm_into[2].wait_recv()
    nrm_into[3].wait_recv()
    project(across)


    ends = []
    total = 0
    for j in range(8):
        total = total + lengths[0, j]
        ends.append(total)

    def segment(pos):
        found = jnp.zeros(pos.shape, i32)
        for j in range(8):
            found = found + jnp.where(ends[j] <= pos, 1, 0)
        return found

    def window(b):
        first = jnp.minimum(jnp.maximum(b - 1, 0), 1) * TOK
        q_pos = b * TOK + iota((TOK, 1), 0)
        k_pos = first + iota((1, WIN), 1)
        said = prompt[:, pl.ds(pl.multiple_of(first, TOK), WIN)]
        k_least = jnp.where(said == 1, -1, k_pos)
        allowed = (segment(q_pos) == segment(k_pos)) & (k_least <= q_pos)
        return pl.ds(pl.multiple_of(first, TOK), WIN), allowed

    lane_low = iota((TOK, 128), 1) < 64

    def head_mask(head, x):
        if head == 2:
            return x
        return jnp.where(lane_low if head == 0 else jnp.logical_not(lane_low), x, jnp.zeros_like(x))

    def head_lanes(head, part):
        return pl.ds(part * PAD_COLS + (head // 2) * 128, 128)

    def attend(b):
        keys, allowed = window(b)
        mine = rows(b * TOK, TOK)
        groups = [None, None]
        for head in range(3):
            q = head_mask(head, qkv[mine, head_lanes(head, 0)])
            s = dot(q, qkv[keys, head_lanes(head, 1)], NT)
            s = jnp.where(allowed, s, NEGATIVE)
            top = jnp.max(s, axis=-1, keepdims=True)
            p = jnp.exp(s - top)
            total = jnp.sum(p, axis=-1, keepdims=True)
            lse[mine, head : head + 1] = top + jnp.log(total)
            o = dot(p.astype(bf16), qkv[keys, head_lanes(head, 2)]) * (1.0 / total)
            o = head_mask(head, o)
            g = head // 2
            groups[g] = o if groups[g] is None else groups[g] + o
        att_snd[b, :, 0:128] = groups[0].astype(bf16)
        att_snd[b, :, 128:256] = groups[1].astype(bf16)

    def att_copy(i):
        p = lax.rem(h + 1 + i, 4)
        return remote(att_snd.at[p], att.at[h], att_s.at[i], att_r.at[i], (p, e, d))

    def attend_away(i, carry):
        attend(lax.rem(h + 1 + i, 4))
        att_copy(i).start()
        return carry

    lax.fori_loop(0, 3, attend_away, 0)
    attend(h)
    start(g_low, 0, 1)
    att_out = [att_copy(i) for i in range(3)]
    att[h] = att_snd[h]

    for i in range(3):
        wo_into[i].wait_recv()
        wo_out2[i].start()
    arrive(att_out, 0, 1, 2)
    for c in wo_into2:
        c.wait_recv()
    for i in range(4):
        part = dot(att[i], wo_full[i])
        hid[...] = (tok[...].astype(f32) if i == 0 else hid[...]) + part
    two, _ = norm_parts(hid[...])
    snd_b[...] = dot(disp[...], (two * gain2).astype(bf16)).astype(bf16)
    spread(snd_b, x_own, xd_s, xd_r)

    arrive(c_out, 0, 1, 2, 3)
    c_pair.start()
    arrive(g_low, 2)
    start(g_low, 5, 6)
    dn_load.wait()

    def back_down(c, carry):
        part = pl.ds(pl.multiple_of(c * FF_CHUNK, FF_CHUNK), FF_CHUNK)
        ag[:, part] = dot(g_own[...], dn[part, :], NT).astype(bf16)
        return carry

    lax.fori_loop(0, FF // FF_CHUNK, back_down, 0)
    up_load.wait()
    spread_sent(snd_a, g_own, gd_s, gd_r)
    arrive(g_low, 0, 1)
    start(g_low, 3, 4)
    start(g_high, 0, 1)
    spread_recv(snd_b, x_own, xd_s, xd_r, last=8)

    eacc[...] = jnp.zeros_like(eacc)

    def expert(r):
        def step(c, carry):
            part = rows(c * WIDE_CHUNK, WIDE_CHUNK)
            value, slope = gelu_pair(dot(x_own[r, :], up[:, part]))
            act[r, part] = value.astype(bf16)
            pre_grad = (ag[r, part].astype(f32) * slope).astype(bf16)
            ag[r, part] = pre_grad
            eacc[r, :] += dot(pre_grad, up[:, part], NT)
            return carry

        lax.fori_loop(0, FF // WIDE_CHUNK, step, 0)
        snd_a[r, :] = eacc[r, :].astype(bf16)

    expert(pl.ds(0, HALF))
    spread(snd_a, eg_rcv, eg_s, eg_r, True, last=8)
    spread_recv(snd_b, x_own, xd_s, xd_r, first=8)
    xc[...] = dot(pack[...], x_own[...], TN).astype(bf16)
    start(x_low, 0, 1)
    expert(pl.ds(HALF, HALF))
    spread(snd_a, eg_rcv, eg_s, eg_r, True, first=8)
    start(x_low, 2)
    arrive(g_low, 3, 4)
    start(g_low, 7)
    spread_sent(snd_b, x_own, xd_s, xd_r)
    eacc[...] = jnp.zeros_like(eacc)

    def produce(c, carry):
        part = pl.ds(pl.multiple_of(c * FF_CHUNK, FF_CHUNK), FF_CHUNK)
        eacc[...] += dot(act[:, part], dn[part, :])
        return carry

    lax.fori_loop(0, FF // FF_CHUNK, produce, 0)
    snd_b[...] = eacc[...].astype(bf16)
    arrive(x_low, 0, 1)
    start(x_low, 3, 4)
    spread_recv(snd_a, eg_rcv, eg_s, eg_r, True)

    two, scale2 = norm_parts(hid[...])
    back = dot(disp_t[...], eg_rcv[...])
    sm_x[h, 1:2, :] = jnp.sum(back * two, axis=0, keepdims=True)
    hgrad[...] = og[...].astype(f32) + norm_pull(back, two, scale2, gain2)
    mixed[...] = hgrad[...].astype(bf16)

    for c in wo_out + wo_out2:
        c.wait_send()
    agr_out, agr_into = cross(agr_snd, agr, agr_s, agr_r)
    for i, p in ((2, across), (0, right), (1, left)):
        agr_snd[p] = dot(mixed[...], wo_full[p], NT).astype(bf16)
        agr_out[i].start()
    agr[h] = dot(mixed[...], wo_full[h], NT).astype(bf16)
    arrive(x_low, 3, 4)
    start(x_low, 7)
    start(g_high, 2)

    def output_grad(i, carry):
        wog_snd[i] = dot(att[i], mixed[...], TN).astype(bf16)
        return carry

    lax.fori_loop(0, 4, output_grad, 0)
    wog_twin = [
        remote(wog_snd.at[i, wo_twin], wog_pair.at[i], wog_s.at[3 + i], wog_r.at[3 + i], (h, twin, d))
        for i in range(4)
    ]
    for c in wog_twin:
        c.start()
    dk[...] = jnp.zeros_like(dk)
    dv[...] = jnp.zeros_like(dv)
    for c in agr_into:
        c.wait_recv()

    def attend_back(b, carry):
        keys, allowed = window(b)
        mine = rows(b * TOK, TOK)
        groups = [None, None]
        for head in range(3):
            lanes = pl.ds((head // 2) * 128, 128)
            q = head_mask(head, qkv[mine, head_lanes(head, 0)])
            k = qkv[keys, head_lanes(head, 1)]
            v = qkv[keys, head_lanes(head, 2)]
            u = head_mask(head, agr[b, :, lanes])
            inner = jnp.sum(u.astype(f32) * att_snd[b, :, lanes].astype(f32), axis=-1, keepdims=True)
            s = jnp.where(allowed, dot(q, k, NT), NEGATIVE)
            chances = jnp.exp(s - lse[mine, head : head + 1])
            score_grad = (chances * (dot(u, v, NT) - inner)).astype(bf16)
            part = head_mask(head, dot(score_grad, k)) * 0.125
            g = head // 2
            groups[g] = part if groups[g] is None else groups[g] + part
            dk[keys, lanes] += dot(score_grad, q, TN)
            dv[keys, lanes] += dot(chances.astype(bf16), u, TN)
        jg[mine, 0:128] = groups[0].astype(bf16)
        jg[mine, 128:256] = groups[1].astype(bf16)
        return carry

    for i in range(4):
        wog_twin[i].wait_recv()
        wog_pair[i] = (wog_snd[i, wo_mine, :].astype(f32) + wog_pair[i].astype(f32)).astype(bf16)
    y = lax.div(e, 4)
    over_y = [
        remote(
            wog_pair.at[lax.rem(y + i, 4)], wog_rcv.at[i], wog_s.at[i - 1], wog_r.at[i - 1],
            (h, lax.rem(e + 4 * i, EXPERTS), d),
        )
        for i in range(1, 4)
    ]
    for c in over_y:
        c.start()
    lax.fori_loop(0, 2, attend_back, 0)
    arrive(over_y, 0, 1, 2)
    wog_sum[...] = (
        wog_pair[y].astype(f32) + wog_rcv[1].astype(f32) + wog_rcv[2].astype(f32) + wog_rcv[3].astype(f32)
    ).astype(bf16)
    over_x = [
        remote(wog_sum, wog_x.at[i], wox_s.at[i], wox_r.at[i], (lax.rem(h + i, 4), e, d)) for i in range(1, 4)
    ]
    for i in range(1, 4):

        @pl.when(lax.rem(h + i, 4) == y)
        def _(i=i):
            over_x[i - 1].start()

    arrive(x_low, 2)
    start(x_low, 5, 6)
    arrive(g_high, 0, 1)
    start(g_high, 3, 4)
    lax.fori_loop(2, 4, attend_back, 0)
    jg[:, PAD_COLS : 2 * PAD_COLS] = dk[...].astype(bf16)
    jg[:, 2 * PAD_COLS : 3 * PAD_COLS] = dv[...].astype(bf16)

    du_out = jg.at[pl.ds(0, D), pl.ds(0, FF_CHUNK)]
    dd_out = eg_rcv

    def fill_copies(c):
        part = rows(c * FF_CHUNK, FF_CHUNK)
        return (
            pltpu.make_async_copy(du_out, du_hbm.at[:, part], fill_sem.at[0]),
            pltpu.make_async_copy(dd_out, dd_hbm.at[part], fill_sem.at[1]),
        )

    def fill(c):
        part = rows(c * FF_CHUNK, FF_CHUNK)
        du[...] = dot(x_own[...], ag[:, part], TN)
        eacc[...] = dot(act[:, part], g_own[...], TN)

        def tile(i, carry):
            @pl.when(jnp.logical_and(c == 0, i == 1))
            def _():
                arrive(g_low, 5, 6, 7)
                arrive(x_low, 5, 6, 7)

            r = rows(i * FILL_TILE, FILL_TILE)
            x, g = x_lo[r, :], g_lo[r, :]
            value, slope = gelu_pair(dot(x, up[:, part]))
            pre_grad = (dot(g, dn[part, :], NT) * slope).astype(bf16)
            du[...] += dot(x, pre_grad, TN)
            eacc[...] += dot(value.astype(bf16), g, TN)
            return carry

        lax.fori_loop(0, BLOCKS * HALF // FILL_TILE, tile, 0)

        @pl.when(c > 0)
        def _():
            for copy in fill_copies(c - 1):
                copy.wait()

        du_out[...] = du[...].astype(bf16)
        dd_out[...] = eacc[...].astype(bf16)
        for copy in fill_copies(c):
            copy.start()

    for c in wog_twin:
        c.wait_send()
    ng_out, ng_into = cross(wog_snd, wo_full, ng_s, ng_r)
    for i, p in enumerate((across, right, left)):
        wog_snd[p] = dot(jg[rows(p * TOK, TOK), :], wjt[...]).astype(bf16)
        ng_out[(2, 0, 1)[i]].start()
    spread(snd_b, out_rcv, out_s, out_r, True)

    gain1_part = jnp.zeros((1, D), f32)
    for part in range(3):
        grad = jnp.zeros((PAD_COLS, D), f32)
        for b in range(4):
            grad = grad + dot(jg[b * TOK : (b + 1) * TOK, part * PAD_COLS : (part + 1) * PAD_COLS], gath[b], TN)
        gain1_part = gain1_part + jnp.sum(
            grad * wjt[part * PAD_COLS : (part + 1) * PAD_COLS, :].astype(f32), axis=0, keepdims=True
        )
        gfull[part * HEAD_COLS : (part + 1) * HEAD_COLS, :] = grad[0:HEAD_COLS, :].astype(bf16)
    sm_x[h, 0:1, :] = gain1_part / gain1

    mine_half = rows(core * 384, 384)
    twin_half = rows((1 - core) * 384, 384)
    mine_part = pl.ds(pl.multiple_of(core * 288, 288), 288)
    twin_part = pl.ds(pl.multiple_of((1 - core) * 288, 288), 288)
    ca_out = remote(gfull.at[twin_part], rs_core, ca_s.at[0], ca_r.at[0], (h, twin, d))
    ca_out.start()
    sx_out, sx_into = gather(sm_x, sx_s, sx_r)
    for c in sx_out:
        c.start()
    start(x_high, 0, 1, 2)
    arrive(g_high, 2)
    start(g_high, 5, 6)

    tgrad[...] = dot(jg[rows(h * TOK, TOK), :], wjt[...])
    unit = lax.div(e, 2)
    here = rows(core * 384 + unit * 48, 48)

    def peer(k):
        return lax.rem(unit + k, 8)

    def a2_copy(k, where):
        p = peer(k)
        return remote(
            gpart.at[rows(p * 48, 48)], rs_rcv.at[where], a2_s.at[k], a2_r.at[k], (h, p * 2 + core, d)
        )

    def small_copy(k, p, where):
        return remote(sm_e.at[e], sm_e.at[where], se_s.at[k], se_r.at[k], (h, p, d))

    def small_start(k, carry):
        p = lax.rem(e + k, EXPERTS)
        small_copy(k, p, e).start()
        return carry

    a3 = remote(rs_pair.at[d], rs_pair.at[d], a3_s.at[0], a3_r.at[0], (h, e, other))
    a3_in = remote(rs_pair.at[other], rs_pair.at[other], a3_s.at[0], a3_r.at[0], (h, e, other))
    def a4_copy(k, p, place):
        return remote(gsum.at[place], gsum.at[place], a4_s.at[k], a4_r.at[k], (h, p * 2 + core, d))


    def small_recv(k, carry):
        p = lax.rem(e + EXPERTS - k, EXPERTS)
        small_copy(k, p, p).wait_recv()
        return carry

    sd = remote(sm_d.at[d], sm_d.at[d], sd_s.at[0], sd_r.at[0], (h, e, other))
    sd_in = remote(sm_d.at[other], sm_d.at[other], sd_s.at[0], sd_r.at[0], (h, e, other))
    a5 = remote(gsum.at[mine_half], gsum.at[mine_half], ca_s.at[1], ca_r.at[1], (h, twin, d))
    a5_in = remote(gsum.at[twin_half], gsum.at[twin_half], ca_s.at[1], ca_r.at[1], (h, twin, d))

    def chunk(c, carry):
        @pl.when(c == 1)
        def _():
            ca_out.wait_recv()
            gpart[288:384, :] = jnp.zeros((96, D), bf16)

            @pl.when(y == h)
            def _():
                wog = wog_sum[...].astype(f32)
                for i in range(1, 4):
                    over_x[i - 1].wait_recv()
                    wog = wog + wog_x[i].astype(f32)
                gpart[288:384, :] = wog.astype(bf16)

            for i in range(1, 4):

                @pl.when(lax.rem(h + i, 4) == y)
                def _(i=i):
                    over_x[i - 1].wait_send()

            gpart[0:288, :] = (gfull[mine_part, :].astype(f32) + rs_core[...].astype(f32)).astype(bf16)

            for k in range(1, 8):
                a2_copy(k, unit).start()
            rs_rcv[unit] = gpart[rows(unit * 48, 48), :]

        @pl.when(c == 3)
        def _():
            for c in sx_into:
                c.wait_recv()
            sm_e[e] = (sm_x[0] + sm_x[1]) + (sm_x[2] + sm_x[3])
            lax.fori_loop(1, EXPERTS, small_start, 0)

            for k in range(1, 8):
                a2_copy(k, peer(8 - k)).wait_recv()
            reduced = rs_rcv[0].astype(f32)
            for k in range(1, 8):
                reduced = reduced + rs_rcv[k].astype(f32)
            rs_pair[d] = reduced.astype(bf16)
            a3.start()

        @pl.when(c == 4)
        def _():
            for c in ng_into:
                c.wait_recv()
            own_grad = tgrad[...]
            for p in x_from:
                own_grad = own_grad + wo_full[p].astype(f32)
            one, scale1 = norm_parts(tok[...].astype(f32))
            tgrad[...] = hgrad[...] + norm_pull(own_grad, one, scale1, gain1)
            arrive(x_high, 0, 1)
            start(x_high, 3, 4)
            arrive(x_high, 2)
            start(x_high, 5, 6)
            arrive(g_high, 3, 4)
            start(g_high, 7)

            spread_recv(snd_b, out_rcv, out_s, out_r, True)
            final[...] = hid[...] + dot(disp_t[...], out_rcv[...])

            a3_in.wait_recv()
            gsum[here, :] = (rs_pair[0].astype(f32) + rs_pair[1].astype(f32)).astype(bf16)

            for k in range(1, 8):
                a4_copy(k, peer(k), here).start()

            lax.fori_loop(1, EXPERTS, small_recv, 0)
            gathered = sm_e[0]
            for k in range(1, EXPERTS):
                gathered = gathered + sm_e[k]
            sm_d[d] = gathered
            sd.start()

        @pl.when(c == 5)
        def _():
            arrive(x_high, 3, 4)
            start(x_high, 7)
            for k in range(1, 8):
                p = peer(8 - k)
                a4_copy(k, p, rows(core * 384 + p * 48, 48)).wait_recv()
            for k in range(1, 8):
                a4_copy(k, peer(k), here).wait_send()
            a5.start()

        fill(c)
        return carry

    lax.fori_loop(0, FF // FF_CHUNK, chunk, 0)

    spread_sent(snd_a, eg_rcv, eg_s, eg_r, True)
    spread_sent(snd_b, out_rcv, out_s, out_r, True)

    def small_sent(k, carry):
        p = lax.rem(e + k, EXPERTS)
        small_copy(k, p, e).wait_send()
        return carry

    lax.fori_loop(1, EXPERTS, small_sent, 0)
    for k in range(1, 8):
        a2_copy(k, unit).wait_send()
    for c in (
        nrm_out + att_out + g_low + g_high + x_low + x_high[:7] + c_out + [c_pair] + agr_out + over_y + ng_out
        + sx_out + [ca_out, a3, sd]
    ):
        c.wait_send()

    sd_in.wait_recv()
    small[...] = sm_d[0] + sm_d[1]
    a5_in.wait_recv()
    arrive(g_high, 5, 6, 7)
    arrive(x_high, 5, 6, 7)
    c_pair.wait_recv()
    for copy in fill_copies(5):
        copy.wait()
    x_high[7].wait_send()
    a5.wait_send()


def block_call(*args):
    vmem = pl.BlockSpec(memory_space=pltpu.VMEM)
    hbm = pl.BlockSpec(memory_space=pl.ANY)
    smem = pl.BlockSpec(memory_space=pltpu.SMEM)
    dma = pltpu.SemaphoreType.DMA

    def buf(*shape, dtype=bf16):
        return pltpu.VMEM(shape, dtype)

    scratch = [
        buf(8, 128, dtype=f32), buf(D, D), buf(4, TOK, D), buf(ROW, D), buf(4, TOK, PAD_COLS), buf(4, TOK, PAD_COLS),
        buf(4, PAD_COLS, D), buf(D, FF), buf(FF, D), buf(SLOTS, D), buf(SLOTS, D), buf(SLOTS, D),
        buf(SLOTS, D), buf(SLOTS, D), buf(SLOTS, D),
        buf(SLOTS, SLOTS), buf(SLOTS, FF), buf(SLOTS, FF), buf(SLOTS, D, dtype=f32),
        buf(SLOTS, D), buf(SLOTS, D), buf(SLOTS, TOK), buf(TOK, SLOTS),
        buf(TOK, D, dtype=f32), buf(TOK, D, dtype=f32), buf(TOK, D), buf(4, TOK, PAD_COLS), buf(4, TOK, PAD_COLS),
        buf(ROW, 128, dtype=f32), buf(BLOCKS * HALF, D), buf(BLOCKS * HALF, D), buf(D, FF_CHUNK, dtype=f32),
        buf(ROW, PAD_COLS, dtype=f32), buf(ROW, PAD_COLS, dtype=f32),
        buf(ROW, D), buf(4, PAD_COLS, D), buf(4, 96, D), buf(4, 96, D), buf(96, D), buf(4, 96, D),
        buf(3 * HEAD_COLS, D), buf(384, D), buf(288, D), buf(8, 48, D), buf(2, 48, D),
        buf(4, 8, D, dtype=f32), buf(EXPERTS, 8, D, dtype=f32), buf(2, 8, D, dtype=f32),
        dma((2,)), dma((2,)),
    ]
    for n in (4, 6, 16, 16, 16, 16, 3, 3, 3, 7, 4, 8, 8, 8, 8, 5, 2, 8, 1, 8, 3, 16, 1):
        scratch += [dma((n,)), dma((n,))]
    return pl.pallas_call(
        block_kernel,
        out_shape=[
            jax.ShapeDtypeStruct((TOK, D), f32),
            jax.ShapeDtypeStruct((TOK, D), f32),
            jax.ShapeDtypeStruct((D, D), bf16),
            jax.ShapeDtypeStruct((8, D), f32),
            jax.ShapeDtypeStruct((BLOCKS * HALF, D), bf16),
            jax.ShapeDtypeStruct((BLOCKS * HALF, D), bf16),
            jax.ShapeDtypeStruct((BLOCKS, 8, 128), f32),
            jax.ShapeDtypeStruct((D, FF), bf16),
            jax.ShapeDtypeStruct((FF, D), bf16),
        ],
        in_specs=[vmem] * 8 + [hbm, hbm, vmem, vmem, smem, vmem],
        out_specs=[vmem] * 4 + [hbm, hbm, vmem, hbm, hbm],
        scratch_shapes=scratch,
        compiler_params=pltpu.CompilerParams(
            collective_id=1, has_side_effects=True, vmem_limit_bytes=64 * 2**20 - 2**16
        ),
    )(*args)


GRAD_TILE = 512
REST_TILE = 256


def finish_kernel(
    cnt, x_ref, g_ref, up_ref, dn_ref, du0, dd0, gsum, small, final_in, tgrad_in,
    du_ref, dd_ref, final, tgrad, wq, wk, wv, wo, gain1, gain2, loads,
    xs, gs, total_ref,
):
    step = pl.program_id(0)
    final[...] = final_in[...]
    tgrad[...] = tgrad_in[...]

    @pl.when(step == 0)
    def _():
        total = 0
        for b in range(BLOCKS):
            there = pl.ds(pl.multiple_of(total, 16), HALF)
            more = jnp.maximum(cnt[b, 0, 0].astype(i32) - HALF, 0)

            @pl.when(more > 0)
            def _(b=b, there=there):
                xs[there, :] = x_ref[b * HALF : (b + 1) * HALF, :]
                gs[there, :] = g_ref[b * HALF : (b + 1) * HALF, :]

            total = total + lax.div(more + 15, 16) * 16
        tail = pl.ds(pl.multiple_of(total, 16), GRAD_TILE)
        xs[tail, :] = jnp.zeros((GRAD_TILE, D), bf16)
        gs[tail, :] = jnp.zeros((GRAD_TILE, D), bf16)
        total_ref[0] = total
        for i, w in enumerate((wq, wk, wv)):
            first = i * HEAD_COLS
            for piece in range(12):
                r = first + piece * 16
                at = r if r < 288 else r + 96
                w[piece * 16 : piece * 16 + 16, :] = gsum[at : at + 16, :].astype(f32)
        wo[0:96, :] = gsum[288:384, :].astype(f32)
        wo[96:192, :] = gsum[672:768, :].astype(f32)
        gain1[...] = small[0:1, :].reshape(D)
        gain2[...] = small[1:2, :].reshape(D)
        loads[...] = small[2:3, 0:128].astype(i32).reshape(128)

    total = total_ref[0]
    du_ref[...] = du0[...].astype(f32)
    dd_ref[...] = dd0[...].astype(f32)

    for count in range(1, BLOCKS * HALF // REST_TILE + 1):

        @pl.when(lax.div(total + REST_TILE - 1, REST_TILE) == count)
        def _(size=count * REST_TILE):
            x, g = xs[0:size, :], gs[0:size, :]
            value, slope = gelu_pair(dot(x, up_ref[...]))
            pre_grad = (dot(g, dn_ref[...], NT) * slope).astype(bf16)
            du_ref[...] += dot(x, pre_grad, TN)
            dd_ref[...] += dot(value.astype(bf16), g, TN)


def finish_call(cnt, x_hi, g_hi, up, dn, du0, dd0, gsum, small, final, tgrad):
    def whole(*shape):
        return pl.BlockSpec(shape, lambda i: (0,) * len(shape))

    share = pl.BlockSpec((TOK, D // 6), lambda i: (0, i))
    columns = pl.BlockSpec((D, FF_CHUNK), lambda i: (0, i))
    lines = pl.BlockSpec((FF_CHUNK, D), lambda i: (i, 0))
    return pl.pallas_call(
        finish_kernel,
        grid=(FF // FF_CHUNK,),
        in_specs=[
            pl.BlockSpec((BLOCKS, 8, 128), lambda i: (0, 0, 0), memory_space=pltpu.SMEM), whole(BLOCKS * HALF, D), whole(BLOCKS * HALF, D),
            columns, lines, columns, lines, whole(D, D), whole(8, D), share, share,
        ],
        out_specs=[columns, lines, share, share] + [whole(HEAD_COLS, D)] * 4 + [whole(D), whole(D), whole(128)],
        out_shape=[
            jax.ShapeDtypeStruct((D, FF), f32),
            jax.ShapeDtypeStruct((FF, D), f32),
            jax.ShapeDtypeStruct((TOK, D), f32),
            jax.ShapeDtypeStruct((TOK, D), f32),
        ]
        + [jax.ShapeDtypeStruct((HEAD_COLS, D), f32)] * 4
        + [
            jax.ShapeDtypeStruct((D,), f32),
            jax.ShapeDtypeStruct((D,), f32),
            jax.ShapeDtypeStruct((128,), i32),
        ],
        scratch_shapes=[
            pltpu.VMEM((BLOCKS * HALF + GRAD_TILE, D), bf16),
            pltpu.VMEM((BLOCKS * HALF + GRAD_TILE, D), bf16),
            pltpu.SMEM((1,), i32),
        ],
        compiler_params=pltpu.CompilerParams(vmem_limit_bytes=64 * 2**20 - 2**16),
    )(cnt, x_hi, g_hi, up, dn, du0, dd0, gsum, small, final, tgrad)


def body(
    tokens, out_grad, w_query, w_key, w_value, w_output, gain_one, gain_two, expert_up, expert_down,
    hash_table, token_ids, doc_lengths, turn_mask,
):
    final, tokens_grad, gsum, small, x_hi, g_hi, cnt, du0, dd0 = block_call(
        tokens[0], out_grad[0], w_query.T, w_key.T, w_value.T, w_output, gain_one, gain_two,
        expert_up[0], expert_down[0], hash_table.reshape(256, 128), token_ids, doc_lengths, turn_mask,
    )
    up_grad, down_grad, final, tokens_grad, wq, wk, wv, wo, gain1, gain2, loads = finish_call(
        cnt, x_hi, g_hi, expert_up[0], expert_down[0], du0, dd0, gsum, small, final, tokens_grad
    )
    return (
        final[None], tokens_grad[None], wq.T, wk.T, wv.T, wo, gain1, gain2, up_grad[None], down_grad[None],
        loads[:EXPERTS],
    )


def solution(mesh):
    rows_spec = P(("expert", "dp"), "head", None)
    in_specs = (
        rows_spec, rows_spec, P(None, "head"), P(None, "head"), P(None, "head"), P("head", None),
        P(), P(), P("expert", None, None), P("expert", None, None), P(),
        P(("expert", "dp"), "head"), P(("expert", "dp"), None), P(("expert", "dp"), None),
    )
    out_specs = (
        rows_spec, rows_spec, P(None, "head"), P(None, "head"), P(None, "head"), P("head", None),
        P(), P(), P("expert", None, None), P("expert", None, None), P(),
    )
    return jax.shard_map(body, mesh=mesh, in_specs=in_specs, out_specs=out_specs, check_vma=False)
```
